128 devices in a mesh: row: 8 (over x, core), col: 16 (over z, y).
Axes of the slice: x: 4, y: 4, z: 4, core: 2. Of those that a mesh axis runs over, the one named last changes fastest.
Arguments:
- out_grad: bfloat16 [4096, 7, 7, 256], P(('row', 'col')), may hold values from -6 to 6
- saved: bfloat16 [2, 4096, 7, 7, 256], P(None, ('row', 'col')), may hold values from -6 to 6
- conv_weight: bfloat16 [2, 9, 256, 256], replicated, may hold values from -0.125 to 0.125
- conv_bias: float32 [2, 256], replicated, may hold values from -3 to 3
- tile_ids: int32 [4096, 4], P(('row', 'col')), may hold values from 0 to 127, all different within a row; in each aligned block of 32 rows (0 to 31, 32 to 63, ...) at most 2 rows name the same one
- corner_rows: int32 [4096, 4, 7], P(('row', 'col')), may hold values from 0 to 62
- corner_cols: int32 [4096, 4, 7], P(('row', 'col')), may hold values from 0 to 62
- row_weight: bfloat16 [4096, 4, 7, 2], P(('row', 'col')), may hold values from 0 to 1
- col_weight: bfloat16 [4096, 4, 7, 2], P(('row', 'col')), may hold values from 0 to 1
Outputs:
- weight_grad: float32 [2, 2304, 256], replicated
- bias_grad: float32 [2, 256], replicated
- feature_grad: float32 [512, 1024, 256], P('row', 'col')
The draws below stay inside these ranges and needn't reach their ends.
Inputs may be any that keep to these rules, and one draw needn't show every extreme that they name: `tile_ids`: each box names 4 different tiles. Among the boxes of one device (aligned blocks of 32 boxes) no tile is named more than 2 times, and in some device's boxes some tile is named exactly 2 times.
All inputs are finite; a program needn't handle non-finite values.
Results may differ from the reference program's by a relative error of at most 0.015.
Values may be sent and summed in bfloat16 or wider, within the bound.
No kernel may reach another device: no remote copies, remote signals or barrier semaphores. Data moves between devices by JAX's collectives and lax.ppermute only.
A program may use at most 128 MiB of HBM per device.

```python
import math
import jax
import jax.numpy as jnp
import numpy as np
from jax import lax

C = 256
BINS = 7
LAYERS = 2
TILE = 64
TOP = 4
BOX_DEV = 32
BOXES = 4096
MOST = 2
N_ROW = 8
N_COL = 16
DEVICES = 128


def set_ends(values, stream_key, low, high):
    shape = values.shape
    place = [jax.random.randint(jax.random.fold_in(stream_key, axis), (), 0, shape[axis]) for axis in range(len(shape))]
    values = values.at[tuple(place)].set(low)
    longest = shape.index(max(shape))
    place[longest] = (place[longest] + 1) % shape[longest]
    return values.at[tuple(place)].set(high)


def shard_levels(rng, dims, cuts, low, top_value):
    gain = 1.0
    for dim, parts in cuts:
        steps = jax.random.uniform(jax.random.fold_in(jax.random.fold_in(rng, 6), dim), (parts,), jnp.float32, low / len(cuts), top_value / len(cuts))
        gain = gain * jnp.repeat(jnp.exp(steps), dims[dim] // parts).reshape((-1,) + (1,) * (len(dims) - 1 - dim))
    return gain


def shared_out(key, own, number, rows, count, top, limit, lean):
    sequence = jax.random.permutation(key, count)
    crowded, common = shares(count, rows * top, limit, lean, True), shares(count, rows * top, limit, lean, False)
    places = jnp.arange(count)

    def named(tallies, rotation):
        used = int((tallies > 0).sum())
        fixed = max(1, used // 4)
        moved = fixed + (places - fixed + rotation * (used - fixed)) % max(1, count - fixed)
        return jnp.zeros((count,), jnp.int32).at[sequence[jnp.where(places < fixed, places, moved)]].set(jnp.asarray(tallies, jnp.int32))

    tallies = jnp.where(number % 4 == 0, named(crowded, number // 4), named(common, number - number // 4 - 1))
    mixed = jax.random.permutation(jax.random.fold_in(own, 3), count)
    donor, taker = mixed[0:count // 2 * 2:2], mixed[1:count // 2 * 2:2]
    margin = jnp.minimum(tallies[donor] - 1, limit - tallies[taker]) // 2
    margin = jnp.where((donor == sequence[0]) | (taker == sequence[0]) | (tallies[taker] == 0), 0, jnp.maximum(margin, 0))
    moved = jax.random.randint(jax.random.fold_in(own, 4), (count // 2,), 0, 1 << 20) % (margin + 1)
    tallies = tallies.at[donor].add(-moved).at[taker].add(moved)
    labels = jnp.searchsorted(jnp.cumsum(tallies), jnp.arange(rows * top), side="right").astype(jnp.int32)
    listing = labels.reshape(top, rows).T
    listing = listing[jax.random.permutation(jax.random.fold_in(own, 1), rows)]
    rotation = jax.random.randint(jax.random.fold_in(own, 2), (rows, 1), 0, top)
    return jnp.take_along_axis(listing, (jnp.arange(top)[None, :] + rotation) % top, axis=1)


def shares(count, total, limit, slope, full):
    loads = [(1 << 20) // math.isqrt(grade ** slope) + 1 for grade in range(1, count + 1)]
    largest = limit if full else min(limit, max(-(-total // count), total * loads[0] // sum(loads)))
    least = 1 if total - largest >= count - 1 else 0
    given, spare = [largest] + [least] * (count - 1), total - largest - least * (count - 1)
    while spare > 0:
        free = [i for i in range(1, count) if given[i] < largest] or [i for i in range(1, count) if given[i] < limit]
        whole, remaining = sum([loads[i] for i in free]), spare
        for i in free:
            more = min(limit - given[i], max(1, remaining * loads[i] // whole), spare)
            given[i] = given[i] + more
            spare = spare - more
    return np.array(given)


def normal_values(rng, shape, scale, limit, split=(), held_as=jnp.bfloat16):
    array = jax.random.normal(rng, shape, jnp.float32) * scale
    if len(split) > 0:
        array = shard_levels(rng, shape, split, -0.22, 0.18) * array
    return jnp.clip(array, min=-limit, max=limit).astype(held_as)


def setup_inputs(seed: int = 0) -> dict:
    key_list = jax.random.split(jax.random.key(seed), 10)
    out_grad = normal_values(key_list[0], (BOXES, BINS, BINS, C), 1.0, 6.0, ((0, 128),))
    saved = normal_values(key_list[1], (LAYERS, BOXES, BINS, BINS, C), 1.0, 6.0, ((1, 128),))
    conv_weight = normal_values(key_list[2], (LAYERS, 9, C, C), (9 * C) ** -0.5, 0.125)
    conv_bias = normal_values(key_list[3], (LAYERS, C), 0.5, 3.0, (), jnp.float32)
    tile_ids_keys = jax.random.split(jax.random.fold_in(key_list[4], 1), BOXES // BOX_DEV)
    tile_ids_turns = jax.random.permutation(jax.random.fold_in(key_list[4], 3), BOXES // BOX_DEV)
    tile_ids = jax.vmap(lambda own, number: shared_out(jax.random.fold_in(key_list[4], 2), own, number, BOX_DEV, DEVICES, TOP, MOST, 2))(tile_ids_keys, tile_ids_turns).reshape((BOXES, TOP))
    corner_rows = set_ends(jax.random.randint(key_list[5], (BOXES, TOP, BINS), 0, TILE - 1), jax.random.fold_in(key_list[5], 1), 0, (TILE - 1) - 1).astype(jnp.int32)
    corner_cols = set_ends(jax.random.randint(key_list[6], (BOXES, TOP, BINS), 0, TILE - 1), jax.random.fold_in(key_list[6], 1), 0, (TILE - 1) - 1).astype(jnp.int32)
    row_weight = jnp.clip(1.0 * jax.random.uniform(key_list[7], (BOXES, TOP, BINS, 2), jnp.float32) ** shard_levels(key_list[7], (BOXES, TOP, BINS, 2), ((0, 128),), -0.2, 0.2), 0.0, 1.0).astype(jnp.bfloat16)
    col_weight = jnp.clip(1.0 * jax.random.uniform(key_list[8], (BOXES, TOP, BINS, 2), jnp.float32) ** shard_levels(key_list[8], (BOXES, TOP, BINS, 2), ((0, 128),), -0.2, 0.2), 0.0, 1.0).astype(jnp.bfloat16)
    return dict(out_grad=out_grad, saved=saved, conv_weight=conv_weight, conv_bias=conv_bias, tile_ids=tile_ids, corner_rows=corner_rows, corner_cols=corner_cols, row_weight=row_weight, col_weight=col_weight)


def gelu_slope(pre_act):
    normal_cdf = 0.5 * (1.0 + lax.erf(pre_act * 0.7071067811865476))
    return normal_cdf + pre_act * jnp.exp(-0.5 * pre_act * pre_act) * 0.3989422804014327

def neighbours(crop_grid):
    extent = crop_grid.shape[1]
    padded = jnp.pad(crop_grid, ((0, 0), (1, 1), (1, 1), (0, 0)))
    pieces = [padded[:, shift_row:shift_row + extent, shift_col:shift_col + extent, :] for shift_row in range(3) for shift_col in range(3)]
    return jnp.concatenate(pieces, axis=3).reshape(-1, 9 * crop_grid.shape[3])

def spread_back(grads, extent):
    box_count = grads.shape[0]
    channels = grads.shape[3] // 9
    summed = jnp.zeros((box_count, extent + 2, extent + 2, channels), grads.dtype)
    for shift_row in range(3):
        for shift_col in range(3):
            offset = (3 * shift_row + shift_col) * channels
            summed = summed.at[:, shift_row:shift_row + extent, shift_col:shift_col + extent, :].add(grads[..., offset:offset + channels])
    return summed[:, 1:extent + 1, 1:extent + 1, :]

def layer_back(saved_in, weight, bias_vec, flow_grad):
    extent = saved_in.shape[1]
    channels = saved_in.shape[3]
    columns = neighbours(saved_in)
    matrix = weight.reshape(9 * channels, channels)
    before = jnp.dot(columns, matrix, preferred_element_type=jnp.float32) + bias_vec[None, :]
    slope_bf = (flow_grad.reshape(-1, channels).astype(jnp.float32) * gelu_slope(before)).astype(jnp.bfloat16)
    weight_term = jnp.dot(columns.T, slope_bf, preferred_element_type=jnp.float32)
    bias_term = lax.optimization_barrier(jnp.sum(slope_bf.astype(jnp.float32), axis=0))
    back_cols = jnp.dot(slope_bf, matrix.T, preferred_element_type=jnp.float32)
    flow_next = spread_back(back_cols.reshape(saved_in.shape[0], extent, extent, 9 * channels), extent)
    return (weight_term, bias_term, flow_next.astype(jnp.bfloat16))

def interpolation(corners, weights, extent):
    positions = jnp.arange(extent, dtype=jnp.int32)
    zero_value = jnp.zeros((), weights.dtype)
    low_part = jnp.where(positions == corners[..., None], weights[..., 0:1], zero_value)
    high_part = jnp.where(positions == corners[..., None] + 1, weights[..., 1:2], zero_value)
    return low_part + high_part

def reference(out_grad, saved, conv_weight, conv_bias, tile_ids, corner_rows, corner_cols, row_weight, col_weight):
    owners = N_ROW * N_COL
    grad_scale = 1.0 / math.sqrt(BOXES * BINS * BINS)
    flow_grad = out_grad
    weight_parts = [None] * LAYERS
    bias_parts = [None] * LAYERS
    for layer_index in range(LAYERS - 1, -1, -1):

        def block_step(running, inputs, layer_index=layer_index):
            saved_block, flow_block = inputs
            weight_term, bias_term, flow_next = layer_back(saved_block, conv_weight[layer_index], conv_bias[layer_index], flow_block)
            return ((running[0] + weight_term, running[1] + bias_term), flow_next)
        start_sums = (jnp.zeros((9 * C, C), jnp.float32), jnp.zeros((C,), jnp.float32))
        (weight_total, bias_total), flows = lax.scan(block_step, start_sums, (saved[layer_index].reshape(owners, BOX_DEV, BINS, BINS, C), flow_grad.reshape(owners, BOX_DEV, BINS, BINS, C)))
        flow_grad = flows.reshape(BOXES, BINS, BINS, C)
        weight_parts[layer_index] = weight_total * grad_scale
        bias_parts[layer_index] = bias_total * grad_scale
    weight_grad = jnp.stack(weight_parts)
    bias_grad = jnp.stack(bias_parts)
    interp_rows = interpolation(corner_rows, row_weight, TILE)
    interp_cols = interpolation(corner_cols, col_weight, TILE)

    def add_box(tile_grads, inputs):
        crop_grid, rows_part, cols_part, targets = inputs
        spread = jnp.einsum('tip,ijc->tpjc', rows_part.astype(jnp.float32), crop_grid.astype(jnp.float32)).astype(jnp.bfloat16)
        addition = jnp.einsum('tjq,tpjc->tpqc', cols_part.astype(jnp.float32), spread.astype(jnp.float32))
        return (tile_grads.at[targets].add(addition), None)
    tile_grads = jnp.zeros((owners, TILE, TILE, C), jnp.float32)
    tile_grads, unused = lax.scan(add_box, tile_grads, (flow_grad, interp_rows, interp_cols, tile_ids))
    feature_grad = tile_grads.reshape(N_ROW, N_COL, TILE, TILE, C).transpose(0, 2, 1, 3, 4)
    feature_grad = feature_grad.reshape(N_ROW * TILE, N_COL * TILE, C)
    return (weight_grad, bias_grad, feature_grad)
```

```python
import math

import jax
import jax.numpy as jnp
from jax import lax
from jax.experimental import pallas as pl
from jax.experimental.pallas import tpu as pltpu
from jax.sharding import PartitionSpec as P

TILE = 64
SLOT_ROWS = 104
GROUP = 32
VMEM = pltpu.MemorySpace.VMEM
SMEM = pltpu.MemorySpace.SMEM
AXES = ("row", "col")


def params(megabytes):
    return pltpu.CompilerParams(vmem_limit_bytes=megabytes * 1024 * 1024)


def gelu_slope(pre_act):
    normal_cdf = 0.5 * (1.0 + lax.erf(pre_act * 0.7071067811865476))
    return normal_cdf + pre_act * jnp.exp(-0.5 * pre_act * pre_act) * 0.3989422804014327


def chain_kernel(
    grad_ref, saved_ref, weight_ref, bias_ref, slope_ref, crops_ref, biases_ref, padded, slopes, flow
):
    extent, boxes, channels = grad_ref.shape[0], grad_ref.shape[2], grad_ref.shape[3]
    rows = extent * boxes
    padded[...] = jnp.zeros_like(padded)
    slopes[...] = jnp.zeros_like(slopes)
    for layer in (1, 0):
        padded[1 : extent + 1, 1 : extent + 1] = saved_ref[layer]

        def forward(i, sums, layer=layer):
            pieces = [
                padded[i + a, b : b + extent].reshape(rows, channels)
                for a in range(3)
                for b in range(3)
            ]
            pre = jnp.dot(
                jnp.concatenate(pieces, axis=1),
                weight_ref[layer].reshape(9 * channels, channels),
                preferred_element_type=jnp.float32,
            )
            pre = pre + bias_ref[layer : layer + 1, :]
            upper = grad_ref[i] if layer == 1 else flow[i]
            upper = upper.reshape(rows, channels).astype(jnp.float32)
            slope = (upper * gelu_slope(pre)).astype(jnp.bfloat16)
            slopes[i + 1, 1 : extent + 1] = slope.reshape(extent, boxes, channels)
            slope_ref[layer, i] = slope.reshape(extent, boxes, channels)
            return sums + jnp.sum(
                slope.astype(jnp.float32).reshape(rows // 8, 8, channels), axis=0
            )

        sums = lax.fori_loop(0, extent, forward, jnp.zeros((8, channels), jnp.float32))
        biases_ref[layer : layer + 1, :] = jnp.sum(sums, axis=0, keepdims=True)

        def backward(i, carry, layer=layer):
            total = jnp.zeros((rows, channels), jnp.float32)
            for a in range(3):
                for b in range(3):
                    piece = slopes[i + 2 - a, 2 - b : 2 - b + extent].reshape(rows, channels)
                    total = total + lax.dot_general(
                        piece,
                        weight_ref[layer, 3 * a + b],
                        (((1,), (1,)), ((), ())),
                        preferred_element_type=jnp.float32,
                    )
            if layer == 1:
                flow[i] = total.astype(jnp.bfloat16).reshape(extent, boxes, channels)
            else:
                place = pl.ds(pl.multiple_of(i * rows, 8), rows)
                crops_ref[0, place, :] = total[:, : channels // 2]
                crops_ref[1, place, :] = total[:, channels // 2 :]
            return carry

        lax.fori_loop(0, extent, backward, 0)


def conv_chain(grad_t, saved_t, weight, bias):
    extent, boxes, channels = grad_t.shape[0], grad_t.shape[2], grad_t.shape[3]
    layers = saved_t.shape[0]
    padded = (extent + 2, extent + 2, boxes, channels)
    return pl.pallas_call(
        chain_kernel,
        name="conv_chain",
        out_shape=(
            jax.ShapeDtypeStruct((layers, extent, extent, boxes, channels), jnp.bfloat16),
            jax.ShapeDtypeStruct((2, extent * extent * boxes, channels // 2), jnp.float32),
            jax.ShapeDtypeStruct((layers, channels), jnp.float32),
        ),
        in_specs=[pl.BlockSpec(memory_space=VMEM)] * 4,
        out_specs=(pl.BlockSpec(memory_space=VMEM),) * 3,
        scratch_shapes=[
            pltpu.VMEM(padded, jnp.bfloat16),
            pltpu.VMEM(padded, jnp.bfloat16),
            pltpu.VMEM((extent, extent, boxes, channels), jnp.bfloat16),
        ],
        compiler_params=params(40),
        cost_estimate=pl.CostEstimate(
            flops=8 * extent * extent * boxes * 9 * channels * channels,
            bytes_accessed=10_000_000,
            transcendentals=0,
        ),
    )(grad_t, saved_t, weight, bias)


def pack_kernel(box_ref, crops_ref, tail_ref, out_ref, held, staged):
    slots = out_ref.shape[0]
    boxes = held.shape[0]
    bins = crops_ref.shape[1] // boxes
    step = pl.program_id(0)

    @pl.when(step == 0)
    def _():
        for box in range(boxes):
            for half in range(2):
                staged[box, half * bins : (half + 1) * bins, :] = crops_ref[
                    half, pl.ds(box, bins, stride=boxes), :
                ]
            staged[box, 2 * bins :, :] = tail_ref[...]
            held[box] = staged[box].astype(jnp.bfloat16)

    def place(index, carry):
        out_ref[index] = held[box_ref[step * slots + index]]
        return carry

    lax.fori_loop(0, slots, place, 0, unroll=4)


def pack(box_of_slot, crops, tail, boxes):
    slots = box_of_slot.shape[0]
    steps = 8
    half = crops.shape[2]
    return pl.pallas_call(
        pack_kernel,
        name="pack",
        out_shape=jax.ShapeDtypeStruct((slots, SLOT_ROWS, half), jnp.bfloat16),
        grid_spec=pltpu.PrefetchScalarGridSpec(
            num_scalar_prefetch=1,
            grid=(steps,),
            in_specs=[
                pl.BlockSpec(crops.shape, lambda g, ids: (0, 0, 0)),
                pl.BlockSpec(tail.shape, lambda g, ids: (0, 0)),
            ],
            out_specs=pl.BlockSpec((slots // steps, SLOT_ROWS, half), lambda g, ids: (g, 0, 0)),
            scratch_shapes=[
                pltpu.VMEM((boxes, SLOT_ROWS, half), jnp.bfloat16),
                pltpu.VMEM((boxes, SLOT_ROWS, half), jnp.float32),
            ],
        ),
        compiler_params=params(24),
        cost_estimate=pl.CostEstimate(flops=1_000_000, bytes_accessed=9_000_000, transcendentals=0),
    )(box_of_slot, crops, tail)


def weight_kernel(slope_ref, saved_ref, out_ref, padded):
    extent, boxes, channels = saved_ref.shape[1], saved_ref.shape[3], saved_ref.shape[4]
    bins = extent * extent * boxes
    offset = pl.program_id(1)

    @pl.when(offset == 0)
    def _():
        padded[...] = jnp.zeros_like(padded)
        padded[1 : extent + 1, 1 : extent + 1] = saved_ref[0]

    a, b = offset // 3, offset % 3
    piece = padded[pl.ds(a, extent), pl.ds(b, extent)].reshape(bins, channels)
    term = lax.dot_general(
        piece,
        slope_ref[0].reshape(bins, channels),
        (((0,), (0,)), ((), ())),
        preferred_element_type=jnp.float32,
    )
    out_ref[0, 0, 0] = term[:, : channels // 2].astype(jnp.bfloat16)
    out_ref[0, 1, 0] = term[:, channels // 2 :].astype(jnp.bfloat16)


def weight_terms(slope, saved_t):
    layers, extent, boxes, channels = slope.shape[0], slope.shape[1], slope.shape[3], slope.shape[4]
    block = (1, extent, extent, boxes, channels)
    return pl.pallas_call(
        weight_kernel,
        name="weight_terms",
        out_shape=jax.ShapeDtypeStruct((layers, 2, 9, channels, channels // 2), jnp.bfloat16),
        grid=(layers, 9),
        in_specs=[pl.BlockSpec(block, lambda l, o: (l, 0, 0, 0, 0))] * 2,
        out_specs=pl.BlockSpec((1, 2, 1, channels, channels // 2), lambda l, o: (l, 0, o, 0, 0)),
        scratch_shapes=[pltpu.VMEM((extent + 2, extent + 2, boxes, channels), jnp.bfloat16)],
        compiler_params=params(24),
        cost_estimate=pl.CostEstimate(
            flops=4 * extent * extent * boxes * 9 * channels * channels,
            bytes_accessed=6_000_000,
            transcendentals=0,
        ),
    )(slope, saved_t)


def hop_core():
    return [(r, r ^ 1) for r in range(8)]


def hop_x(k):
    return [(r, (r // 2 + k) % 4 * 2 + r % 2) for r in range(8)]


def hop_y(k):
    return [(c, c // 4 * 4 + (c % 4 + k) % 4) for c in range(16)]


def hop_z(k):
    return [(c, (c // 4 + k) % 4 * 4 + c % 4) for c in range(16)]


def sum_everywhere(terms):
    row, col = lax.axis_index("row"), lax.axis_index("col")
    core, x, z, y = row % 2, row // 2, col // 4, col % 4
    chunk = terms.shape[2:]

    def take(array, index):
        return lax.dynamic_index_in_dim(array, index, 0, keepdims=False)

    own = take(terms, core)
    other = lax.ppermute(take(terms, 1 - core), "row", hop_core())
    total = own.astype(jnp.float32) + other.astype(jnp.float32)
    stages = ((x, "row", hop_x), (y, "col", hop_y), (z, "col", hop_z))
    for place, name, hop in stages:
        held = total.astype(jnp.bfloat16)
        held = held.reshape((4, held.shape[0] // 4) + chunk)
        arrived = [
            lax.ppermute(take(held, (place + k) % 4), name, hop(k)) for k in range(1, 4)
        ]
        total = take(held, place).astype(jnp.float32)
        for piece in arrived:
            total = total + piece.astype(jnp.float32)
    held = total.astype(jnp.bfloat16)
    for place, name, hop in reversed(stages):
        arrived = [held] + [lax.ppermute(held, name, hop(k)) for k in (3, 2, 1)]
        ring = jnp.stack(arrived + arrived)
        held = lax.dynamic_slice_in_dim(ring, (4 - place) % 4, 4, 0)
        held = held.reshape((-1,) + chunk)
    other = lax.ppermute(held, "row", hop_core())
    return jnp.where(core == 0, jnp.stack([held, other]), jnp.stack([other, held]))


def order_kernel(rows_ref, weights_ref, start_ref, base_ref, owner_ref, scale_ref, count):
    places = start_ref.shape[0]
    extent = 7
    slots = rows_ref.shape[0] // extent

    def begin(p, carry):
        count[p] = start_ref[p]
        return carry

    lax.fori_loop(0, places, begin, 0)

    def clear(n, carry):
        base_ref[n] = 0
        owner_ref[n] = 0
        scale_ref[n] = 0.0
        return carry

    lax.fori_loop(0, base_ref.shape[0], clear, 0, unroll=8)

    def enter(slot, carry):
        @pl.when(rows_ref[slot * extent] >= 0)
        def _():
            for i in range(extent):
                first = rows_ref[slot * extent + i]
                for a in range(2):
                    n = count[first + a]
                    count[first + a] = n + 1
                    base_ref[n] = slot * SLOT_ROWS + extent * i
                    owner_ref[n] = slot
                    scale_ref[n] = weights_ref[(slot * extent + i) * 2 + a]

        return carry

    lax.fori_loop(0, slots, enter, 0)


def order_entries(rows, weights, start, entries):
    return pl.pallas_call(
        order_kernel,
        name="order_entries",
        out_shape=(
            jax.ShapeDtypeStruct((entries,), jnp.int32),
            jax.ShapeDtypeStruct((entries,), jnp.int32),
            jax.ShapeDtypeStruct((entries,), jnp.float32),
        ),
        in_specs=[pl.BlockSpec(memory_space=SMEM)] * 3,
        out_specs=(pl.BlockSpec(memory_space=SMEM),) * 3,
        scratch_shapes=[pltpu.SMEM((TILE,), jnp.int32)],
        cost_estimate=pl.CostEstimate(flops=10_000_000, bytes_accessed=30_000_000, transcendentals=0),
    )(rows, weights, start)


def tile_kernel(
    base_ref, place_ref, groups_ref, got_ref, columns_ref, out_ref, biases_ref, crops
):
    step = pl.program_id(0)
    slots, half = got_ref.shape[0], got_ref.shape[2]
    bins = 49
    block = slots * SLOT_ROWS
    wide = got_ref[...].astype(jnp.float32)
    crops[pl.ds(pl.multiple_of(step * block, 8), block), :] = wide.reshape(block, half)
    spare = jnp.sum(wide[:, SLOT_ROWS - 8 :, :], axis=0)

    @pl.when(step == 0)
    def _():
        biases_ref[...] = spare

    @pl.when(step > 0)
    def _():
        biases_ref[...] += spare

    @pl.when(step == pl.num_programs(0) - 1)
    def _():
        out_ref[...] = jnp.zeros_like(out_ref)

        def group(t, carry):
            left, right = [], []
            for n in range(GROUP):
                base = base_ref[t * GROUP + n]
                left.append(crops[pl.ds(base, 8), :])
                right.append(crops[pl.ds(base + bins, 8), :])
            values = jnp.concatenate(
                [jnp.concatenate(left, axis=0), jnp.concatenate(right, axis=0)], axis=1
            ).astype(jnp.bfloat16)
            out_ref[place_ref[t]] += jnp.dot(
                columns_ref[t], values, preferred_element_type=jnp.float32
            )
            return carry

        lax.fori_loop(0, groups_ref[0], group, 0)


def tile_sum(base, place, groups, got, columns, channels):
    steps = 8
    slots, half = got.shape[0], got.shape[2]
    return pl.pallas_call(
        tile_kernel,
        name="tile_sum",
        out_shape=(
            jax.ShapeDtypeStruct((TILE, TILE, channels), jnp.float32),
            jax.ShapeDtypeStruct((8, half), jnp.float32),
        ),
        grid_spec=pltpu.PrefetchScalarGridSpec(
            num_scalar_prefetch=3,
            grid=(steps,),
            in_specs=[
                pl.BlockSpec((slots // steps, SLOT_ROWS, half), lambda g, *refs: (g, 0, 0)),
                pl.BlockSpec(columns.shape, lambda g, *refs: (0, 0, 0)),
            ],
            out_specs=(
                pl.BlockSpec((TILE, TILE, channels), lambda g, *refs: (0, 0, 0)),
                pl.BlockSpec((8, half), lambda g, *refs: (0, 0)),
            ),
            scratch_shapes=[pltpu.VMEM((slots * SLOT_ROWS, half), jnp.float32)],
        ),
        compiler_params=params(48),
        cost_estimate=pl.CostEstimate(
            flops=2 * columns.size * channels, bytes_accessed=17_000_000, transcendentals=0
        ),
    )(base, place, groups, got, columns)


def choose(targets, owners):
    count = targets.shape[-1]
    pieces = jnp.arange(count, dtype=jnp.int32)
    match = targets[..., None, :] == owners[:, None]
    first = jnp.min(jnp.where(match, pieces, count), axis=-1)
    last = jnp.max(jnp.where(match, pieces, -1), axis=-1)
    picked = jnp.stack([first, last], axis=-1)
    used = jnp.stack([first < count, last > first], axis=-1)
    return picked, used & (picked >= 0)


def prepare(fields, extent):
    me = lax.axis_index("row") * lax.axis_size("col") + lax.axis_index("col")
    devices, pieces = fields.shape[0], fields.shape[2]
    targets = fields[:, 0, :].astype(jnp.int32)
    picked, used = choose(targets, me.reshape(1))
    picked, used = picked[:, 0], used[:, 0]
    select = (picked[:, :, None] == jnp.arange(pieces)) & used[:, :, None]
    slots = lax.dot_general(
        select.astype(jnp.bfloat16),
        fields,
        (((2,), (2,)), ((0,), (0,))),
        preferred_element_type=jnp.float32,
    ).reshape(2 * devices, fields.shape[1])
    used = used.reshape(-1)
    cuts = [1 + extent, 1 + 2 * extent, 1 + 4 * extent, 1 + 6 * extent]
    rows = slots[:, 1 : cuts[0]].astype(jnp.int32)
    rows = jnp.where(used[:, None], rows, -4)
    row_weight = slots[:, cuts[1] : cuts[2]]
    table = jnp.concatenate(
        [slots[:, cuts[0] : cuts[1]], slots[:, cuts[2] : cuts[3]]], axis=1
    ).astype(jnp.bfloat16)
    return rows, row_weight, table


def arrange(rows, row_weight, table):
    slots, extent = rows.shape
    groups = slots * extent * 2 // GROUP + TILE
    entries = groups * GROUP
    pixel = jnp.arange(TILE, dtype=jnp.int32)
    flat = rows.reshape(-1)
    hits = (flat[:, None] == pixel).astype(jnp.int32) + (flat[:, None] + 1 == pixel).astype(jnp.int32)
    tally = jnp.sum(hits, axis=0)
    needed = (tally + GROUP - 1) // GROUP
    ends = jnp.sum(jnp.where(pixel[None, :] <= pixel[:, None], needed[None, :], 0), axis=1)
    start = (ends - needed) * GROUP
    place = jnp.sum((jnp.arange(groups)[:, None] >= ends[None, :]).astype(jnp.int32), axis=1)
    base, owner, scale = order_entries(flat, row_weight.reshape(-1), start, entries)
    chosen = (owner[:, None] == jnp.arange(slots)).astype(jnp.bfloat16)
    values = jnp.dot(chosen, table, preferred_element_type=jnp.float32)
    corner = values[:, :extent]
    low = values[:, extent::2] * scale[:, None]
    high = values[:, extent + 1 :: 2] * scale[:, None]

    def lanes(array, fill):
        array = jnp.pad(array, ((0, 0), (0, 8 - extent)), constant_values=fill)
        return array.reshape(groups, 1, GROUP * 8)

    corner, low, high = lanes(corner, -4.0), lanes(low, 0.0), lanes(high, 0.0)
    position = jnp.arange(TILE, dtype=jnp.float32)[None, :, None]
    columns = jnp.where(position == corner, low, 0.0) + jnp.where(position == corner + 1.0, high, 0.0)
    return base, place, ends[-1:], columns.astype(jnp.bfloat16)


def shards(
    out_grad,
    saved,
    conv_weight,
    conv_bias,
    tile_ids,
    corner_rows,
    corner_cols,
    row_weight,
    col_weight,
):
    boxes, extent, channels = out_grad.shape[0], out_grad.shape[1], out_grad.shape[3]
    layers, per_box = saved.shape[0], tile_ids.shape[1]
    devices = lax.axis_size("row") * lax.axis_size("col")
    grad_scale = 1.0 / math.sqrt(boxes * devices * extent * extent)
    pieces = boxes * per_box

    targets = tile_ids.reshape(pieces)
    fields = jnp.concatenate(
        [
            targets.reshape(pieces, 1).astype(jnp.bfloat16),
            corner_rows.reshape(pieces, extent).astype(jnp.bfloat16),
            corner_cols.reshape(pieces, extent).astype(jnp.bfloat16),
            row_weight.reshape(pieces, 2 * extent),
            col_weight.reshape(pieces, 2 * extent),
        ],
        axis=1,
    ).T
    fields = jnp.pad(fields, ((0, -fields.shape[0] % 16), (0, 0)))
    every = lax.all_gather(fields, AXES, axis=0, tiled=False)

    picked, used = choose(targets, jnp.arange(devices, dtype=jnp.int32))
    box_of_slot = jnp.where(used, picked // per_box, 0).reshape(2 * devices)

    grad_t = jnp.transpose(out_grad, (1, 2, 0, 3))
    saved_t = jnp.transpose(saved, (0, 2, 3, 1, 4))
    slope, crops, biases = conv_chain(grad_t, saved_t, conv_weight, conv_bias)
    tail = jnp.pad(biases.reshape(layers * 2, channels // 2), ((0, 2), (0, 0)))
    send = pack(box_of_slot, crops, tail, boxes)
    got = lax.all_to_all(send, AXES, split_axis=0, concat_axis=0, tiled=True)

    terms = weight_terms(slope, saved_t)
    rows_all = terms.shape[1] * terms.shape[2] * terms.shape[3]
    terms = terms.reshape(layers, 64, rows_all // 64, channels // 2)
    totals = sum_everywhere(terms).reshape(layers, 2, 9 * channels, channels // 2)
    weight_grad = jnp.concatenate(
        [totals[:, 0].astype(jnp.float32), totals[:, 1].astype(jnp.float32)], axis=2
    ) * grad_scale

    base, place, groups, columns = arrange(*prepare(every, extent))
    feature_grad, spare = tile_sum(base, place, groups, got, columns, channels)
    bias_grad = (spare[2 : 2 + 2 * layers] * (0.5 * grad_scale)).reshape(layers, channels)
    return (weight_grad, bias_grad, feature_grad)


def solution(mesh):
    in_specs = (
        P(AXES, None, None, None),
        P(None, AXES, None, None, None),
        P(),
        P(),
        P(AXES, None),
        P(AXES, None, None),
        P(AXES, None, None),
        P(AXES, None, None, None),
        P(AXES, None, None, None),
    )
    out_specs = (P(), P(), P("row", "col", None))
    return jax.shard_map(shards, mesh=mesh, in_specs=in_specs, out_specs=out_specs, check_vma=False)
```

```python
import functools
import math

import jax
import jax.numpy as jnp
from jax import lax
from jax.experimental import pallas as pl
from jax.experimental.pallas import tpu as pltpu
from jax.sharding import PartitionSpec as P

TILE = 64
SLOT_ROWS = 104
GROUP = 32
UNROLL = 8
VMEM = pltpu.MemorySpace.VMEM
SMEM = pltpu.MemorySpace.SMEM
AXES = ("row", "col")


def params(megabytes):
    return pltpu.CompilerParams(vmem_limit_bytes=megabytes * 1024 * 1024)


def gelu_slope(pre_act):
    normal_cdf = 0.5 * (1.0 + lax.erf(pre_act * 0.7071067811865476))
    return normal_cdf + pre_act * jnp.exp(-0.5 * pre_act * pre_act) * 0.3989422804014327


def chain_kernel(
    grad_ref, saved_ref, weight_ref, bias_ref, slope_ref, crops_ref, biases_ref, padded, slopes, flow
):
    extent, boxes, channels = grad_ref.shape[0], grad_ref.shape[2], grad_ref.shape[3]
    rows = extent * boxes
    padded[...] = jnp.zeros_like(padded)
    slopes[...] = jnp.zeros_like(slopes)
    for layer in (1, 0):
        padded[1 : extent + 1, 1 : extent + 1] = saved_ref[layer]

        def forward(i, sums, layer=layer):
            pieces = [
                padded[i + a, b : b + extent].reshape(rows, channels)
                for a in range(3)
                for b in range(3)
            ]
            pre = jnp.dot(
                jnp.concatenate(pieces, axis=1),
                weight_ref[layer].reshape(9 * channels, channels),
                preferred_element_type=jnp.float32,
            )
            pre = pre + bias_ref[layer : layer + 1, :]
            upper = grad_ref[i] if layer == 1 else flow[i]
            upper = upper.reshape(rows, channels).astype(jnp.float32)
            slope = (upper * gelu_slope(pre)).astype(jnp.bfloat16)
            slopes[i + 1, 1 : extent + 1] = slope.reshape(extent, boxes, channels)
            slope_ref[layer, i] = slope.reshape(extent, boxes, channels)
            return sums + jnp.sum(
                slope.astype(jnp.float32).reshape(rows // 8, 8, channels), axis=0
            )

        sums = lax.fori_loop(0, extent, forward, jnp.zeros((8, channels), jnp.float32))
        biases_ref[layer : layer + 1, :] = jnp.sum(sums, axis=0, keepdims=True)

        def backward(i, carry, layer=layer):
            total = jnp.zeros((rows, channels), jnp.float32)
            for a in range(3):
                for b in range(3):
                    piece = slopes[i + 2 - a, 2 - b : 2 - b + extent].reshape(rows, channels)
                    total = total + lax.dot_general(
                        piece,
                        weight_ref[layer, 3 * a + b],
                        (((1,), (1,)), ((), ())),
                        preferred_element_type=jnp.float32,
                    )
            if layer == 1:
                flow[i] = total.astype(jnp.bfloat16).reshape(extent, boxes, channels)
            else:
                place = pl.ds(pl.multiple_of(i * rows, 8), rows)
                crops_ref[0, place, :] = total[:, : channels // 2]
                crops_ref[1, place, :] = total[:, channels // 2 :]
            return carry

        lax.fori_loop(0, extent, backward, 0)


def conv_chain(grad_t, saved_t, weight, bias):
    extent, boxes, channels = grad_t.shape[0], grad_t.shape[2], grad_t.shape[3]
    layers = saved_t.shape[0]
    padded = (extent + 2, extent + 2, boxes, channels)
    return pl.pallas_call(
        chain_kernel,
        name="conv_chain",
        out_shape=(
            jax.ShapeDtypeStruct((layers, extent, extent, boxes, channels), jnp.bfloat16),
            jax.ShapeDtypeStruct((2, extent * extent * boxes, channels // 2), jnp.float32),
            jax.ShapeDtypeStruct((layers, channels), jnp.float32),
        ),
        in_specs=[pl.BlockSpec(memory_space=VMEM)] * 4,
        out_specs=(pl.BlockSpec(memory_space=VMEM),) * 3,
        scratch_shapes=[
            pltpu.VMEM(padded, jnp.bfloat16),
            pltpu.VMEM(padded, jnp.bfloat16),
            pltpu.VMEM((extent, extent, boxes, channels), jnp.bfloat16),
        ],
        compiler_params=params(40),
        cost_estimate=pl.CostEstimate(flops=15000000000, bytes_accessed=5000000, transcendentals=0),
    )(grad_t, saved_t, weight, bias)


def pack_kernel(box_ref, crops_ref, tail_ref, out_ref, held, staged):
    slots = out_ref.shape[0]
    boxes = held.shape[0]
    bins = crops_ref.shape[1] // boxes
    step = pl.program_id(0)

    @pl.when(step == 0)
    def _():
        for box in range(boxes):
            for half in range(2):
                staged[box, half * bins : (half + 1) * bins, :] = crops_ref[
                    half, pl.ds(box, bins, stride=boxes), :
                ]
            staged[box, 2 * bins :, :] = tail_ref[...]
            held[box] = staged[box].astype(jnp.bfloat16)

    def place(index, carry):
        slot = step * slots + index
        owners = box_ref.shape[0] // 2
        out_ref[index] = held[box_ref[lax.rem(slot, 2) * owners + lax.div(slot, 2)]]
        return carry

    lax.fori_loop(0, slots, place, 0, unroll=4)


def pack(box_of_slot, crops, tail, boxes):
    slots = box_of_slot.shape[0]
    steps = 8
    half = crops.shape[2]
    return pl.pallas_call(
        pack_kernel,
        name="pack",
        out_shape=jax.ShapeDtypeStruct((slots, SLOT_ROWS, half), jnp.bfloat16),
        grid_spec=pltpu.PrefetchScalarGridSpec(
            num_scalar_prefetch=1,
            grid=(steps,),
            in_specs=[
                pl.BlockSpec(crops.shape, lambda g, ids: (0, 0, 0)),
                pl.BlockSpec(tail.shape, lambda g, ids: (0, 0)),
            ],
            out_specs=pl.BlockSpec((slots // steps, SLOT_ROWS, half), lambda g, ids: (g, 0, 0)),
            scratch_shapes=[
                pltpu.VMEM((boxes, SLOT_ROWS, half), jnp.bfloat16),
                pltpu.VMEM((boxes, SLOT_ROWS, half), jnp.float32),
            ],
        ),
        compiler_params=params(24),
        cost_estimate=pl.CostEstimate(flops=1000000, bytes_accessed=9000000, transcendentals=0),
    )(box_of_slot, crops, tail)


def weight_kernel(slope_ref, saved_ref, out_ref, padded):
    extent, boxes, channels = saved_ref.shape[1], saved_ref.shape[3], saved_ref.shape[4]
    bins = extent * extent * boxes
    offset = pl.program_id(1)

    @pl.when(offset == 0)
    def _():
        padded[...] = jnp.zeros_like(padded)
        padded[1 : extent + 1, 1 : extent + 1] = saved_ref[0]

    a, b = offset // 3, offset % 3
    piece = padded[pl.ds(a, extent), pl.ds(b, extent)].reshape(bins, channels)
    term = lax.dot_general(
        piece,
        slope_ref[0].reshape(bins, channels),
        (((0,), (0,)), ((), ())),
        preferred_element_type=jnp.float32,
    )
    out_ref[0, 0, 0] = term[:, : channels // 2].astype(jnp.bfloat16)
    out_ref[0, 1, 0] = term[:, channels // 2 :].astype(jnp.bfloat16)


def weight_terms(slope, saved_t):
    layers, extent, boxes, channels = slope.shape[0], slope.shape[1], slope.shape[3], slope.shape[4]
    block = (1, extent, extent, boxes, channels)
    return pl.pallas_call(
        weight_kernel,
        name="weight_terms",
        out_shape=jax.ShapeDtypeStruct((layers, 2, 9, channels, channels // 2), jnp.bfloat16),
        grid=(layers, 9),
        in_specs=[pl.BlockSpec(block, lambda l, o: (l, 0, 0, 0, 0))] * 2,
        out_specs=pl.BlockSpec((1, 2, 1, channels, channels // 2), lambda l, o: (l, 0, o, 0, 0)),
        scratch_shapes=[pltpu.VMEM((extent + 2, extent + 2, boxes, channels), jnp.bfloat16)],
        compiler_params=params(24),
        cost_estimate=pl.CostEstimate(flops=7400000000, bytes_accessed=5000000, transcendentals=0),
    )(slope, saved_t)


def hop_core():
    return [(r, r ^ 1) for r in range(8)]


def hop_x(k):
    return [(r, (r // 2 + k) % 4 * 2 + r % 2) for r in range(8)]


def pick(array, index):
    return lax.dynamic_index_in_dim(array, index, 0, keepdims=False)


def sum_lines(terms):
    row = lax.axis_index("row")
    core, x = row % 2, row // 2
    other = lax.ppermute(pick(terms, 1 - core), "row", hop_core())
    total = pick(terms, core).astype(jnp.float32) + other.astype(jnp.float32)
    held = total.astype(jnp.bfloat16)
    sent = [pick(held, (x + k) % 4) for k in range(1, 4)]
    return held, sent


def finish_lines(held, arrived):
    total = pick(held, lax.axis_index("row") // 2).astype(jnp.float32)
    for piece in arrived:
        total = total + piece.astype(jnp.float32)
    return total


def gather_lines(part):
    ring = jnp.stack([part] + [lax.ppermute(part, "row", hop_x(k)) for k in (3, 2, 1)])
    return ring, lax.ppermute(ring, "row", hop_core())


def widen_kernel(place_ref, own_ref, other_ref, out_ref, *, scale):
    mine = pl.program_id(0) == place_ref[1]
    chunk = jnp.where(mine, own_ref[0].astype(jnp.float32), other_ref[0].astype(jnp.float32))
    out_ref[0] = chunk * scale


def widen(own, other, layers, scale):
    row = lax.axis_index("row")
    place = jnp.stack([row // 2, row % 2]).astype(jnp.int32)
    chunks, rows, half = own.shape

    def source(layer, chunk, place):
        return (lax.rem(chunk + chunks - place[0], chunks), 0, 0)

    return pl.pallas_call(
        functools.partial(widen_kernel, scale=scale),
        name="widen",
        out_shape=jax.ShapeDtypeStruct((layers, chunks // 2 * rows, 2 * half), jnp.float32),
        grid_spec=pltpu.PrefetchScalarGridSpec(
            num_scalar_prefetch=1,
            grid=(layers, chunks),
            in_specs=[pl.BlockSpec((1, rows, half), source)] * 2,
            out_specs=pl.BlockSpec(
                (1, rows, half), lambda l, m, place: (l, lax.rem(m, chunks // 2), lax.div(m, chunks // 2))
            ),
        ),
        compiler_params=params(16),
        cost_estimate=pl.CostEstimate(flops=3_000_000, bytes_accessed=10_000_000, transcendentals=0),
    )(place, own, other)


def order_kernel(rows_ref, start_ref, end_ref, entry_ref, count):
    places = start_ref.shape[0]
    extent = 7
    slots = rows_ref.shape[0] // extent

    def begin(p, carry):
        count[p] = start_ref[p]
        return carry

    lax.fori_loop(0, places, begin, 0)

    def enter(slot, carry):
        @pl.when(rows_ref[slot * extent] >= 0)
        def _():
            for i in range(extent):
                first = rows_ref[slot * extent + i]
                for a in range(2):
                    n = count[first + a]
                    count[first + a] = n + 1
                    entry_ref[n] = slot * 16 + 2 * i + a

        return carry

    lax.fori_loop(0, slots, enter, 0)

    def fill(p, carry):
        def blank(n, inner):
            entry_ref[n] = 14
            return inner

        return lax.fori_loop(count[p], end_ref[p], blank, carry)

    lax.fori_loop(0, places, fill, 0)


def order_entries(rows, start, end, entries):
    return pl.pallas_call(
        order_kernel,
        name="order_entries",
        out_shape=jax.ShapeDtypeStruct((entries,), jnp.int32),
        in_specs=[pl.BlockSpec(memory_space=SMEM)] * 3,
        out_specs=pl.BlockSpec(memory_space=SMEM),
        scratch_shapes=[pltpu.SMEM((TILE,), jnp.int32)],
        cost_estimate=pl.CostEstimate(flops=10_000_000, bytes_accessed=30_000_000, transcendentals=0),
    )(rows, start, end)


def tile_kernel(
    base_ref, place_ref, groups_ref, got_ref, columns_ref, out_ref, biases_ref, crops
):
    step = pl.program_id(0)
    slots, half = got_ref.shape[0], got_ref.shape[2]
    bins = 49
    block = slots * SLOT_ROWS
    wide = got_ref[...].astype(jnp.float32)
    crops[pl.ds(pl.multiple_of(step * block, 8), block), :] = wide.reshape(block, half)
    spare = jnp.sum(wide[:, SLOT_ROWS - 8 :, :], axis=0)

    @pl.when(step == 0)
    def _():
        biases_ref[...] = spare

    @pl.when(step > 0)
    def _():
        biases_ref[...] += spare

    @pl.when(step == pl.num_programs(0) - 1)
    def _():
        out_ref[...] = jnp.zeros_like(out_ref)

        def group(t):
            left, right = [], []
            for n in range(GROUP):
                base = base_ref[t * GROUP + n]
                left.append(crops[pl.ds(base, 8), :])
                right.append(crops[pl.ds(base + bins, 8), :])
            values = jnp.concatenate(
                [jnp.concatenate(left, axis=0), jnp.concatenate(right, axis=0)], axis=1
            ).astype(jnp.bfloat16)
            return jnp.dot(columns_ref[t], values, preferred_element_type=jnp.float32)

        def several(t, carry):
            terms = [group(t * UNROLL + u) for u in range(UNROLL)]
            for u in range(UNROLL):
                out_ref[place_ref[t * UNROLL + u]] += terms[u]
            return carry

        lax.fori_loop(0, (groups_ref[0] + UNROLL - 1) // UNROLL, several, 0)


def tile_sum(base, place, groups, got, columns, channels):
    steps = 8
    slots, half = got.shape[0], got.shape[2]
    return pl.pallas_call(
        tile_kernel,
        name="tile_sum",
        out_shape=(
            jax.ShapeDtypeStruct((TILE, TILE, channels), jnp.float32),
            jax.ShapeDtypeStruct((8, half), jnp.float32),
        ),
        grid_spec=pltpu.PrefetchScalarGridSpec(
            num_scalar_prefetch=3,
            grid=(steps,),
            in_specs=[
                pl.BlockSpec((slots // steps, SLOT_ROWS, half), lambda g, *refs: (g, 0, 0)),
                pl.BlockSpec(columns.shape, lambda g, *refs: (0, 0, 0)),
            ],
            out_specs=(
                pl.BlockSpec((TILE, TILE, channels), lambda g, *refs: (0, 0, 0)),
                pl.BlockSpec((8, half), lambda g, *refs: (0, 0)),
            ),
            scratch_shapes=[pltpu.VMEM((slots * SLOT_ROWS, half), jnp.float32)],
        ),
        compiler_params=params(48),
        cost_estimate=pl.CostEstimate(
            flops=2 * columns.size * channels, bytes_accessed=17_000_000, transcendentals=0
        ),
    )(base, place, groups, got, columns)


def fields_kernel(tiles_ref, rows_ref, cols_ref, row_weight_ref, col_weight_ref, send_ref, boxes_ref):
    per_box, boxes = tiles_ref.shape
    extent = rows_ref.shape[0]
    pieces = per_box * boxes

    def wide(parts):
        return jnp.concatenate(parts, axis=1)

    targets = wide([tiles_ref[t : t + 1, :].astype(jnp.float32) for t in range(per_box)])
    rows = wide([rows_ref[:, t, :].astype(jnp.float32) for t in range(per_box)])
    cols = wide([cols_ref[:, t, :].astype(jnp.float32) for t in range(per_box)])
    row_weight = [
        wide([row_weight_ref[t, :, a, :].astype(jnp.float32) for t in range(per_box)])
        for a in range(2)
    ]
    col_weight = [
        wide([col_weight_ref[t, :, a, :].astype(jnp.float32) for t in range(per_box)])
        for a in range(2)
    ]
    blank = jnp.zeros((1, pieces), jnp.float32)
    parts = [targets, jnp.zeros((6, pieces), jnp.float32), jnp.ones((1, pieces), jnp.float32)]
    for array in [rows, cols] + row_weight + col_weight:
        parts = parts + [array, blank]
    parts.append(jnp.zeros((8, pieces), jnp.float32))
    fields = jnp.concatenate(parts, axis=0).astype(jnp.bfloat16)
    tile = lax.broadcasted_iota(jnp.int32, (pieces, pieces), 0)
    piece = lax.broadcasted_iota(jnp.int32, (pieces, pieces), 1)
    match = targets.astype(jnp.int32) == tile
    upper = jnp.where(tile < piece, 1.0, 0.0).astype(jnp.bfloat16)
    chosen = jnp.where(match, 1.0, 0.0)
    earlier = jnp.dot(chosen.astype(jnp.bfloat16), upper, preferred_element_type=jnp.float32)
    box = (lax.broadcasted_iota(jnp.int32, (8, pieces), 1) % boxes).astype(jnp.float32)
    slots = []
    for rank in range(2):
        ranked = jnp.where(earlier == float(rank), chosen, 0.0).astype(jnp.bfloat16)
        found = lax.dot_general(
            box.astype(jnp.bfloat16),
            ranked,
            (((1,), (1,)), ((), ())),
            preferred_element_type=jnp.float32,
        )
        boxes_ref[rank : rank + 1, :] = found[:1].astype(jnp.int32)
        slots.append(
            lax.dot_general(
                ranked, fields, (((1,), (1,)), ((), ())), preferred_element_type=jnp.float32
            )
        )
    send_ref[...] = jnp.concatenate(slots, axis=1).astype(jnp.bfloat16)


def describe(tile_ids, corner_rows, corner_cols, row_weight, col_weight):
    pieces = tile_ids.size
    extent = corner_rows.shape[2]
    return pl.pallas_call(
        fields_kernel,
        name="describe",
        out_shape=(
            jax.ShapeDtypeStruct((pieces, 128), jnp.bfloat16),
            jax.ShapeDtypeStruct((2, pieces), jnp.int32),
        ),
        in_specs=[pl.BlockSpec(memory_space=VMEM)] * 5,
        out_specs=(pl.BlockSpec(memory_space=VMEM),) * 2,
        compiler_params=params(8),
        cost_estimate=pl.CostEstimate(flops=10_000_000, bytes_accessed=200_000, transcendentals=0),
    )(
        jnp.transpose(tile_ids),
        jnp.transpose(corner_rows, (2, 1, 0)),
        jnp.transpose(corner_cols, (2, 1, 0)),
        jnp.transpose(row_weight, (1, 2, 3, 0)),
        jnp.transpose(col_weight, (1, 2, 3, 0)),
    )


def arrange(slots, extent):
    count = slots.shape[0]
    groups = count * extent * 2 // GROUP + TILE
    entries = groups * GROUP
    wide = extent + 1
    rows = jnp.where(slots[:, 7:8] > 0.5, slots[:, 8 : 8 + extent], -4.0).astype(jnp.int32)
    pixel = jnp.arange(TILE, dtype=jnp.int32)
    flat = rows.reshape(-1)
    hits = (flat == pixel[:, None]).astype(jnp.int32) + (flat + 1 == pixel[:, None]).astype(jnp.int32)
    tally = jnp.sum(hits, axis=1)
    needed = (tally + GROUP - 1) // GROUP
    ends = jnp.sum(jnp.where(pixel[None, :] <= pixel[:, None], needed[None, :], 0), axis=1)
    start = (ends - needed) * GROUP
    place = jnp.sum((jnp.arange(groups)[:, None] >= ends[None, :-1]).astype(jnp.int32), axis=1)
    entry = order_entries(flat, start, ends * GROUP, entries)
    inside = jnp.arange(entries, dtype=jnp.int32) < ends[-1] * GROUP
    entry = jnp.where(inside, entry, 14)
    owner, code = entry // 16, entry % 16
    line = jnp.minimum(code // 2, extent - 1)
    base = owner * SLOT_ROWS + extent * line
    chosen = (owner[:, None] == jnp.arange(count)).astype(jnp.bfloat16)
    values = jnp.dot(chosen, slots[:, 8:].astype(jnp.bfloat16), preferred_element_type=jnp.float32)
    which = jnp.arange(2 * wide, dtype=jnp.int32)
    wanted = (which[None, :] % wide == line[:, None]) & (which[None, :] // wide == code[:, None] % 2)
    wanted = wanted & (code[:, None] < 2 * extent)
    scale = jnp.sum(jnp.where(wanted, values[:, 2 * wide : 4 * wide], 0.0), axis=1)
    corner = values[:, wide : 2 * wide]
    low = values[:, 4 * wide : 5 * wide] * scale[:, None]
    high = values[:, 5 * wide : 6 * wide] * scale[:, None]

    def lanes(array):
        return array.reshape(groups, 1, GROUP * wide)

    corner, low, high = lanes(corner), lanes(low), lanes(high)
    position = jnp.arange(TILE, dtype=jnp.float32)[None, :, None]
    columns = jnp.where(position == corner, low, 0.0) + jnp.where(position == corner + 1.0, high, 0.0)
    return base, place, ends[-1:], columns.astype(jnp.bfloat16)


def shards(
    out_grad,
    saved,
    conv_weight,
    conv_bias,
    tile_ids,
    corner_rows,
    corner_cols,
    row_weight,
    col_weight,
):
    boxes, extent, channels = out_grad.shape[0], out_grad.shape[1], out_grad.shape[3]
    layers = saved.shape[0]
    devices = lax.axis_size("row") * lax.axis_size("col")
    grad_scale = 1.0 / math.sqrt(boxes * devices * extent * extent)
    slots, box_of_slot = describe(tile_ids, corner_rows, corner_cols, row_weight, col_weight)
    slots = lax.all_to_all(
        slots.reshape(devices, 1, -1), AXES, split_axis=0, concat_axis=0, tiled=True
    )

    grad_t = jnp.transpose(out_grad, (1, 2, 0, 3))
    saved_t = jnp.transpose(saved, (0, 2, 3, 1, 4))
    slope, crops, biases = conv_chain(grad_t, saved_t, conv_weight, conv_bias)
    terms = weight_terms(slope, saved_t)
    terms, slots = lax.optimization_barrier((terms, slots))
    lines = terms.size // layers // (channels // 2)
    terms = terms.reshape(layers, 4, lines // 4, channels // 2)
    held, sent = sum_lines(terms)
    tail = jnp.pad(biases.reshape(layers * 2, channels // 2), ((0, 2), (0, 0)))
    send = pack(box_of_slot.reshape(-1), crops, tail, boxes)
    arrived = [lax.ppermute(sent[k - 1], "row", hop_x(k)) for k in range(1, 4)]
    send, arrived, slots = lax.optimization_barrier((send, arrived, slots))
    got = lax.all_to_all(send, AXES, split_axis=0, concat_axis=0, tiled=True)
    part = lax.psum(finish_lines(held, arrived).astype(jnp.bfloat16), "col")

    base, place, groups, columns = arrange(slots.reshape(2 * devices, -1).astype(jnp.float32), extent)
    got, part, columns = lax.optimization_barrier((got, part, columns))
    feature_grad, spare = tile_sum(base, place, groups, got, columns, channels)
    own, other = gather_lines(part)
    weight_grad = widen(own, other, layers, grad_scale)
    bias_grad = (spare[2 : 2 + 2 * layers] * (0.5 * grad_scale)).reshape(layers, channels)
    return (weight_grad, bias_grad, feature_grad)


def solution(mesh):
    in_specs = (
        P(AXES, None, None, None),
        P(None, AXES, None, None, None),
        P(),
        P(),
        P(AXES, None),
        P(AXES, None, None),
        P(AXES, None, None),
        P(AXES, None, None, None),
        P(AXES, None, None, None),
    )
    out_specs = (P(), P(), P("row", "col", None))
    return jax.shard_map(shards, mesh=mesh, in_specs=in_specs, out_specs=out_specs, check_vma=False)
```

```python
import functools
import math

import jax
import jax.numpy as jnp
from jax import lax
from jax.experimental import pallas as pl
from jax.experimental.pallas import tpu as pltpu
from jax.sharding import PartitionSpec as P

TILE = 64
SLOT_ROWS = 104
SUM_ROWS = 40
GROUP = 32
UNROLL = 8
VMEM = pltpu.MemorySpace.VMEM
SMEM = pltpu.MemorySpace.SMEM
AXES = ("row", "col")


def params(megabytes):
    return pltpu.CompilerParams(vmem_limit_bytes=megabytes * 1024 * 1024)


def gelu_slope(pre_act):
    normal_cdf = 0.5 * (1.0 + lax.erf(pre_act * 0.7071067811865476))
    return normal_cdf + pre_act * jnp.exp(-0.5 * pre_act * pre_act) * 0.3989422804014327


def chain_kernel(
    grad_ref, saved_ref, weight_ref, bias_ref, slope_ref, crops_ref, biases_ref, padded, slopes, flow
):
    extent, boxes, channels = grad_ref.shape[0], grad_ref.shape[2], grad_ref.shape[3]
    rows = extent * boxes
    padded[...] = jnp.zeros_like(padded)
    slopes[...] = jnp.zeros_like(slopes)
    for layer in (1, 0):
        padded[1 : extent + 1, 1 : extent + 1] = saved_ref[layer]

        def forward(i, sums, layer=layer):
            pieces = [
                padded[i + a, b : b + extent].reshape(rows, channels)
                for a in range(3)
                for b in range(3)
            ]
            pre = jnp.dot(
                jnp.concatenate(pieces, axis=1),
                weight_ref[layer].reshape(9 * channels, channels),
                preferred_element_type=jnp.float32,
            )
            pre = pre + bias_ref[layer : layer + 1, :]
            upper = grad_ref[i] if layer == 1 else flow[i]
            upper = upper.reshape(rows, channels).astype(jnp.float32)
            slope = (upper * gelu_slope(pre)).astype(jnp.bfloat16)
            slopes[i + 1, 1 : extent + 1] = slope.reshape(extent, boxes, channels)
            slope_ref[layer, i] = slope.reshape(extent, boxes, channels)
            return sums + jnp.sum(
                slope.astype(jnp.float32).reshape(rows // 8, 8, channels), axis=0
            )

        sums = lax.fori_loop(0, extent, forward, jnp.zeros((8, channels), jnp.float32))
        biases_ref[layer : layer + 1, :] = jnp.sum(sums, axis=0, keepdims=True)

        def backward(i, carry, layer=layer):
            total = jnp.zeros((rows, channels), jnp.float32)
            for a in range(3):
                for b in range(3):
                    piece = slopes[i + 2 - a, 2 - b : 2 - b + extent].reshape(rows, channels)
                    total = total + lax.dot_general(
                        piece,
                        weight_ref[layer, 3 * a + b],
                        (((1,), (1,)), ((), ())),
                        preferred_element_type=jnp.float32,
                    )
            if layer == 1:
                flow[i] = total.astype(jnp.bfloat16).reshape(extent, boxes, channels)
            else:
                place = pl.ds(pl.multiple_of(i * rows, 8), rows)
                crops_ref[0, place, :] = total[:, : channels // 2]
                crops_ref[1, place, :] = total[:, channels // 2 :]
            return carry

        lax.fori_loop(0, extent, backward, 0)


def conv_chain(grad_t, saved_t, weight, bias):
    extent, boxes, channels = grad_t.shape[0], grad_t.shape[2], grad_t.shape[3]
    layers = saved_t.shape[0]
    padded = (extent + 2, extent + 2, boxes, channels)
    return pl.pallas_call(
        chain_kernel,
        name="conv_chain",
        out_shape=(
            jax.ShapeDtypeStruct((layers, extent, extent, boxes, channels), jnp.bfloat16),
            jax.ShapeDtypeStruct((2, extent * extent * boxes, channels // 2), jnp.float32),
            jax.ShapeDtypeStruct((layers, channels), jnp.float32),
        ),
        in_specs=[pl.BlockSpec(memory_space=VMEM)] * 4,
        out_specs=(pl.BlockSpec(memory_space=VMEM),) * 3,
        scratch_shapes=[
            pltpu.VMEM(padded, jnp.bfloat16),
            pltpu.VMEM(padded, jnp.bfloat16),
            pltpu.VMEM((extent, extent, boxes, channels), jnp.bfloat16),
        ],
        compiler_params=params(40),
        cost_estimate=pl.CostEstimate(flops=15000000000, bytes_accessed=5000000, transcendentals=0),
    )(grad_t, saved_t, weight, bias)


def pack_kernel(box_ref, crops_ref, tail_ref, sums_ref, out_ref, staged):
    count = out_ref.shape[0]
    boxes = staged.shape[0]
    bins = crops_ref.shape[1] // boxes
    owners = box_ref.shape[0] // 2
    step = pl.program_id(0)

    @pl.when(step == 0)
    def _():
        for box in range(boxes):
            for half in range(2):
                staged[box, half * bins : (half + 1) * bins, :] = crops_ref[
                    half, pl.ds(box, bins, stride=boxes), :
                ]
            staged[box, 2 * bins :, :] = tail_ref[...]

    def place(index, carry):
        owner = step * count + index
        out_ref[index] = jnp.concatenate(
            [staged[box_ref[owner]], staged[box_ref[owners + owner]], sums_ref[index]], axis=0
        ).astype(jnp.bfloat16)
        return carry

    lax.fori_loop(0, count, place, 0, unroll=4)


def pack(box_of_slot, crops, tail, sums, boxes):
    owners = sums.shape[0]
    steps = 8
    half = crops.shape[2]
    rows = 2 * SLOT_ROWS + SUM_ROWS
    return pl.pallas_call(
        pack_kernel,
        name="pack",
        out_shape=jax.ShapeDtypeStruct((owners, rows, half), jnp.bfloat16),
        grid_spec=pltpu.PrefetchScalarGridSpec(
            num_scalar_prefetch=1,
            grid=(steps,),
            in_specs=[
                pl.BlockSpec(crops.shape, lambda g, ids: (0, 0, 0)),
                pl.BlockSpec(tail.shape, lambda g, ids: (0, 0)),
                pl.BlockSpec((owners // steps, SUM_ROWS, half), lambda g, ids: (g, 0, 0)),
            ],
            out_specs=pl.BlockSpec((owners // steps, rows, half), lambda g, ids: (g, 0, 0)),
            scratch_shapes=[pltpu.VMEM((boxes, SLOT_ROWS, half), jnp.float32)],
        ),
        compiler_params=params(56),
        cost_estimate=pl.CostEstimate(flops=1_000_000, bytes_accessed=9_000_000, transcendentals=0),
    )(box_of_slot, crops, tail, sums)


def weight_kernel(slope_ref, saved_ref, out_ref, padded):
    extent, boxes, channels = saved_ref.shape[1], saved_ref.shape[3], saved_ref.shape[4]
    bins = extent * extent * boxes
    offset = pl.program_id(1)

    @pl.when(offset == 0)
    def _():
        padded[...] = jnp.zeros_like(padded)
        padded[1 : extent + 1, 1 : extent + 1] = saved_ref[0]

    a, b = offset // 3, offset % 3
    piece = padded[pl.ds(a, extent), pl.ds(b, extent)].reshape(bins, channels)
    term = lax.dot_general(
        piece,
        slope_ref[0].reshape(bins, channels),
        (((0,), (0,)), ((), ())),
        preferred_element_type=jnp.float32,
    )
    out_ref[0, 0, 0] = term[:, : channels // 2].astype(jnp.bfloat16)
    out_ref[0, 1, 0] = term[:, channels // 2 :].astype(jnp.bfloat16)


def weight_terms(slope, saved_t):
    layers, extent, boxes, channels = slope.shape[0], slope.shape[1], slope.shape[3], slope.shape[4]
    block = (1, extent, extent, boxes, channels)
    return pl.pallas_call(
        weight_kernel,
        name="weight_terms",
        out_shape=jax.ShapeDtypeStruct((layers, 2, 9, channels, channels // 2), jnp.bfloat16),
        grid=(layers, 9),
        in_specs=[pl.BlockSpec(block, lambda l, o: (l, 0, 0, 0, 0))] * 2,
        out_specs=pl.BlockSpec((1, 2, 1, channels, channels // 2), lambda l, o: (l, 0, o, 0, 0)),
        scratch_shapes=[pltpu.VMEM((extent + 2, extent + 2, boxes, channels), jnp.bfloat16)],
        compiler_params=params(24),
        cost_estimate=pl.CostEstimate(flops=7400000000, bytes_accessed=5000000, transcendentals=0),
    )(slope, saved_t)


def hop_core():
    return [(r, r ^ 1) for r in range(8)]


def hop_x(k):
    return [(r, (r // 2 + k) % 4 * 2 + r % 2) for r in range(8)]


def hop_y(k):
    return [(c, c // 4 * 4 + (c % 4 + k) % 4) for c in range(16)]


def hop_z(k):
    return [(c, (c // 4 + k) % 4 * 4 + c % 4) for c in range(16)]


def pick(array, index):
    return lax.dynamic_index_in_dim(array, index, 0, keepdims=False)


def sum_chip(terms, owners):
    core = lax.axis_index("row") % 2
    other = lax.ppermute(pick(terms, 1 - core), "row", hop_core())
    total = pick(terms, core).astype(jnp.float32) + other.astype(jnp.float32)
    total = jnp.pad(total, ((0, owners * SUM_ROWS - total.shape[0]), (0, 0)))
    return total.reshape(owners, SUM_ROWS, total.shape[1])


def ring(part, name, hop):
    return jnp.stack([part] + [lax.ppermute(part, name, hop(k)) for k in (3, 2, 1)])


def widen_kernel(place_ref, own_ref, other_ref, out_ref, *, scale):
    length, half = out_ref.shape[1], out_ref.shape[2] // 2
    turns = [[lax.rem(q + 4 - place_ref[axis], 4) for q in range(4)] for axis in range(3)]

    def copy(core, source_ref):
        for x in range(4):
            for z in range(4):
                for y in range(4):
                    start = (((x * 2 + core) * 4 + z) * 4 + y) * SUM_ROWS
                    values = source_ref[turns[0][x], turns[1][y], turns[2][z]].astype(jnp.float32)
                    values = values * scale
                    for column in range(2):
                        low = max(start, column * length)
                        high = min(start + SUM_ROWS, (column + 1) * length)
                        if low < high:
                            out_ref[
                                :,
                                low - column * length : high - column * length,
                                column * half : (column + 1) * half,
                            ] = values[:, low - start : high - start, :]

    for core in range(2):

        @pl.when(place_ref[3] == core)
        def _(core=core):
            copy(core, own_ref)
            copy(1 - core, other_ref)


def widen(own, other, length, scale):
    row, col = lax.axis_index("row"), lax.axis_index("col")
    place = jnp.stack([row // 2, col % 4, col // 4, row % 2]).astype(jnp.int32)
    layers, half = own.shape[3], own.shape[5]
    return pl.pallas_call(
        functools.partial(widen_kernel, scale=scale),
        name="widen",
        out_shape=jax.ShapeDtypeStruct((layers, length, 2 * half), jnp.float32),
        in_specs=[
            pl.BlockSpec(memory_space=SMEM),
            pl.BlockSpec(memory_space=VMEM),
            pl.BlockSpec(memory_space=VMEM),
        ],
        out_specs=pl.BlockSpec(memory_space=VMEM),
        compiler_params=params(24),
        cost_estimate=pl.CostEstimate(flops=3_000_000, bytes_accessed=10_000_000, transcendentals=0),
    )(place, own, other)


def order_kernel(rows_ref, start_ref, end_ref, entry_ref, count):
    places = start_ref.shape[0]
    extent = 7
    slots = rows_ref.shape[0] // extent

    def begin(p, carry):
        count[p] = start_ref[p]
        return carry

    lax.fori_loop(0, places, begin, 0)

    def enter(slot, carry):
        @pl.when(rows_ref[slot * extent] >= 0)
        def _():
            for i in range(extent):
                first = rows_ref[slot * extent + i]
                for a in range(2):
                    n = count[first + a]
                    count[first + a] = n + 1
                    entry_ref[n] = slot * 16 + 2 * i + a

        return carry

    lax.fori_loop(0, slots, enter, 0)

    def fill(p, carry):
        def blank(n, inner):
            entry_ref[n] = 14
            return inner

        return lax.fori_loop(count[p], end_ref[p], blank, carry)

    lax.fori_loop(0, places, fill, 0)


def order_entries(rows, start, end, entries):
    return pl.pallas_call(
        order_kernel,
        name="order_entries",
        out_shape=jax.ShapeDtypeStruct((entries,), jnp.int32),
        in_specs=[pl.BlockSpec(memory_space=SMEM)] * 3,
        out_specs=pl.BlockSpec(memory_space=SMEM),
        scratch_shapes=[pltpu.SMEM((TILE,), jnp.int32)],
        cost_estimate=pl.CostEstimate(flops=10_000_000, bytes_accessed=30_000_000, transcendentals=0),
    )(rows, start, end)


def tile_kernel(
    base_ref, place_ref, groups_ref, got_ref, columns_ref, out_ref, biases_ref, crops
):
    step = pl.program_id(0)
    owners, half = got_ref.shape[0], got_ref.shape[2]
    bins = 49
    block = 2 * owners * SLOT_ROWS
    wide = got_ref[...].astype(jnp.float32)[:, : 2 * SLOT_ROWS, :]
    crops[pl.ds(pl.multiple_of(step * block, 8), block), :] = wide.reshape(block, half)
    spare = jnp.sum(wide[:, SLOT_ROWS - 8 : SLOT_ROWS, :], axis=0)

    @pl.when(step == 0)
    def _():
        biases_ref[...] = spare

    @pl.when(step > 0)
    def _():
        biases_ref[...] += spare

    @pl.when(step == pl.num_programs(0) - 1)
    def _():
        out_ref[...] = jnp.zeros_like(out_ref)

        def group(t):
            left, right = [], []
            for n in range(GROUP):
                base = base_ref[t * GROUP + n]
                left.append(crops[pl.ds(base, 8), :])
                right.append(crops[pl.ds(base + bins, 8), :])
            values = jnp.concatenate(
                [jnp.concatenate(left, axis=0), jnp.concatenate(right, axis=0)], axis=1
            ).astype(jnp.bfloat16)
            return jnp.dot(columns_ref[t], values, preferred_element_type=jnp.float32)

        def several(t, carry):
            terms = [group(t * UNROLL + u) for u in range(UNROLL)]
            for u in range(UNROLL):
                out_ref[place_ref[t * UNROLL + u]] += terms[u]
            return carry

        lax.fori_loop(0, (groups_ref[0] + UNROLL - 1) // UNROLL, several, 0)


def tile_sum(base, place, groups, got, columns, channels):
    steps = 8
    owners, rows, half = got.shape
    return pl.pallas_call(
        tile_kernel,
        name="tile_sum",
        out_shape=(
            jax.ShapeDtypeStruct((TILE, TILE, channels), jnp.float32),
            jax.ShapeDtypeStruct((8, half), jnp.float32),
        ),
        grid_spec=pltpu.PrefetchScalarGridSpec(
            num_scalar_prefetch=3,
            grid=(steps,),
            in_specs=[
                pl.BlockSpec((owners // steps, rows, half), lambda g, *refs: (g, 0, 0)),
                pl.BlockSpec(columns.shape, lambda g, *refs: (0, 0, 0)),
            ],
            out_specs=(
                pl.BlockSpec((TILE, TILE, channels), lambda g, *refs: (0, 0, 0)),
                pl.BlockSpec((8, half), lambda g, *refs: (0, 0)),
            ),
            scratch_shapes=[pltpu.VMEM((2 * owners * SLOT_ROWS, half), jnp.float32)],
        ),
        compiler_params=params(48),
        cost_estimate=pl.CostEstimate(
            flops=2 * columns.size * channels, bytes_accessed=17_000_000, transcendentals=0
        ),
    )(base, place, groups, got, columns)


def fields_kernel(tiles_ref, rows_ref, cols_ref, row_weight_ref, col_weight_ref, send_ref, boxes_ref):
    per_box, boxes = tiles_ref.shape
    extent = rows_ref.shape[0]
    pieces = per_box * boxes

    def wide(parts):
        return jnp.concatenate(parts, axis=1)

    targets = wide([tiles_ref[t : t + 1, :].astype(jnp.float32) for t in range(per_box)])
    rows = wide([rows_ref[:, t, :].astype(jnp.float32) for t in range(per_box)])
    cols = wide([cols_ref[:, t, :].astype(jnp.float32) for t in range(per_box)])
    row_weight = [
        wide([row_weight_ref[t, :, a, :].astype(jnp.float32) for t in range(per_box)])
        for a in range(2)
    ]
    col_weight = [
        wide([col_weight_ref[t, :, a, :].astype(jnp.float32) for t in range(per_box)])
        for a in range(2)
    ]
    blank = jnp.zeros((1, pieces), jnp.float32)
    parts = [targets, jnp.zeros((6, pieces), jnp.float32), jnp.ones((1, pieces), jnp.float32)]
    for array in [rows, cols] + row_weight + col_weight:
        parts = parts + [array, blank]
    parts.append(jnp.zeros((8, pieces), jnp.float32))
    fields = jnp.concatenate(parts, axis=0).astype(jnp.bfloat16)
    tile = lax.broadcasted_iota(jnp.int32, (pieces, pieces), 0)
    piece = lax.broadcasted_iota(jnp.int32, (pieces, pieces), 1)
    match = targets.astype(jnp.int32) == tile
    upper = jnp.where(tile < piece, 1.0, 0.0).astype(jnp.bfloat16)
    chosen = jnp.where(match, 1.0, 0.0)
    earlier = jnp.dot(chosen.astype(jnp.bfloat16), upper, preferred_element_type=jnp.float32)
    box = (lax.broadcasted_iota(jnp.int32, (8, pieces), 1) % boxes).astype(jnp.float32)
    slots = []
    for rank in range(2):
        ranked = jnp.where(earlier == float(rank), chosen, 0.0).astype(jnp.bfloat16)
        found = lax.dot_general(
            box.astype(jnp.bfloat16),
            ranked,
            (((1,), (1,)), ((), ())),
            preferred_element_type=jnp.float32,
        )
        boxes_ref[rank : rank + 1, :] = found[:1].astype(jnp.int32)
        slots.append(
            lax.dot_general(
                ranked, fields, (((1,), (1,)), ((), ())), preferred_element_type=jnp.float32
            )
        )
    send_ref[...] = jnp.concatenate(slots, axis=1).astype(jnp.bfloat16)


def describe(tile_ids, corner_rows, corner_cols, row_weight, col_weight):
    pieces = tile_ids.size
    extent = corner_rows.shape[2]
    return pl.pallas_call(
        fields_kernel,
        name="describe",
        out_shape=(
            jax.ShapeDtypeStruct((pieces, 128), jnp.bfloat16),
            jax.ShapeDtypeStruct((2, pieces), jnp.int32),
        ),
        in_specs=[pl.BlockSpec(memory_space=VMEM)] * 5,
        out_specs=(pl.BlockSpec(memory_space=VMEM),) * 2,
        compiler_params=params(8),
        cost_estimate=pl.CostEstimate(flops=10_000_000, bytes_accessed=200_000, transcendentals=0),
    )(
        jnp.transpose(tile_ids),
        jnp.transpose(corner_rows, (2, 1, 0)),
        jnp.transpose(corner_cols, (2, 1, 0)),
        jnp.transpose(row_weight, (1, 2, 3, 0)),
        jnp.transpose(col_weight, (1, 2, 3, 0)),
    )


def arrange(slots, extent):
    count = slots.shape[0]
    groups = count * extent * 2 // GROUP + TILE
    entries = groups * GROUP
    wide = extent + 1
    rows = jnp.where(slots[:, 7:8] > 0.5, slots[:, 8 : 8 + extent], -4.0).astype(jnp.int32)
    pixel = jnp.arange(TILE, dtype=jnp.int32)
    flat = rows.reshape(-1)
    hits = (flat == pixel[:, None]).astype(jnp.int32) + (flat + 1 == pixel[:, None]).astype(jnp.int32)
    tally = jnp.sum(hits, axis=1)
    needed = (tally + GROUP - 1) // GROUP
    ends = jnp.sum(jnp.where(pixel[None, :] <= pixel[:, None], needed[None, :], 0), axis=1)
    start = (ends - needed) * GROUP
    place = jnp.sum((jnp.arange(groups)[:, None] >= ends[None, :-1]).astype(jnp.int32), axis=1)
    entry = order_entries(flat, start, ends * GROUP, entries)
    inside = jnp.arange(entries, dtype=jnp.int32) < ends[-1] * GROUP
    entry = jnp.where(inside, entry, 14)
    owner, code = entry // 16, entry % 16
    line = jnp.minimum(code // 2, extent - 1)
    base = owner * SLOT_ROWS + extent * line
    chosen = (owner[:, None] == jnp.arange(count)).astype(jnp.bfloat16)
    values = jnp.dot(chosen, slots[:, 8:].astype(jnp.bfloat16), preferred_element_type=jnp.float32)
    which = jnp.arange(2 * wide, dtype=jnp.int32)
    wanted = (which[None, :] % wide == line[:, None]) & (which[None, :] // wide == code[:, None] % 2)
    wanted = wanted & (code[:, None] < 2 * extent)
    scale = jnp.sum(jnp.where(wanted, values[:, 2 * wide : 4 * wide], 0.0), axis=1)
    corner = values[:, wide : 2 * wide]
    low = values[:, 4 * wide : 5 * wide] * scale[:, None]
    high = values[:, 5 * wide : 6 * wide] * scale[:, None]

    def lanes(array):
        return array.reshape(groups, 1, GROUP * wide)

    corner, low, high = lanes(corner), lanes(low), lanes(high)
    position = jnp.arange(TILE, dtype=jnp.float32)[None, :, None]
    columns = jnp.where(position == corner, low, 0.0) + jnp.where(position == corner + 1.0, high, 0.0)
    return base, place, ends[-1:], columns.astype(jnp.bfloat16)


def shards(
    out_grad,
    saved,
    conv_weight,
    conv_bias,
    tile_ids,
    corner_rows,
    corner_cols,
    row_weight,
    col_weight,
):
    boxes, extent, channels = out_grad.shape[0], out_grad.shape[1], out_grad.shape[3]
    layers = saved.shape[0]
    devices = lax.axis_size("row") * lax.axis_size("col")
    grad_scale = 1.0 / math.sqrt(boxes * devices * extent * extent)
    slots, box_of_slot = describe(tile_ids, corner_rows, corner_cols, row_weight, col_weight)
    slots = lax.all_to_all(
        slots.reshape(devices, 1, -1), AXES, split_axis=0, concat_axis=0, tiled=True
    )

    grad_t = jnp.transpose(out_grad, (1, 2, 0, 3))
    saved_t = jnp.transpose(saved, (0, 2, 3, 1, 4))
    slope, crops, biases = conv_chain(grad_t, saved_t, conv_weight, conv_bias)
    terms = weight_terms(slope, saved_t)
    terms, slots = lax.optimization_barrier((terms, slots))
    sums = sum_chip(terms.reshape(layers, -1, channels // 2), devices)
    tail = jnp.pad(biases.reshape(layers * 2, channels // 2), ((0, 2), (0, 0)))
    send = pack(box_of_slot.reshape(-1), crops, tail, sums, boxes)
    send, slots = lax.optimization_barrier((send, slots))
    got = lax.all_to_all(send, AXES, split_axis=0, concat_axis=0, tiled=True)

    base, place, groups, columns = arrange(slots.reshape(2 * devices, -1).astype(jnp.float32), extent)
    got, columns = lax.optimization_barrier((got, columns))
    cols = lax.axis_size("col")
    arrived = got[:, 2 * SLOT_ROWS :, :].reshape(-1, layers, cols, SUM_ROWS, channels // 2)
    part = jnp.sum(arrived.astype(jnp.float32), axis=(0, 2)).astype(jnp.bfloat16)
    part = ring(ring(part, "col", hop_z), "col", hop_y)
    part, got = lax.optimization_barrier((part, got))
    own = ring(part, "row", hop_x)
    feature_grad, spare = tile_sum(base, place, groups, got, columns, channels)
    own, feature_grad = lax.optimization_barrier((own, feature_grad))
    other = lax.ppermute(own, "row", hop_core())
    weight_grad = widen(own, other, 9 * channels, grad_scale)
    bias_grad = (spare[2 : 2 + 2 * layers] * grad_scale).reshape(layers, channels)
    return (weight_grad, bias_grad, feature_grad)


def solution(mesh):
    in_specs = (
        P(AXES, None, None, None),
        P(None, AXES, None, None, None),
        P(),
        P(),
        P(AXES, None),
        P(AXES, None, None),
        P(AXES, None, None),
        P(AXES, None, None, None),
        P(AXES, None, None, None),
    )
    out_specs = (P(), P(), P("row", "col", None))
    return jax.shard_map(shards, mesh=mesh, in_specs=in_specs, out_specs=out_specs, check_vma=False)
```

```python
import functools
import math

import jax
import jax.numpy as jnp
from jax import lax
from jax.experimental import pallas as pl
from jax.experimental.pallas import tpu as pltpu
from jax.sharding import PartitionSpec as P

TILE = 64
SUM_ROWS = 40
GROUP = 32
UNROLL = 8
VMEM = pltpu.MemorySpace.VMEM
SMEM = pltpu.MemorySpace.SMEM
AXES = ("row", "col")


def params(megabytes):
    return pltpu.CompilerParams(vmem_limit_bytes=megabytes * 1024 * 1024)


def gelu_slope(pre_act):
    normal_cdf = 0.5 * (1.0 + lax.erf(pre_act * 0.7071067811865476))
    return normal_cdf + pre_act * jnp.exp(-0.5 * pre_act * pre_act) * 0.3989422804014327


def chain_kernel(
    grad_hbm,
    saved_hbm,
    weight_hbm,
    bias_ref,
    slope_ref,
    crops_ref,
    biases_ref,
    both,
    slopes,
    flow,
    grad_ref,
    weight_ref,
    sems,
):
    extent, boxes, channels = grad_ref.shape[0], grad_ref.shape[2], grad_ref.shape[3]
    rows = extent * boxes
    inner = pl.ds(1, extent)
    fetches = {}
    for layer in (1, 0):
        fetches[layer] = [
            pltpu.make_async_copy(
                saved_hbm.at[layer], both.at[layer, inner, inner], sems.at[2 * layer]
            ),
            pltpu.make_async_copy(
                weight_hbm.at[layer], weight_ref.at[layer], sems.at[2 * layer + 1]
            ),
        ]
    fetches[1].append(pltpu.make_async_copy(grad_hbm, grad_ref, sems.at[4]))
    for layer in (1, 0):
        for fetch in fetches[layer]:
            fetch.start()
    slopes[...] = jnp.zeros_like(slopes)
    edge = jnp.zeros((extent + 2, boxes, channels), jnp.bfloat16)
    for layer in (1, 0):
        for end in (0, extent + 1):
            both[layer, end] = edge
            both[layer, 1 : extent + 1, end] = edge[:extent]
    for layer in (1, 0):
        padded = both.at[layer]
        for fetch in fetches[layer]:
            fetch.wait()

        def forward(i, sums, layer=layer, padded=padded):
            pieces = [
                padded[i + a, b : b + extent].reshape(rows, channels)
                for a in range(3)
                for b in range(3)
            ]
            pre = jnp.dot(
                jnp.concatenate(pieces, axis=1),
                weight_ref[layer].reshape(9 * channels, channels),
                preferred_element_type=jnp.float32,
            )
            pre = pre + bias_ref[layer : layer + 1, :]
            upper = grad_ref[i] if layer == 1 else flow[i]
            upper = upper.reshape(rows, channels).astype(jnp.float32)
            slope = (upper * gelu_slope(pre)).astype(jnp.bfloat16)
            slopes[i + 1, 1 : extent + 1] = slope.reshape(extent, boxes, channels)
            slope_ref[layer, i] = slope.reshape(extent, boxes, channels)
            return sums + jnp.sum(
                slope.astype(jnp.float32).reshape(rows // 8, 8, channels), axis=0
            )

        sums = jnp.zeros((8, channels), jnp.float32)
        for i in range(extent):
            sums = forward(i, sums)
        biases_ref[layer : layer + 1, :] = jnp.sum(sums, axis=0, keepdims=True)

        def backward(i, carry, layer=layer):
            total = jnp.zeros((rows, channels), jnp.float32)
            for a in range(3):
                for b in range(3):
                    piece = slopes[i + 2 - a, 2 - b : 2 - b + extent].reshape(rows, channels)
                    total = total + lax.dot_general(
                        piece,
                        weight_ref[layer, 3 * a + b],
                        (((1,), (1,)), ((), ())),
                        preferred_element_type=jnp.float32,
                    )
            if layer == 1:
                flow[i] = total.astype(jnp.bfloat16).reshape(extent, boxes, channels)
            else:
                place = pl.ds(i * rows, rows)
                crops_ref[0, place, :] = total[:, : channels // 2]
                crops_ref[1, place, :] = total[:, channels // 2 :]
            return carry

        for i in range(extent):
            backward(i, 0)


def conv_chain(grad_t, saved_t, weight, bias):
    extent, boxes, channels = grad_t.shape[0], grad_t.shape[2], grad_t.shape[3]
    layers = saved_t.shape[0]
    padded = (extent + 2, extent + 2, boxes, channels)
    return pl.pallas_call(
        chain_kernel,
        name="conv_chain",
        out_shape=(
            jax.ShapeDtypeStruct((layers, extent, extent, boxes, channels), jnp.bfloat16),
            jax.ShapeDtypeStruct((2, extent * extent * boxes, channels // 2), jnp.float32),
            jax.ShapeDtypeStruct((layers, channels), jnp.float32),
        ),
        in_specs=[pl.BlockSpec(memory_space=pl.ANY)] * 3 + [pl.BlockSpec(memory_space=VMEM)],
        out_specs=(pl.BlockSpec(memory_space=VMEM),) * 3,
        scratch_shapes=[
            pltpu.VMEM((layers,) + padded, jnp.bfloat16),
            pltpu.VMEM(padded, jnp.bfloat16),
            pltpu.VMEM((extent, extent, boxes, channels), jnp.bfloat16),
            pltpu.VMEM(grad_t.shape, jnp.bfloat16),
            pltpu.VMEM(weight.shape, jnp.bfloat16),
            pltpu.SemaphoreType.DMA((5,)),
        ],
        compiler_params=params(56),
        cost_estimate=pl.CostEstimate(flops=15000000000, bytes_accessed=5000000, transcendentals=0),
    )(grad_t, saved_t, weight, bias)


def pack_kernel(box_ref, crops_ref, tail_ref, sums_ref, out_ref, first, second, staged):
    count = out_ref.shape[0]
    boxes = first.shape[0]
    bins = crops_ref.shape[1] // boxes
    owners = box_ref.shape[0] // 2
    step = pl.program_id(0)

    @pl.when(step == 0)
    def _():
        staged[...] = jnp.zeros_like(staged)
        for box in range(boxes):
            for half in range(2):
                rows = crops_ref[half, pl.ds(box, bins, stride=boxes), :]
                staged[0, box, half * bins : (half + 1) * bins, :] = rows
                staged[1, box, half * bins + 2 : (half + 1) * bins + 2, :] = rows
            staged[1, box, 2 * bins + 2 : 2 * bins + 6, :] = tail_ref[...]
            first[box] = staged[0, box].astype(jnp.bfloat16)
            second[box] = staged[1, box].astype(jnp.bfloat16)

    def both(left, right):
        return (left.astype(jnp.float32) + right.astype(jnp.float32)).astype(jnp.bfloat16)

    def place(index, carry):
        owner = step * count + index
        one, two = first[box_ref[owner]], second[box_ref[owners + owner]]
        sums = sums_ref[index]
        out_ref[index] = jnp.concatenate(
            [
                one[:96],
                both(one[96:112], two[:16]),
                two[16:96],
                both(two[96:112], sums[:16]),
                sums[16:48],
            ],
            axis=0,
        )
        return carry

    lax.fori_loop(0, count, place, 0, unroll=4)


def pack(box_of_slot, crops, tail, sums, boxes):
    owners = sums.shape[0]
    steps = 8
    half = crops.shape[2]
    rows = 200 + SUM_ROWS
    sums = jnp.pad(sums.astype(jnp.bfloat16), ((0, 0), (8, 0), (0, 0)))
    return pl.pallas_call(
        pack_kernel,
        name="pack",
        out_shape=jax.ShapeDtypeStruct((owners, rows, half), jnp.bfloat16),
        grid_spec=pltpu.PrefetchScalarGridSpec(
            num_scalar_prefetch=1,
            grid=(steps,),
            in_specs=[
                pl.BlockSpec(crops.shape, lambda g, ids: (0, 0, 0)),
                pl.BlockSpec(tail.shape, lambda g, ids: (0, 0)),
                pl.BlockSpec((owners // steps, 8 + SUM_ROWS, half), lambda g, ids: (g, 0, 0)),
            ],
            out_specs=pl.BlockSpec((owners // steps, rows, half), lambda g, ids: (g, 0, 0)),
            scratch_shapes=[
                pltpu.VMEM((boxes, 112, half), jnp.bfloat16),
                pltpu.VMEM((boxes, 112, half), jnp.bfloat16),
                pltpu.VMEM((2, boxes, 112, half), jnp.float32),
            ],
        ),
        compiler_params=params(56),
        cost_estimate=pl.CostEstimate(flops=1_000_000, bytes_accessed=9_000_000, transcendentals=0),
    )(box_of_slot, crops, tail, sums)


def weight_kernel(slope_ref, saved_ref, out_ref, padded):
    extent, boxes, channels = saved_ref.shape[1], saved_ref.shape[3], saved_ref.shape[4]
    bins = extent * extent * boxes
    step = pl.program_id(1)

    @pl.when(step == 0)
    def _():
        padded[...] = jnp.zeros_like(padded)
        padded[1 : extent + 1, 1 : extent + 1] = saved_ref[0]

    for k in range(9):
        a, b = k // 3, k % 3
        piece = padded[pl.ds(a, extent), pl.ds(b, extent)].reshape(bins, channels)
        term = lax.dot_general(
            piece,
            slope_ref[0].reshape(bins, channels),
            (((0,), (0,)), ((), ())),
            preferred_element_type=jnp.float32,
        )
        out_ref[0, 0, k] = term[:, : channels // 2].astype(jnp.bfloat16)
        out_ref[0, 1, k] = term[:, channels // 2 :].astype(jnp.bfloat16)


def weight_terms(slope, saved_t):
    layers, extent, boxes, channels = slope.shape[0], slope.shape[1], slope.shape[3], slope.shape[4]
    block = (1, extent, extent, boxes, channels)
    return pl.pallas_call(
        weight_kernel,
        name="weight_terms",
        out_shape=jax.ShapeDtypeStruct((layers, 2, 9, channels, channels // 2), jnp.bfloat16),
        grid=(layers, 1),
        in_specs=[pl.BlockSpec(block, lambda l, o: (l, 0, 0, 0, 0))] * 2,
        out_specs=pl.BlockSpec((1, 2, 9, channels, channels // 2), lambda l, o: (l, 0, o, 0, 0)),
        scratch_shapes=[pltpu.VMEM((extent + 2, extent + 2, boxes, channels), jnp.bfloat16)],
        compiler_params=params(24),
        cost_estimate=pl.CostEstimate(flops=7400000000, bytes_accessed=5000000, transcendentals=0),
    )(slope, saved_t)


def hop_core():
    return [(r, r ^ 1) for r in range(8)]


def hop_x(k):
    return [(r, (r // 2 + k) % 4 * 2 + r % 2) for r in range(8)]


def hop_y(k):
    return [(c, c // 4 * 4 + (c % 4 + k) % 4) for c in range(16)]


def hop_z(k):
    return [(c, (c // 4 + k) % 4 * 4 + c % 4) for c in range(16)]


def pick(array, index):
    return lax.dynamic_index_in_dim(array, index, 0, keepdims=False)


def sum_chip(terms, owners):
    core = lax.axis_index("row") % 2
    other = lax.ppermute(pick(terms, 1 - core), "row", hop_core())
    total = pick(terms, core).astype(jnp.float32) + other.astype(jnp.float32)
    total = jnp.pad(total, ((0, owners * SUM_ROWS - total.shape[0]), (0, 0)))
    return total.reshape(owners, SUM_ROWS, total.shape[1])


def ring(part, name, hop):
    return jnp.stack([part] + [lax.ppermute(part, name, hop(k)) for k in (3, 2, 1)])


def widen_kernel(place_ref, own_ref, other_ref, out_ref, *, scale):
    length, half = out_ref.shape[1], out_ref.shape[2] // 2
    turns = [[lax.rem(q + 4 - place_ref[axis], 4) for q in range(4)] for axis in range(3)]

    def copy(core, source_ref):
        for x in range(4):
            for z in range(4):
                for y in range(4):
                    start = (((x * 2 + core) * 4 + z) * 4 + y) * SUM_ROWS
                    values = source_ref[turns[0][x], turns[1][y], turns[2][z]].astype(jnp.float32)
                    values = values * scale
                    for column in range(2):
                        low = max(start, column * length)
                        high = min(start + SUM_ROWS, (column + 1) * length)
                        if low < high:
                            out_ref[
                                :,
                                low - column * length : high - column * length,
                                column * half : (column + 1) * half,
                            ] = values[:, low - start : high - start, :]

    for core in range(2):

        @pl.when(place_ref[3] == core)
        def _(core=core):
            copy(core, own_ref)
            copy(1 - core, other_ref)


def widen(own, other, length, scale):
    row, col = lax.axis_index("row"), lax.axis_index("col")
    place = jnp.stack([row // 2, col % 4, col // 4, row % 2]).astype(jnp.int32)
    layers, half = own.shape[3], own.shape[5]
    return pl.pallas_call(
        functools.partial(widen_kernel, scale=scale),
        name="widen",
        out_shape=jax.ShapeDtypeStruct((layers, length, 2 * half), jnp.float32),
        in_specs=[
            pl.BlockSpec(memory_space=SMEM),
            pl.BlockSpec(memory_space=VMEM),
            pl.BlockSpec(memory_space=VMEM),
        ],
        out_specs=pl.BlockSpec(memory_space=VMEM),
        compiler_params=params(24),
        cost_estimate=pl.CostEstimate(flops=3_000_000, bytes_accessed=10_000_000, transcendentals=0),
    )(place, own, other)


def order_kernel(rows_ref, start_ref, end_ref, entry_ref, count):
    places = start_ref.shape[0]
    extent = 7
    slots = rows_ref.shape[0] // extent

    def begin(p, carry):
        count[p] = start_ref[p]
        return carry

    lax.fori_loop(0, places, begin, 0)

    def enter(slot, carry):
        @pl.when(rows_ref[slot * extent] >= 0)
        def _():
            for i in range(extent):
                first = rows_ref[slot * extent + i]
                for a in range(2):
                    n = count[first + a]
                    count[first + a] = n + 1
                    entry_ref[n] = slot * 16 + 2 * i + a

        return carry

    lax.fori_loop(0, slots, enter, 0)

    def fill(p, carry):
        def blank(n, inner):
            entry_ref[n] = 14
            return inner

        return lax.fori_loop(count[p], end_ref[p], blank, carry)

    lax.fori_loop(0, places, fill, 0)


def order_entries(rows, start, end, entries):
    return pl.pallas_call(
        order_kernel,
        name="order_entries",
        out_shape=jax.ShapeDtypeStruct((entries,), jnp.int32),
        in_specs=[pl.BlockSpec(memory_space=SMEM)] * 3,
        out_specs=pl.BlockSpec(memory_space=SMEM),
        scratch_shapes=[pltpu.SMEM((TILE,), jnp.int32)],
        cost_estimate=pl.CostEstimate(flops=10_000_000, bytes_accessed=30_000_000, transcendentals=0),
    )(rows, start, end)


def tile_kernel(
    base_ref, place_ref, groups_ref, got_ref, columns_hbm, out_ref, biases_ref, crops, columns_ref, sem
):
    step = pl.program_id(0)
    owners, half = got_ref.shape[0], got_ref.shape[2]
    bins = 49
    block = owners * 200
    fetch = pltpu.make_async_copy(columns_hbm, columns_ref, sem)

    @pl.when(step == 0)
    def _():
        fetch.start()

    wide = got_ref[...].astype(jnp.float32)[:, :200, :]
    crops[pl.ds(pl.multiple_of(step * block, 8), block), :] = wide.reshape(block, half)
    spare = jnp.sum(wide[:, 192:, :], axis=0)

    @pl.when(step == 0)
    def _():
        biases_ref[...] = spare

    @pl.when(step > 0)
    def _():
        biases_ref[...] += spare

    @pl.when(step == pl.num_programs(0) - 1)
    def _():
        out_ref[...] = jnp.zeros_like(out_ref)
        fetch.wait()

        def group(t):
            left, right = [], []
            for n in range(GROUP):
                base = base_ref[t * GROUP + n]
                left.append(crops[pl.ds(base, 8), :])
                right.append(crops[pl.ds(base + bins, 8), :])
            values = jnp.concatenate(
                [jnp.concatenate(left, axis=0), jnp.concatenate(right, axis=0)], axis=1
            ).astype(jnp.bfloat16)
            return jnp.dot(columns_ref[t], values, preferred_element_type=jnp.float32)

        def several(t, carry):
            terms = [group(t * UNROLL + u) for u in range(UNROLL)]
            for u in range(UNROLL):
                out_ref[place_ref[t * UNROLL + u]] += terms[u]
            return carry

        lax.fori_loop(0, (groups_ref[0] + UNROLL - 1) // UNROLL, several, 0)


def tile_sum(base, place, groups, got, columns, channels):
    steps = 8
    owners, rows, half = got.shape
    return pl.pallas_call(
        tile_kernel,
        name="tile_sum",
        out_shape=(
            jax.ShapeDtypeStruct((TILE, TILE, channels), jnp.float32),
            jax.ShapeDtypeStruct((8, half), jnp.float32),
        ),
        grid_spec=pltpu.PrefetchScalarGridSpec(
            num_scalar_prefetch=3,
            grid=(steps,),
            in_specs=[
                pl.BlockSpec((owners // steps, rows, half), lambda g, *refs: (g, 0, 0)),
                pl.BlockSpec(memory_space=pl.ANY),
            ],
            out_specs=(
                pl.BlockSpec((TILE, TILE, channels), lambda g, *refs: (0, 0, 0)),
                pl.BlockSpec((8, half), lambda g, *refs: (0, 0)),
            ),
            scratch_shapes=[
                pltpu.VMEM((owners * 200, half), jnp.float32),
                pltpu.VMEM(columns.shape, jnp.bfloat16),
                pltpu.SemaphoreType.DMA(()),
            ],
        ),
        compiler_params=params(48),
        cost_estimate=pl.CostEstimate(
            flops=2 * columns.size * channels, bytes_accessed=17_000_000, transcendentals=0
        ),
    )(base, place, groups, got, columns)


def fields_kernel(tiles_ref, rows_ref, cols_ref, row_weight_ref, col_weight_ref, send_ref, boxes_ref):
    per_box, boxes = tiles_ref.shape
    extent = rows_ref.shape[0]
    pieces = per_box * boxes

    def wide(parts):
        return jnp.concatenate(parts, axis=1)

    targets = wide([tiles_ref[t : t + 1, :].astype(jnp.float32) for t in range(per_box)])
    rows = wide([rows_ref[:, t, :].astype(jnp.float32) for t in range(per_box)])
    cols = wide([cols_ref[:, t, :].astype(jnp.float32) for t in range(per_box)])
    row_weight = [
        wide([row_weight_ref[t, :, a, :].astype(jnp.float32) for t in range(per_box)])
        for a in range(2)
    ]
    col_weight = [
        wide([col_weight_ref[t, :, a, :].astype(jnp.float32) for t in range(per_box)])
        for a in range(2)
    ]
    blank = jnp.zeros((1, pieces), jnp.float32)
    parts = [targets, jnp.zeros((6, pieces), jnp.float32), jnp.ones((1, pieces), jnp.float32)]
    for array in [rows, cols] + row_weight + col_weight:
        parts = parts + [array, blank]
    parts.append(jnp.zeros((8, pieces), jnp.float32))
    fields = jnp.concatenate(parts, axis=0).astype(jnp.bfloat16)
    tile = lax.broadcasted_iota(jnp.int32, (pieces, pieces), 0)
    piece = lax.broadcasted_iota(jnp.int32, (pieces, pieces), 1)
    match = targets.astype(jnp.int32) == tile
    upper = jnp.where(tile < piece, 1.0, 0.0).astype(jnp.bfloat16)
    chosen = jnp.where(match, 1.0, 0.0)
    earlier = jnp.dot(chosen.astype(jnp.bfloat16), upper, preferred_element_type=jnp.float32)
    box = (lax.broadcasted_iota(jnp.int32, (8, pieces), 1) % boxes).astype(jnp.float32)
    slots = []
    for rank in range(2):
        ranked = jnp.where(earlier == float(rank), chosen, 0.0).astype(jnp.bfloat16)
        found = lax.dot_general(
            box.astype(jnp.bfloat16),
            ranked,
            (((1,), (1,)), ((), ())),
            preferred_element_type=jnp.float32,
        )
        boxes_ref[rank : rank + 1, :] = found[:1].astype(jnp.int32)
        slots.append(
            lax.dot_general(
                ranked, fields, (((1,), (1,)), ((), ())), preferred_element_type=jnp.float32
            )
        )
    send_ref[...] = jnp.concatenate(slots, axis=1).astype(jnp.bfloat16)


def describe(tile_ids, corner_rows, corner_cols, row_weight, col_weight):
    pieces = tile_ids.size
    extent = corner_rows.shape[2]
    return pl.pallas_call(
        fields_kernel,
        name="describe",
        out_shape=(
            jax.ShapeDtypeStruct((pieces, 128), jnp.bfloat16),
            jax.ShapeDtypeStruct((2, pieces), jnp.int32),
        ),
        in_specs=[pl.BlockSpec(memory_space=VMEM)] * 5,
        out_specs=(pl.BlockSpec(memory_space=VMEM),) * 2,
        compiler_params=params(8),
        cost_estimate=pl.CostEstimate(flops=10_000_000, bytes_accessed=200_000, transcendentals=0),
    )(
        jnp.transpose(tile_ids),
        jnp.transpose(corner_rows, (2, 1, 0)),
        jnp.transpose(corner_cols, (2, 1, 0)),
        jnp.transpose(row_weight, (1, 2, 3, 0)),
        jnp.transpose(col_weight, (1, 2, 3, 0)),
    )


def arrange(slots, extent):
    count = slots.shape[0]
    groups = count * extent * 2 // GROUP + TILE
    entries = groups * GROUP
    wide = extent + 1
    rows = jnp.where(slots[:, 7:8] > 0.5, slots[:, 8 : 8 + extent], -4.0).astype(jnp.int32)
    pixel = jnp.arange(TILE, dtype=jnp.int32)
    flat = rows.reshape(-1)
    hits = (flat == pixel[:, None]).astype(jnp.int32) + (flat + 1 == pixel[:, None]).astype(jnp.int32)
    tally = jnp.sum(hits, axis=1)
    needed = (tally + GROUP - 1) // GROUP
    ends = jnp.sum(jnp.where(pixel[None, :] <= pixel[:, None], needed[None, :], 0), axis=1)
    start = (ends - needed) * GROUP
    place = jnp.sum((jnp.arange(groups)[:, None] >= ends[None, :-1]).astype(jnp.int32), axis=1)
    entry = order_entries(flat, start, ends * GROUP, entries)
    inside = jnp.arange(entries, dtype=jnp.int32) < ends[-1] * GROUP
    entry = jnp.where(inside, entry, 14)
    owner, code = entry // 16, entry % 16
    line = jnp.minimum(code // 2, extent - 1)
    base = owner // 2 * 200 + owner % 2 * 98 + extent * line
    chosen = (owner[:, None] == jnp.arange(count)).astype(jnp.bfloat16)
    values = jnp.dot(chosen, slots[:, 8:].astype(jnp.bfloat16), preferred_element_type=jnp.float32)
    which = jnp.arange(2 * wide, dtype=jnp.int32)
    wanted = (which[None, :] % wide == line[:, None]) & (which[None, :] // wide == code[:, None] % 2)
    wanted = wanted & (code[:, None] < 2 * extent)
    scale = jnp.sum(jnp.where(wanted, values[:, 2 * wide : 4 * wide], 0.0), axis=1)
    corner = values[:, wide : 2 * wide]
    low = values[:, 4 * wide : 5 * wide] * scale[:, None]
    high = values[:, 5 * wide : 6 * wide] * scale[:, None]

    def lanes(array):
        return array.reshape(groups, 1, GROUP * wide)

    corner, low, high = lanes(corner), lanes(low), lanes(high)
    position = jnp.arange(TILE, dtype=jnp.float32)[None, :, None]
    columns = jnp.where(position == corner, low, 0.0) + jnp.where(position == corner + 1.0, high, 0.0)
    return base, place, ends[-1:], columns.astype(jnp.bfloat16)


def shards(
    out_grad,
    saved,
    conv_weight,
    conv_bias,
    tile_ids,
    corner_rows,
    corner_cols,
    row_weight,
    col_weight,
):
    boxes, extent, channels = out_grad.shape[0], out_grad.shape[1], out_grad.shape[3]
    layers = saved.shape[0]
    devices = lax.axis_size("row") * lax.axis_size("col")
    grad_scale = 1.0 / math.sqrt(boxes * devices * extent * extent)
    slots, box_of_slot = describe(tile_ids, corner_rows, corner_cols, row_weight, col_weight)
    slots = lax.all_to_all(
        slots.reshape(devices, 1, -1), AXES, split_axis=0, concat_axis=0, tiled=True
    )

    grad_t = jnp.transpose(out_grad, (1, 2, 0, 3))
    saved_t = jnp.transpose(saved, (0, 2, 3, 1, 4))
    slope, crops, biases = conv_chain(grad_t, saved_t, conv_weight, conv_bias)
    terms = weight_terms(slope, saved_t)
    terms, slots = lax.optimization_barrier((terms, slots))
    sums = sum_chip(terms.reshape(layers, -1, channels // 2), devices)
    tail = biases.reshape(layers * 2, channels // 2)
    send = pack(box_of_slot.reshape(-1), crops, tail, sums, boxes)
    send, slots = lax.optimization_barrier((send, slots))
    got = lax.all_to_all(send, AXES, split_axis=0, concat_axis=0, tiled=True)

    base, place, groups, columns = arrange(slots.reshape(2 * devices, -1).astype(jnp.float32), extent)
    got, columns = lax.optimization_barrier((got, columns))
    cols = lax.axis_size("col")
    arrived = got[:, 200:, :].reshape(-1, layers, cols, SUM_ROWS, channels // 2)
    part = jnp.sum(arrived.astype(jnp.float32), axis=(0, 2)).astype(jnp.bfloat16)
    part = ring(ring(part, "col", hop_z), "col", hop_y)
    part, got = lax.optimization_barrier((part, got))
    own = ring(part, "row", hop_x)
    feature_grad, spare = tile_sum(base, place, groups, got, columns, channels)
    own, feature_grad = lax.optimization_barrier((own, feature_grad))
    other = lax.ppermute(own, "row", hop_core())
    weight_grad = widen(own, other, 9 * channels, grad_scale)
    bias_grad = (spare[4 : 4 + 2 * layers] * grad_scale).reshape(layers, channels)
    return (weight_grad, bias_grad, feature_grad)


def solution(mesh):
    in_specs = (
        P(AXES, None, None, None),
        P(None, AXES, None, None, None),
        P(),
        P(),
        P(AXES, None),
        P(AXES, None, None),
        P(AXES, None, None),
        P(AXES, None, None, None),
        P(AXES, None, None, None),
    )
    out_specs = (P(), P(), P("row", "col", None))
    return jax.shard_map(shards, mesh=mesh, in_specs=in_specs, out_specs=out_specs, check_vma=False)
```

```python
import functools
import math

import jax
import jax.numpy as jnp
from jax import lax
from jax.experimental import pallas as pl
from jax.experimental.pallas import tpu as pltpu
from jax.sharding import PartitionSpec as P

TILE = 64
SUM_ROWS = 40
GROUP = 32
UNROLL = 8
VMEM = pltpu.MemorySpace.VMEM
SMEM = pltpu.MemorySpace.SMEM
AXES = ("row", "col")


def params(megabytes):
    return pltpu.CompilerParams(vmem_limit_bytes=megabytes * 1024 * 1024)


def gelu_slope(pre_act):
    normal_cdf = 0.5 * (1.0 + lax.erf(pre_act * 0.7071067811865476))
    return normal_cdf + pre_act * jnp.exp(-0.5 * pre_act * pre_act) * 0.3989422804014327


def chain_kernel(
    grad_hbm,
    saved_hbm,
    weight_hbm,
    bias_ref,
    terms_ref,
    crops_ref,
    biases_ref,
    both,
    slopes,
    flow,
    grad_ref,
    weight_ref,
    sems,
):
    extent, boxes, channels = grad_ref.shape[0], grad_ref.shape[2], grad_ref.shape[3]
    rows = extent * boxes
    inner = pl.ds(1, extent)
    fetches = {}
    for layer in (1, 0):
        fetches[layer] = [
            pltpu.make_async_copy(
                saved_hbm.at[layer], both.at[layer, inner, inner], sems.at[2 * layer]
            ),
            pltpu.make_async_copy(
                weight_hbm.at[layer], weight_ref.at[layer], sems.at[2 * layer + 1]
            ),
        ]
    fetches[1].append(pltpu.make_async_copy(grad_hbm, grad_ref, sems.at[4]))
    for layer in (1, 0):
        for fetch in fetches[layer]:
            fetch.start()
    slopes[...] = jnp.zeros_like(slopes)
    edge = jnp.zeros((extent + 2, boxes, channels), jnp.bfloat16)
    for layer in (1, 0):
        for end in (0, extent + 1):
            both[layer, end] = edge
            both[layer, 1 : extent + 1, end] = edge[:extent]
    for layer in (1, 0):
        padded = both.at[layer]
        for fetch in fetches[layer]:
            fetch.wait()

        def forward(i, sums, layer=layer, padded=padded):
            pieces = [
                padded[i + a, b : b + extent].reshape(rows, channels)
                for a in range(3)
                for b in range(3)
            ]
            pre = jnp.dot(
                jnp.concatenate(pieces, axis=1),
                weight_ref[layer].reshape(9 * channels, channels),
                preferred_element_type=jnp.float32,
            )
            pre = pre + bias_ref[layer : layer + 1, :]
            upper = grad_ref[i] if layer == 1 else flow[i]
            upper = upper.reshape(rows, channels).astype(jnp.float32)
            slope = (upper * gelu_slope(pre)).astype(jnp.bfloat16)
            slopes[i + 1, 1 : extent + 1] = slope.reshape(extent, boxes, channels)
            return sums + jnp.sum(
                slope.astype(jnp.float32).reshape(rows // 8, 8, channels), axis=0
            )

        sums = jnp.zeros((8, channels), jnp.float32)
        for i in range(extent):
            sums = forward(i, sums)
        biases_ref[layer : layer + 1, :] = jnp.sum(sums, axis=0, keepdims=True)

        whole = slopes[1 : extent + 1, 1 : extent + 1].reshape(extent * rows, channels)
        for k in range(9):
            piece = padded[pl.ds(k // 3, extent), pl.ds(k % 3, extent)]
            term = lax.dot_general(
                piece.reshape(extent * rows, channels),
                whole,
                (((0,), (0,)), ((), ())),
                preferred_element_type=jnp.float32,
            ).astype(jnp.bfloat16)
            for half in range(2):
                terms_ref[layer, (9 * half + k) * channels : (9 * half + k + 1) * channels, :] = (
                    term[:, half * channels // 2 : (half + 1) * channels // 2]
                )
        last = 18 * channels
        terms_ref[layer, last:, :] = jnp.zeros(
            (terms_ref.shape[1] - last, channels // 2), jnp.bfloat16
        )

        def backward(i, carry, layer=layer):
            total = jnp.zeros((rows, channels), jnp.float32)
            for a in range(3):
                for b in range(3):
                    piece = slopes[i + 2 - a, 2 - b : 2 - b + extent].reshape(rows, channels)
                    total = total + lax.dot_general(
                        piece,
                        weight_ref[layer, 3 * a + b],
                        (((1,), (1,)), ((), ())),
                        preferred_element_type=jnp.float32,
                    )
            if layer == 1:
                flow[i] = total.astype(jnp.bfloat16).reshape(extent, boxes, channels)
            else:
                place = pl.ds(i * rows, rows)
                crops_ref[0, place, :] = total[:, : channels // 2]
                crops_ref[1, place, :] = total[:, channels // 2 :]
            return carry

        for i in range(extent):
            backward(i, 0)


def conv_chain(grad_t, saved_t, weight, bias, lines):
    extent, boxes, channels = grad_t.shape[0], grad_t.shape[2], grad_t.shape[3]
    layers = saved_t.shape[0]
    padded = (extent + 2, extent + 2, boxes, channels)
    return pl.pallas_call(
        chain_kernel,
        name="conv_chain",
        out_shape=(
            jax.ShapeDtypeStruct((layers, lines, channels // 2), jnp.bfloat16),
            jax.ShapeDtypeStruct((2, extent * extent * boxes, channels // 2), jnp.float32),
            jax.ShapeDtypeStruct((layers, channels), jnp.float32),
        ),
        in_specs=[pl.BlockSpec(memory_space=pl.ANY)] * 3 + [pl.BlockSpec(memory_space=VMEM)],
        out_specs=(pl.BlockSpec(memory_space=VMEM),) * 3,
        scratch_shapes=[
            pltpu.VMEM((layers,) + padded, jnp.bfloat16),
            pltpu.VMEM(padded, jnp.bfloat16),
            pltpu.VMEM((extent, extent, boxes, channels), jnp.bfloat16),
            pltpu.VMEM(grad_t.shape, jnp.bfloat16),
            pltpu.VMEM(weight.shape, jnp.bfloat16),
            pltpu.SemaphoreType.DMA((5,)),
        ],
        compiler_params=params(56),
        cost_estimate=pl.CostEstimate(flops=22000000000, bytes_accessed=9000000, transcendentals=0),
    )(grad_t, saved_t, weight, bias)


def pack_kernel(
    box_ref,
    core_ref,
    crops_ref,
    tail_ref,
    own_ref,
    other_ref,
    out_hbm,
    first,
    second,
    staged,
    sums,
    out_ref,
    sems,
):
    del core_ref
    steps = sems.shape[0]
    owners = out_ref.shape[0]
    count = owners // steps
    lines = count * SUM_ROWS
    boxes = first.shape[0]
    bins = crops_ref.shape[1] // boxes
    staged[...] = jnp.zeros_like(staged)
    for box in range(boxes):
        for half in range(2):
            rows = crops_ref[half, pl.ds(box, bins, stride=boxes), :]
            staged[0, box, half * bins : (half + 1) * bins, :] = rows
            staged[1, box, half * bins + 2 : (half + 1) * bins + 2, :] = rows
        staged[1, box, 2 * bins + 2 : 2 * bins + 6, :] = tail_ref[...]
        first[box] = staged[0, box].astype(jnp.bfloat16)
        second[box] = staged[1, box].astype(jnp.bfloat16)
    blank = jnp.zeros((8, sums.shape[1]), jnp.float32)

    def both(left, right):
        return (left.astype(jnp.float32) + right.astype(jnp.float32)).astype(jnp.bfloat16)

    sends = []
    for step in range(steps):
        block = slice(step * lines, (step + 1) * lines)
        sums[...] = own_ref[0, block, :].astype(jnp.float32) + other_ref[block, :].astype(jnp.float32)

        def place(index, carry, step=step):
            owner = step * count + index
            one, two = first[box_ref[owner]], second[box_ref[owners + owner]]
            chunk = sums[pl.ds(pl.multiple_of(index * SUM_ROWS, 8), SUM_ROWS), :]
            chunk = jnp.concatenate([blank, chunk], axis=0).astype(jnp.bfloat16)
            out_ref[owner] = jnp.concatenate(
                [
                    one[:96],
                    both(one[96:112], two[:16]),
                    two[16:96],
                    both(two[96:112], chunk[:16]),
                    chunk[16:],
                ],
                axis=0,
            )
            return carry

        lax.fori_loop(0, count, place, 0, unroll=4)
        part = pl.ds(step * count, count)
        send = pltpu.make_async_copy(out_ref.at[part], out_hbm.at[part], sems.at[step])
        send.start()
        sends.append(send)
    for send in sends:
        send.wait()


def pack(box_of_slot, core, crops, tail, own, other, boxes):
    owners = box_of_slot.shape[0] // 2
    steps = 16
    half = crops.shape[2]
    rows = 200 + SUM_ROWS
    return pl.pallas_call(
        pack_kernel,
        name="pack",
        out_shape=jax.ShapeDtypeStruct((owners, rows, half), jnp.bfloat16),
        grid_spec=pltpu.PrefetchScalarGridSpec(
            num_scalar_prefetch=2,
            grid=(1,),
            in_specs=[
                pl.BlockSpec(crops.shape, lambda g, ids, core: (0, 0, 0)),
                pl.BlockSpec(tail.shape, lambda g, ids, core: (0, 0)),
                pl.BlockSpec((1,) + other.shape, lambda g, ids, core: (core[0], 0, 0)),
                pl.BlockSpec(other.shape, lambda g, ids, core: (0, 0)),
            ],
            out_specs=pl.BlockSpec(memory_space=pl.ANY),
            scratch_shapes=[
                pltpu.VMEM((boxes, 112, half), jnp.bfloat16),
                pltpu.VMEM((boxes, 112, half), jnp.bfloat16),
                pltpu.VMEM((2, boxes, 112, half), jnp.float32),
                pltpu.VMEM((owners // steps * SUM_ROWS, half), jnp.float32),
                pltpu.VMEM((owners, rows, half), jnp.bfloat16),
                pltpu.SemaphoreType.DMA((steps,)),
            ],
        ),
        compiler_params=params(56),
        cost_estimate=pl.CostEstimate(flops=1_000_000, bytes_accessed=9_000_000, transcendentals=0),
    )(box_of_slot, core.reshape(1), crops, tail, own, other)


def hop_core():
    return [(r, r ^ 1) for r in range(8)]


def hop_x(k):
    return [(r, (r // 2 + k) % 4 * 2 + r % 2) for r in range(8)]


def hop_y(k):
    return [(c, c // 4 * 4 + (c % 4 + k) % 4) for c in range(16)]


def hop_z(k):
    return [(c, (c // 4 + k) % 4 * 4 + c % 4) for c in range(16)]


def pick(array, index):
    return lax.dynamic_index_in_dim(array, index, 0, keepdims=False)


def ring(part, name, hop):
    return jnp.stack([part] + [lax.ppermute(part, name, hop(k)) for k in (3, 2, 1)])


def widen_kernel(place_ref, own_ref, other_ref, out_ref, *, scale):
    length, half = out_ref.shape[1], out_ref.shape[2] // 2
    turns = [[lax.rem(q + 4 - place_ref[axis], 4) for q in range(4)] for axis in range(3)]

    def copy(core, source_ref):
        for x in range(4):
            for z in range(4):
                for y in range(4):
                    start = (((x * 2 + core) * 4 + z) * 4 + y) * SUM_ROWS
                    values = source_ref[turns[0][x], turns[1][y], turns[2][z]].astype(jnp.float32)
                    values = values * scale
                    for column in range(2):
                        low = max(start, column * length)
                        high = min(start + SUM_ROWS, (column + 1) * length)
                        if low < high:
                            out_ref[
                                :,
                                low - column * length : high - column * length,
                                column * half : (column + 1) * half,
                            ] = values[:, low - start : high - start, :]

    for core in range(2):

        @pl.when(place_ref[3] == core)
        def _(core=core):
            copy(core, own_ref)
            copy(1 - core, other_ref)


def widen(own, other, length, scale):
    row, col = lax.axis_index("row"), lax.axis_index("col")
    place = jnp.stack([row // 2, col % 4, col // 4, row % 2]).astype(jnp.int32)
    layers, half = own.shape[3], own.shape[5]
    return pl.pallas_call(
        functools.partial(widen_kernel, scale=scale),
        name="widen",
        out_shape=jax.ShapeDtypeStruct((layers, length, 2 * half), jnp.float32),
        in_specs=[
            pl.BlockSpec(memory_space=SMEM),
            pl.BlockSpec(memory_space=VMEM),
            pl.BlockSpec(memory_space=VMEM),
        ],
        out_specs=pl.BlockSpec(memory_space=VMEM),
        compiler_params=params(24),
        cost_estimate=pl.CostEstimate(flops=3_000_000, bytes_accessed=10_000_000, transcendentals=0),
    )(place, own, other)


def order_kernel(rows_ref, start_ref, end_ref, entry_ref, count):
    places = start_ref.shape[0]
    extent = 7
    slots = rows_ref.shape[0] // extent

    def begin(p, carry):
        count[p] = start_ref[p]
        return carry

    lax.fori_loop(0, places, begin, 0)

    def enter(slot, carry):
        @pl.when(rows_ref[slot * extent] >= 0)
        def _():
            for i in range(extent):
                first = rows_ref[slot * extent + i]
                for a in range(2):
                    n = count[first + a]
                    count[first + a] = n + 1
                    entry_ref[n] = slot * 16 + 2 * i + a

        return carry

    lax.fori_loop(0, slots, enter, 0)

    def fill(p, carry):
        def blank(n, inner):
            entry_ref[n] = 14
            return inner

        return lax.fori_loop(count[p], end_ref[p], blank, carry)

    lax.fori_loop(0, places, fill, 0)


def order_entries(rows, start, end, entries):
    return pl.pallas_call(
        order_kernel,
        name="order_entries",
        out_shape=jax.ShapeDtypeStruct((entries,), jnp.int32),
        in_specs=[pl.BlockSpec(memory_space=SMEM)] * 3,
        out_specs=pl.BlockSpec(memory_space=SMEM),
        scratch_shapes=[pltpu.SMEM((TILE,), jnp.int32)],
        cost_estimate=pl.CostEstimate(flops=10_000_000, bytes_accessed=30_000_000, transcendentals=0),
    )(rows, start, end)


def tile_kernel(
    base_ref, place_ref, groups_ref, got_ref, columns_hbm, out_ref, biases_ref, crops, columns_ref, sem
):
    step = pl.program_id(0)
    owners, half = got_ref.shape[0], got_ref.shape[2]
    bins = 49
    block = owners * 200
    fetch = pltpu.make_async_copy(columns_hbm, columns_ref, sem)

    @pl.when(step == 0)
    def _():
        fetch.start()

    wide = got_ref[...].astype(jnp.float32)[:, :200, :]
    crops[pl.ds(pl.multiple_of(step * block, 8), block), :] = wide.reshape(block, half)
    spare = jnp.sum(wide[:, 192:, :], axis=0)

    @pl.when(step == 0)
    def _():
        biases_ref[...] = spare

    @pl.when(step > 0)
    def _():
        biases_ref[...] += spare

    @pl.when(step == pl.num_programs(0) - 1)
    def _():
        out_ref[...] = jnp.zeros_like(out_ref)
        fetch.wait()

        def group(t):
            left, right = [], []
            for n in range(GROUP):
                base = base_ref[t * GROUP + n]
                left.append(crops[pl.ds(base, 8), :])
                right.append(crops[pl.ds(base + bins, 8), :])
            values = jnp.concatenate(
                [jnp.concatenate(left, axis=0), jnp.concatenate(right, axis=0)], axis=1
            ).astype(jnp.bfloat16)
            return jnp.dot(columns_ref[t], values, preferred_element_type=jnp.float32)

        def several(t, carry):
            terms = [group(t * UNROLL + u) for u in range(UNROLL)]
            for u in range(UNROLL):
                out_ref[place_ref[t * UNROLL + u]] += terms[u]
            return carry

        lax.fori_loop(0, (groups_ref[0] + UNROLL - 1) // UNROLL, several, 0)


def tile_sum(base, place, groups, got, columns, channels):
    steps = 8
    owners, rows, half = got.shape
    return pl.pallas_call(
        tile_kernel,
        name="tile_sum",
        out_shape=(
            jax.ShapeDtypeStruct((TILE, TILE, channels), jnp.float32),
            jax.ShapeDtypeStruct((8, half), jnp.float32),
        ),
        grid_spec=pltpu.PrefetchScalarGridSpec(
            num_scalar_prefetch=3,
            grid=(steps,),
            in_specs=[
                pl.BlockSpec((owners // steps, rows, half), lambda g, *refs: (g, 0, 0)),
                pl.BlockSpec(memory_space=pl.ANY),
            ],
            out_specs=(
                pl.BlockSpec((TILE, TILE, channels), lambda g, *refs: (0, 0, 0)),
                pl.BlockSpec((8, half), lambda g, *refs: (0, 0)),
            ),
            scratch_shapes=[
                pltpu.VMEM((owners * 200, half), jnp.float32),
                pltpu.VMEM(columns.shape, jnp.bfloat16),
                pltpu.SemaphoreType.DMA(()),
            ],
        ),
        compiler_params=params(58),
        cost_estimate=pl.CostEstimate(
            flops=2 * columns.size * channels, bytes_accessed=17_000_000, transcendentals=0
        ),
    )(base, place, groups, got, columns)


def fields_kernel(tiles_ref, rows_ref, cols_ref, row_weight_ref, col_weight_ref, send_ref, boxes_ref):
    per_box, boxes = tiles_ref.shape
    extent = rows_ref.shape[0]
    pieces = per_box * boxes

    def wide(parts):
        return jnp.concatenate(parts, axis=1)

    targets = wide([tiles_ref[t : t + 1, :].astype(jnp.float32) for t in range(per_box)])
    rows = wide([rows_ref[:, t, :].astype(jnp.float32) for t in range(per_box)])
    cols = wide([cols_ref[:, t, :].astype(jnp.float32) for t in range(per_box)])
    row_weight = [
        wide([row_weight_ref[t, :, a, :].astype(jnp.float32) for t in range(per_box)])
        for a in range(2)
    ]
    col_weight = [
        wide([col_weight_ref[t, :, a, :].astype(jnp.float32) for t in range(per_box)])
        for a in range(2)
    ]
    blank = jnp.zeros((1, pieces), jnp.float32)
    parts = [targets, jnp.zeros((6, pieces), jnp.float32), jnp.ones((1, pieces), jnp.float32)]
    for array in [rows, cols] + row_weight + col_weight:
        parts = parts + [array, blank]
    parts.append(jnp.zeros((8, pieces), jnp.float32))
    fields = jnp.concatenate(parts, axis=0).astype(jnp.bfloat16)
    tile = lax.broadcasted_iota(jnp.int32, (pieces, pieces), 0)
    piece = lax.broadcasted_iota(jnp.int32, (pieces, pieces), 1)
    match = targets.astype(jnp.int32) == tile
    upper = jnp.where(tile < piece, 1.0, 0.0).astype(jnp.bfloat16)
    chosen = jnp.where(match, 1.0, 0.0)
    earlier = jnp.dot(chosen.astype(jnp.bfloat16), upper, preferred_element_type=jnp.float32)
    box = (lax.broadcasted_iota(jnp.int32, (8, pieces), 1) % boxes).astype(jnp.float32)
    slots = []
    for rank in range(2):
        ranked = jnp.where(earlier == float(rank), chosen, 0.0).astype(jnp.bfloat16)
        found = lax.dot_general(
            box.astype(jnp.bfloat16),
            ranked,
            (((1,), (1,)), ((), ())),
            preferred_element_type=jnp.float32,
        )
        boxes_ref[rank : rank + 1, :] = found[:1].astype(jnp.int32)
        slots.append(
            lax.dot_general(
                ranked, fields, (((1,), (1,)), ((), ())), preferred_element_type=jnp.float32
            )
        )
    send_ref[...] = jnp.concatenate(slots, axis=1).astype(jnp.bfloat16)


def describe(tile_ids, corner_rows, corner_cols, row_weight, col_weight):
    pieces = tile_ids.size
    arrays = (
        jnp.transpose(tile_ids),
        jnp.transpose(corner_rows, (2, 1, 0)),
        jnp.transpose(corner_cols, (2, 1, 0)),
        jnp.transpose(row_weight, (1, 2, 3, 0)),
        jnp.transpose(col_weight, (1, 2, 3, 0)),
    )
    return pl.pallas_call(
        fields_kernel,
        name="describe",
        out_shape=(
            jax.ShapeDtypeStruct((pieces, 128), jnp.bfloat16),
            jax.ShapeDtypeStruct((2, pieces), jnp.int32),
        ),
        grid=(1,),
        in_specs=[pl.BlockSpec(array.shape, lambda g, n=array.ndim: (0,) * n) for array in arrays],
        out_specs=(
            pl.BlockSpec((pieces, 128), lambda g: (0, 0)),
            pl.BlockSpec((2, pieces), lambda g: (0, 0)),
        ),
        compiler_params=params(58),
        cost_estimate=pl.CostEstimate(flops=10_000_000, bytes_accessed=200_000, transcendentals=0),
    )(*arrays)


def arrange(slots, extent):
    count = slots.shape[0]
    groups = count * extent * 2 // GROUP + TILE
    entries = groups * GROUP
    wide = extent + 1
    rows = jnp.where(slots[:, 7:8] > 0.5, slots[:, 8 : 8 + extent], -4.0).astype(jnp.int32)
    pixel = jnp.arange(TILE, dtype=jnp.int32)
    flat = rows.reshape(-1)
    hits = (flat == pixel[:, None]).astype(jnp.int32) + (flat + 1 == pixel[:, None]).astype(jnp.int32)
    tally = jnp.sum(hits, axis=1)
    needed = (tally + GROUP - 1) // GROUP
    ends = jnp.sum(jnp.where(pixel[None, :] <= pixel[:, None], needed[None, :], 0), axis=1)
    start = (ends - needed) * GROUP
    place = jnp.sum((jnp.arange(groups)[:, None] >= ends[None, :-1]).astype(jnp.int32), axis=1)
    entry = order_entries(flat, start, ends * GROUP, entries)
    inside = jnp.arange(entries, dtype=jnp.int32) < ends[-1] * GROUP
    entry = jnp.where(inside, entry, 14)
    owner, code = entry // 16, entry % 16
    line = jnp.minimum(code // 2, extent - 1)
    base = owner // 2 * 200 + owner % 2 * 98 + extent * line
    chosen = (owner[:, None] == jnp.arange(count)).astype(jnp.bfloat16)
    values = jnp.dot(chosen, slots[:, 8:].astype(jnp.bfloat16), preferred_element_type=jnp.float32)
    which = jnp.arange(2 * wide, dtype=jnp.int32)
    wanted = (which[None, :] % wide == line[:, None]) & (which[None, :] // wide == code[:, None] % 2)
    wanted = wanted & (code[:, None] < 2 * extent)
    scale = jnp.sum(jnp.where(wanted, values[:, 2 * wide : 4 * wide], 0.0), axis=1)
    corner = values[:, wide : 2 * wide]
    low = values[:, 4 * wide : 5 * wide] * scale[:, None]
    high = values[:, 5 * wide : 6 * wide] * scale[:, None]

    def lanes(array):
        return array.reshape(groups, 1, GROUP * wide)

    corner, low, high = lanes(corner), lanes(low), lanes(high)
    position = jnp.arange(TILE, dtype=jnp.float32)[None, :, None]
    columns = jnp.where(position == corner, low, 0.0) + jnp.where(position == corner + 1.0, high, 0.0)
    return base, place, ends[-1:], columns.astype(jnp.bfloat16)


def shards(
    out_grad,
    saved,
    conv_weight,
    conv_bias,
    tile_ids,
    corner_rows,
    corner_cols,
    row_weight,
    col_weight,
):
    boxes, extent, channels = out_grad.shape[0], out_grad.shape[1], out_grad.shape[3]
    layers = saved.shape[0]
    devices = lax.axis_size("row") * lax.axis_size("col")
    grad_scale = 1.0 / math.sqrt(boxes * devices * extent * extent)
    slots, box_of_slot = describe(tile_ids, corner_rows, corner_cols, row_weight, col_weight)
    slots = lax.all_to_all(
        slots.reshape(devices, 1, -1), AXES, split_axis=0, concat_axis=0, tiled=True
    )

    grad_t = jnp.transpose(out_grad, (1, 2, 0, 3))
    saved_t = jnp.transpose(saved, (0, 2, 3, 1, 4))
    lines = devices * SUM_ROWS
    terms, crops, biases = conv_chain(grad_t, saved_t, conv_weight, conv_bias, lines)
    terms, slots = lax.optimization_barrier((terms, slots))
    core = lax.axis_index("row") % 2
    other = lax.ppermute(pick(terms, 1 - core), "row", hop_core())
    tail = biases.reshape(layers * 2, channels // 2)
    send = pack(box_of_slot.reshape(-1), core, crops, tail, terms, other, boxes)
    send, slots = lax.optimization_barrier((send, slots))
    got = lax.all_to_all(send, AXES, split_axis=0, concat_axis=0, tiled=True)

    base, place, groups, columns = arrange(slots.reshape(2 * devices, -1).astype(jnp.float32), extent)
    got, columns = lax.optimization_barrier((got, columns))
    cols = lax.axis_size("col")
    arrived = got[:, 200:, :].reshape(-1, layers, cols, SUM_ROWS, channels // 2)
    part = jnp.sum(arrived.astype(jnp.float32), axis=(0, 2)).astype(jnp.bfloat16)
    part = ring(ring(part, "col", hop_z), "col", hop_y)
    part, got = lax.optimization_barrier((part, got))
    own = ring(part, "row", hop_x)
    feature_grad, spare = tile_sum(base, place, groups, got, columns, channels)
    own, feature_grad = lax.optimization_barrier((own, feature_grad))
    other = lax.ppermute(own, "row", hop_core())
    weight_grad = widen(own, other, 9 * channels, grad_scale)
    bias_grad = (spare[4 : 4 + 2 * layers] * grad_scale).reshape(layers, channels)
    return (weight_grad, bias_grad, feature_grad)


def solution(mesh):
    in_specs = (
        P(AXES, None, None, None),
        P(None, AXES, None, None, None),
        P(),
        P(),
        P(AXES, None),
        P(AXES, None, None),
        P(AXES, None, None),
        P(AXES, None, None, None),
        P(AXES, None, None, None),
    )
    out_specs = (P(), P(), P("row", "col", None))
    return jax.shard_map(shards, mesh=mesh, in_specs=in_specs, out_specs=out_specs, check_vma=False)
```

```python
import functools
import math

import jax
import jax.numpy as jnp
from jax import lax
from jax.experimental import pallas as pl
from jax.experimental.pallas import tpu as pltpu
from jax.sharding import PartitionSpec as P

TILE = 64
SUM_ROWS = 40
GROUP = 32
UNROLL = 16
VMEM = pltpu.MemorySpace.VMEM
SMEM = pltpu.MemorySpace.SMEM
AXES = ("row", "col")


def params(megabytes):
    return pltpu.CompilerParams(vmem_limit_bytes=megabytes * 1024 * 1024)


def gelu_slope(pre_act):
    normal_cdf = 0.5 * (1.0 + lax.erf(pre_act * 0.7071067811865476))
    return normal_cdf + pre_act * jnp.exp(-0.5 * pre_act * pre_act) * 0.3989422804014327


def chain_kernel(
    grad_hbm,
    saved_hbm,
    weight_hbm,
    bias_ref,
    core_ref,
    own_hbm,
    give_hbm,
    crops_hbm,
    biases_ref,
    terms_ref,
    crops_ref,
    both,
    slopes,
    flow,
    grad_ref,
    weight_ref,
    sems,
    term_sems,
    crop_sems,
):
    extent, boxes, channels = grad_ref.shape[0], grad_ref.shape[2], grad_ref.shape[3]
    rows = extent * boxes
    inner = pl.ds(1, extent)
    fetches = {}
    for layer in (1, 0):
        fetches[layer] = [
            pltpu.make_async_copy(
                saved_hbm.at[layer], both.at[layer, inner, inner], sems.at[2 * layer]
            ),
            pltpu.make_async_copy(
                weight_hbm.at[layer], weight_ref.at[layer], sems.at[2 * layer + 1]
            ),
        ]
    fetches[1].append(pltpu.make_async_copy(grad_hbm, grad_ref, sems.at[4]))
    for layer in (1, 0):
        for fetch in fetches[layer]:
            fetch.start()

    def crop_copy(i):
        part = pl.ds(i * rows, rows)
        return pltpu.make_async_copy(
            crops_ref.at[:, part, :], crops_hbm.at[:, part, :], crop_sems.at[i]
        )

    slopes[...] = jnp.zeros_like(slopes)
    edge = jnp.zeros((extent + 2, boxes, channels), jnp.bfloat16)
    for layer in (1, 0):
        for end in (0, extent + 1):
            both[layer, end] = edge
            both[layer, 1 : extent + 1, end] = edge[:extent]
    for layer in (1, 0):
        padded = both.at[layer]
        for fetch in fetches[layer]:
            fetch.wait()

        def forward(i, sums, layer=layer, padded=padded):
            pieces = [
                padded[i + a, b : b + extent].reshape(rows, channels)
                for a in range(3)
                for b in range(3)
            ]
            pre = jnp.dot(
                jnp.concatenate(pieces, axis=1),
                weight_ref[layer].reshape(9 * channels, channels),
                preferred_element_type=jnp.float32,
            )
            pre = pre + bias_ref[layer : layer + 1, :]
            upper = grad_ref[i] if layer == 1 else flow[i]
            upper = upper.reshape(rows, channels).astype(jnp.float32)
            slope = (upper * gelu_slope(pre)).astype(jnp.bfloat16)
            slopes[i + 1, 1 : extent + 1] = slope.reshape(extent, boxes, channels)
            return sums + jnp.sum(
                slope.astype(jnp.float32).reshape(rows // 8, 8, channels), axis=0
            )

        sums = jnp.zeros((8, channels), jnp.float32)
        for i in range(extent):
            sums = forward(i, sums)
        biases_ref[layer : layer + 1, :] = jnp.sum(sums, axis=0, keepdims=True)

        def emit(target_hbm, layer=layer):
            return pltpu.make_async_copy(terms_ref.at[layer], target_hbm, term_sems.at[layer])

        whole = slopes[1 : extent + 1, 1 : extent + 1].reshape(extent * rows, channels)
        for k in range(9):
            piece = padded[pl.ds(k // 3, extent), pl.ds(k % 3, extent)]
            term = lax.dot_general(
                piece.reshape(extent * rows, channels),
                whole,
                (((0,), (0,)), ((), ())),
                preferred_element_type=jnp.float32,
            ).astype(jnp.bfloat16)
            for half in range(2):
                terms_ref[layer, (9 * half + k) * channels : (9 * half + k + 1) * channels, :] = (
                    term[:, half * channels // 2 : (half + 1) * channels // 2]
                )
        last = 18 * channels
        terms_ref[layer, last:, :] = jnp.zeros(
            (terms_ref.shape[1] - last, channels // 2), jnp.bfloat16
        )

        @pl.when(core_ref[0] == layer)
        def _(emit=emit):
            emit(own_hbm).start()

        @pl.when(core_ref[0] != layer)
        def _(emit=emit):
            emit(give_hbm).start()

        def backward(i, carry, layer=layer):
            total = jnp.zeros((rows, channels), jnp.float32)
            for a in range(3):
                for b in range(3):
                    piece = slopes[i + 2 - a, 2 - b : 2 - b + extent].reshape(rows, channels)
                    total = total + lax.dot_general(
                        piece,
                        weight_ref[layer, 3 * a + b],
                        (((1,), (1,)), ((), ())),
                        preferred_element_type=jnp.float32,
                    )
            if layer == 1:
                flow[i] = total.astype(jnp.bfloat16).reshape(extent, boxes, channels)
            else:
                place = pl.ds(i * rows, rows)
                crops_ref[0, place, :] = total[:, : channels // 2]
                crops_ref[1, place, :] = total[:, channels // 2 :]
                crop_copy(i).start()
            return carry

        for i in range(extent):
            backward(i, 0)
    for layer in (1, 0):
        pltpu.make_async_copy(terms_ref.at[layer], own_hbm, term_sems.at[layer]).wait()
    for i in range(extent):
        crop_copy(i).wait()


def conv_chain(grad_t, saved_t, weight, bias, core, lines):
    extent, boxes, channels = grad_t.shape[0], grad_t.shape[2], grad_t.shape[3]
    layers = saved_t.shape[0]
    padded = (extent + 2, extent + 2, boxes, channels)
    return pl.pallas_call(
        chain_kernel,
        name="conv_chain",
        out_shape=(
            jax.ShapeDtypeStruct((lines, channels // 2), jnp.bfloat16),
            jax.ShapeDtypeStruct((lines, channels // 2), jnp.bfloat16),
            jax.ShapeDtypeStruct((2, extent * extent * boxes, channels // 2), jnp.float32),
            jax.ShapeDtypeStruct((layers, channels), jnp.float32),
        ),
        in_specs=[pl.BlockSpec(memory_space=pl.ANY)] * 3
        + [pl.BlockSpec(memory_space=VMEM), pl.BlockSpec(memory_space=SMEM)],
        out_specs=(pl.BlockSpec(memory_space=pl.ANY),) * 3 + (pl.BlockSpec(memory_space=VMEM),),
        scratch_shapes=[
            pltpu.VMEM((layers, lines, channels // 2), jnp.bfloat16),
            pltpu.VMEM((2, extent * extent * boxes, channels // 2), jnp.float32),
            pltpu.VMEM((layers,) + padded, jnp.bfloat16),
            pltpu.VMEM(padded, jnp.bfloat16),
            pltpu.VMEM((extent, extent, boxes, channels), jnp.bfloat16),
            pltpu.VMEM(grad_t.shape, jnp.bfloat16),
            pltpu.VMEM(weight.shape, jnp.bfloat16),
            pltpu.SemaphoreType.DMA((5,)),
            pltpu.SemaphoreType.DMA((layers,)),
            pltpu.SemaphoreType.DMA((extent,)),
        ],
        compiler_params=params(56),
        cost_estimate=pl.CostEstimate(flops=22000000000, bytes_accessed=9000000, transcendentals=0),
    )(grad_t, saved_t, weight, bias, core.reshape(1))


def pack_kernel(
    box_ref,
    crops_ref,
    tail_ref,
    own_ref,
    other_ref,
    out_hbm,
    first,
    second,
    staged,
    sums,
    out_ref,
    sems,
):
    steps = sems.shape[0]
    owners = out_ref.shape[0]
    count = owners // steps
    lines = count * SUM_ROWS
    boxes = first.shape[0]
    bins = crops_ref.shape[1] // boxes
    staged[...] = jnp.zeros_like(staged)
    for box in range(boxes):
        for half in range(2):
            rows = crops_ref[half, pl.ds(box, bins, stride=boxes), :]
            staged[0, box, half * bins : (half + 1) * bins, :] = rows
            staged[1, box, half * bins + 2 : (half + 1) * bins + 2, :] = rows
        staged[1, box, 2 * bins + 2 : 2 * bins + 6, :] = tail_ref[...]
        first[box] = staged[0, box].astype(jnp.bfloat16)
        second[box] = staged[1, box].astype(jnp.bfloat16)
    blank = jnp.zeros((8, sums.shape[1]), jnp.float32)

    def both(left, right):
        return (left.astype(jnp.float32) + right.astype(jnp.float32)).astype(jnp.bfloat16)

    sends = []
    for step in range(steps):
        block = slice(step * lines, (step + 1) * lines)
        sums[...] = own_ref[block, :].astype(jnp.float32) + other_ref[block, :].astype(jnp.float32)

        def place(index, carry, step=step):
            owner = step * count + index
            one, two = first[box_ref[owner]], second[box_ref[owners + owner]]
            chunk = sums[pl.ds(pl.multiple_of(index * SUM_ROWS, 8), SUM_ROWS), :]
            chunk = jnp.concatenate([blank, chunk], axis=0).astype(jnp.bfloat16)
            out_ref[owner] = jnp.concatenate(
                [
                    one[:96],
                    both(one[96:112], two[:16]),
                    two[16:96],
                    both(two[96:112], chunk[:16]),
                    chunk[16:],
                ],
                axis=0,
            )
            return carry

        lax.fori_loop(0, count, place, 0, unroll=4)
        part = pl.ds(step * count, count)
        send = pltpu.make_async_copy(out_ref.at[part], out_hbm.at[part], sems.at[step])
        send.start()
        sends.append(send)
    for send in sends:
        send.wait()


def pack(box_of_slot, crops, tail, own, other, boxes):
    owners = box_of_slot.shape[0] // 2
    steps = 16
    half = crops.shape[2]
    rows = 200 + SUM_ROWS
    return pl.pallas_call(
        pack_kernel,
        name="pack",
        out_shape=jax.ShapeDtypeStruct((owners, rows, half), jnp.bfloat16),
        grid_spec=pltpu.PrefetchScalarGridSpec(
            num_scalar_prefetch=1,
            grid=(1,),
            in_specs=[
                pl.BlockSpec(crops.shape, lambda g, ids: (0, 0, 0)),
                pl.BlockSpec(tail.shape, lambda g, ids: (0, 0)),
                pl.BlockSpec(own.shape, lambda g, ids: (0, 0)),
                pl.BlockSpec(other.shape, lambda g, ids: (0, 0)),
            ],
            out_specs=pl.BlockSpec(memory_space=pl.ANY),
            scratch_shapes=[
                pltpu.VMEM((boxes, 112, half), jnp.bfloat16),
                pltpu.VMEM((boxes, 112, half), jnp.bfloat16),
                pltpu.VMEM((2, boxes, 112, half), jnp.float32),
                pltpu.VMEM((owners // steps * SUM_ROWS, half), jnp.float32),
                pltpu.VMEM((owners, rows, half), jnp.bfloat16),
                pltpu.SemaphoreType.DMA((steps,)),
            ],
        ),
        compiler_params=params(56),
        cost_estimate=pl.CostEstimate(flops=1_000_000, bytes_accessed=9_000_000, transcendentals=0),
    )(box_of_slot, crops, tail, own, other)


def hop_core():
    return [(r, r ^ 1) for r in range(8)]


def hop_x(k):
    return [(r, (r // 2 + k) % 4 * 2 + r % 2) for r in range(8)]


def hop_y(k):
    return [(c, c // 4 * 4 + (c % 4 + k) % 4) for c in range(16)]


def hop_z(k):
    return [(c, (c // 4 + k) % 4 * 4 + c % 4) for c in range(16)]


def ring(part, name, hop):
    return jnp.stack([part] + [lax.ppermute(part, name, hop(k)) for k in (3, 2, 1)])


def widen_kernel(place_ref, own_ref, other_ref, out_hbm, out_ref, sems, *, scale):
    length, half = out_ref.shape[1], out_ref.shape[2] // 2
    turns = [[lax.rem(q + 4 - place_ref[axis], 4) for q in range(4)] for axis in range(3)]

    def copy(core, source_ref):
        for x in range(4):
            for z in range(4):
                for y in range(4):
                    start = (((x * 2 + core) * 4 + z) * 4 + y) * SUM_ROWS
                    values = source_ref[turns[0][x], turns[1][y], turns[2][z]].astype(jnp.float32)
                    values = values * scale
                    for column in range(2):
                        low = max(start, column * length)
                        high = min(start + SUM_ROWS, (column + 1) * length)
                        if low < high:
                            out_ref[
                                :,
                                low - column * length : high - column * length,
                                column * half : (column + 1) * half,
                            ] = values[:, low - start : high - start, :]

    for core in range(2):

        @pl.when(place_ref[3] == core)
        def _(core=core):
            copy(core, own_ref)
            copy(1 - core, other_ref)

    parts = sems.shape[0]
    rows = length // parts
    sends = []
    for step in range(parts):
        part = pl.ds(step * rows, rows)
        sends.append(
            pltpu.make_async_copy(out_ref.at[:, part, :], out_hbm.at[:, part, :], sems.at[step])
        )
    for send in sends:
        send.start()
    for send in sends:
        send.wait()


def widen(own, other, length, scale):
    row, col = lax.axis_index("row"), lax.axis_index("col")
    place = jnp.stack([row // 2, col % 4, col // 4, row % 2]).astype(jnp.int32)
    layers, half = own.shape[3], own.shape[5]
    return pl.pallas_call(
        functools.partial(widen_kernel, scale=scale),
        name="widen",
        out_shape=jax.ShapeDtypeStruct((layers, length, 2 * half), jnp.float32),
        in_specs=[
            pl.BlockSpec(memory_space=SMEM),
            pl.BlockSpec(memory_space=VMEM),
            pl.BlockSpec(memory_space=VMEM),
        ],
        out_specs=pl.BlockSpec(memory_space=pl.ANY),
        scratch_shapes=[
            pltpu.VMEM((layers, length, 2 * half), jnp.float32),
            pltpu.SemaphoreType.DMA((8,)),
        ],
        compiler_params=params(24),
        cost_estimate=pl.CostEstimate(flops=3_000_000, bytes_accessed=10_000_000, transcendentals=0),
    )(place, own, other)


def order_kernel(rows_ref, start_ref, end_ref, entry_ref, count):
    places = start_ref.shape[0]
    extent = 7
    slots = rows_ref.shape[0] // extent

    def begin(p, carry):
        count[p] = start_ref[p]
        return carry

    lax.fori_loop(0, places, begin, 0)

    def enter(slot, carry):
        @pl.when(rows_ref[slot * extent] >= 0)
        def _():
            for i in range(extent):
                first = rows_ref[slot * extent + i]
                for a in range(2):
                    n = count[first + a]
                    count[first + a] = n + 1
                    entry_ref[n] = slot * 16 + 2 * i + a

        return carry

    lax.fori_loop(0, slots, enter, 0)

    def fill(p, carry):
        def blank(n, inner):
            entry_ref[n] = 14
            return inner

        return lax.fori_loop(count[p], end_ref[p], blank, carry)

    lax.fori_loop(0, places, fill, 0)


def order_entries(rows, start, end, entries):
    return pl.pallas_call(
        order_kernel,
        name="order_entries",
        out_shape=jax.ShapeDtypeStruct((entries,), jnp.int32),
        in_specs=[pl.BlockSpec(memory_space=SMEM)] * 3,
        out_specs=pl.BlockSpec(memory_space=SMEM),
        scratch_shapes=[pltpu.SMEM((TILE,), jnp.int32)],
        cost_estimate=pl.CostEstimate(flops=10_000_000, bytes_accessed=30_000_000, transcendentals=0),
    )(rows, start, end)


def tile_kernel(
    base_ref,
    place_ref,
    groups_ref,
    got_hbm,
    corner_ref,
    low_ref,
    high_ref,
    out_hbm,
    biases_ref,
    landed,
    crops,
    out_ref,
    sems,
    out_sems,
):
    steps = sems.shape[0]
    owners, half = landed.shape[0] // steps, landed.shape[2]
    bins = 49
    block = owners * 200

    def fetch(step):
        part = pl.ds(step * owners, owners)
        used = pl.ds(0, landed.shape[1])
        return pltpu.make_async_copy(
            got_hbm.at[part, used, :], landed.at[part], sems.at[step]
        )

    for step in range(steps):
        fetch(step).start()
    out_ref[...] = jnp.zeros_like(out_ref)

    def convert(step, spare):
        fetch(step).wait()
        wide = landed[pl.ds(step * owners, owners)].astype(jnp.float32)[:, :200, :]
        crops[pl.ds(pl.multiple_of(step * block, 8), block), :] = wide.reshape(block, half)
        return spare + jnp.sum(wide[:, 192:, :], axis=0)

    biases_ref[...] = lax.fori_loop(0, steps, convert, jnp.zeros(biases_ref.shape, jnp.float32))

    position = lax.broadcasted_iota(jnp.int32, (TILE, corner_ref.shape[1]), 0).astype(jnp.float32)

    def columns(t):
        line = pl.ds(t, 1)
        corner = corner_ref[line, :]
        near = jnp.where(position == corner, low_ref[line, :], 0.0)
        far = jnp.where(position == corner + 1.0, high_ref[line, :], 0.0)
        return (near + far).astype(jnp.bfloat16)

    def group(t):
        left, right = [], []
        for n in range(GROUP):
            base = base_ref[t * GROUP + n]
            left.append(crops[pl.ds(base, 8), :])
            right.append(crops[pl.ds(base + bins, 8), :])
        values = jnp.concatenate(
            [jnp.concatenate(left, axis=0), jnp.concatenate(right, axis=0)], axis=1
        ).astype(jnp.bfloat16)
        return jnp.dot(columns(t), values, preferred_element_type=jnp.float32)

    def several(t, carry):
        terms = [group(t * UNROLL + u) for u in range(UNROLL)]
        for u in range(UNROLL):
            out_ref[place_ref[t * UNROLL + u]] += terms[u]
        return carry

    lax.fori_loop(0, (groups_ref[0] + UNROLL - 1) // UNROLL, several, 0)
    rows = out_ref.shape[0] // out_sems.shape[0]
    sends = []
    for step in range(out_sems.shape[0]):
        part = pl.ds(step * rows, rows)
        sends.append(pltpu.make_async_copy(out_ref.at[part], out_hbm.at[part], out_sems.at[step]))
    for send in sends:
        send.start()
    for send in sends:
        send.wait()


def tile_sum(base, place, groups, got, corner, low, high, channels):
    owners, rows, half = got.shape
    tile = (TILE, TILE, channels)
    return pl.pallas_call(
        tile_kernel,
        name="tile_sum",
        out_shape=(
            jax.ShapeDtypeStruct(tile, jnp.float32),
            jax.ShapeDtypeStruct((8, half), jnp.float32),
        ),
        grid_spec=pltpu.PrefetchScalarGridSpec(
            num_scalar_prefetch=3,
            grid=(1,),
            in_specs=[pl.BlockSpec(memory_space=pl.ANY)]
            + [pl.BlockSpec(corner.shape, lambda g, *refs: (0, 0))] * 3,
            out_specs=(
                pl.BlockSpec(memory_space=pl.ANY),
                pl.BlockSpec((8, half), lambda g, *refs: (0, 0)),
            ),
            scratch_shapes=[
                pltpu.VMEM((owners, 208, half), jnp.bfloat16),
                pltpu.VMEM((owners * 200, half), jnp.float32),
                pltpu.VMEM(tile, jnp.float32),
                pltpu.SemaphoreType.DMA((16,)),
                pltpu.SemaphoreType.DMA((8,)),
            ],
        ),
        compiler_params=params(58),
        cost_estimate=pl.CostEstimate(
            flops=2 * TILE * corner.size * channels, bytes_accessed=17_000_000, transcendentals=0
        ),
    )(base, place, groups, got, corner, low, high)


def fields_kernel(tiles_ref, rows_ref, cols_ref, row_weight_ref, col_weight_ref, send_ref, boxes_ref):
    per_box, boxes = tiles_ref.shape
    extent = rows_ref.shape[0]
    pieces = per_box * boxes

    def wide(parts):
        return jnp.concatenate(parts, axis=1)

    targets = wide([tiles_ref[t : t + 1, :].astype(jnp.float32) for t in range(per_box)])
    rows = wide([rows_ref[:, t, :].astype(jnp.float32) for t in range(per_box)])
    cols = wide([cols_ref[:, t, :].astype(jnp.float32) for t in range(per_box)])
    row_weight = [
        wide([row_weight_ref[t, :, a, :].astype(jnp.float32) for t in range(per_box)])
        for a in range(2)
    ]
    col_weight = [
        wide([col_weight_ref[t, :, a, :].astype(jnp.float32) for t in range(per_box)])
        for a in range(2)
    ]
    blank = jnp.zeros((1, pieces), jnp.float32)
    parts = [targets, jnp.zeros((6, pieces), jnp.float32), jnp.ones((1, pieces), jnp.float32)]
    for array in [rows, cols] + row_weight + col_weight:
        parts = parts + [array, blank]
    parts.append(jnp.zeros((8, pieces), jnp.float32))
    fields = jnp.concatenate(parts, axis=0).astype(jnp.bfloat16)
    tile = lax.broadcasted_iota(jnp.int32, (pieces, pieces), 0)
    piece = lax.broadcasted_iota(jnp.int32, (pieces, pieces), 1)
    match = targets.astype(jnp.int32) == tile
    upper = jnp.where(tile < piece, 1.0, 0.0).astype(jnp.bfloat16)
    chosen = jnp.where(match, 1.0, 0.0)
    earlier = jnp.dot(chosen.astype(jnp.bfloat16), upper, preferred_element_type=jnp.float32)
    box = (lax.broadcasted_iota(jnp.int32, (8, pieces), 1) % boxes).astype(jnp.float32)
    slots = []
    for rank in range(2):
        ranked = jnp.where(earlier == float(rank), chosen, 0.0).astype(jnp.bfloat16)
        found = lax.dot_general(
            box.astype(jnp.bfloat16),
            ranked,
            (((1,), (1,)), ((), ())),
            preferred_element_type=jnp.float32,
        )
        boxes_ref[rank : rank + 1, :] = found[:1].astype(jnp.int32)
        slots.append(
            lax.dot_general(
                ranked, fields, (((1,), (1,)), ((), ())), preferred_element_type=jnp.float32
            )
        )
    send_ref[...] = jnp.concatenate(slots, axis=1).astype(jnp.bfloat16)


def describe(tile_ids, corner_rows, corner_cols, row_weight, col_weight):
    pieces = tile_ids.size
    arrays = (
        jnp.transpose(tile_ids),
        jnp.transpose(corner_rows, (2, 1, 0)),
        jnp.transpose(corner_cols, (2, 1, 0)),
        jnp.transpose(row_weight, (1, 2, 3, 0)),
        jnp.transpose(col_weight, (1, 2, 3, 0)),
    )
    return pl.pallas_call(
        fields_kernel,
        name="describe",
        out_shape=(
            jax.ShapeDtypeStruct((pieces, 128), jnp.bfloat16),
            jax.ShapeDtypeStruct((2, pieces), jnp.int32),
        ),
        grid=(1,),
        in_specs=[pl.BlockSpec(array.shape, lambda g, n=array.ndim: (0,) * n) for array in arrays],
        out_specs=(
            pl.BlockSpec((pieces, 128), lambda g: (0, 0)),
            pl.BlockSpec((2, pieces), lambda g: (0, 0)),
        ),
        compiler_params=params(58),
        cost_estimate=pl.CostEstimate(flops=10_000_000, bytes_accessed=200_000, transcendentals=0),
    )(*arrays)


def arrange(slots, extent):
    count = slots.shape[0]
    groups = count * extent * 2 // GROUP + TILE
    entries = groups * GROUP
    wide = extent + 1
    rows = jnp.where(slots[:, 7:8] > 0.5, slots[:, 8 : 8 + extent], -4.0).astype(jnp.int32)
    pixel = jnp.arange(TILE, dtype=jnp.int32)
    flat = rows.reshape(-1)
    hits = (flat == pixel[:, None]).astype(jnp.int32) + (flat + 1 == pixel[:, None]).astype(jnp.int32)
    tally = jnp.sum(hits, axis=1)
    needed = (tally + GROUP - 1) // GROUP
    ends = jnp.sum(jnp.where(pixel[None, :] <= pixel[:, None], needed[None, :], 0), axis=1)
    start = (ends - needed) * GROUP
    place = jnp.sum((jnp.arange(groups)[:, None] >= ends[None, :-1]).astype(jnp.int32), axis=1)
    entry = order_entries(flat, start, ends * GROUP, entries)
    inside = jnp.arange(entries, dtype=jnp.int32) < ends[-1] * GROUP
    entry = jnp.where(inside, entry, 14)
    owner, code = entry // 16, entry % 16
    line = jnp.minimum(code // 2, extent - 1)
    base = owner // 2 * 200 + owner % 2 * 98 + extent * line
    chosen = (owner[:, None] == jnp.arange(count)).astype(jnp.bfloat16)
    values = jnp.dot(chosen, slots[:, 8:].astype(jnp.bfloat16), preferred_element_type=jnp.float32)
    which = jnp.arange(2 * wide, dtype=jnp.int32)
    wanted = (which[None, :] % wide == line[:, None]) & (which[None, :] // wide == code[:, None] % 2)
    wanted = wanted & (code[:, None] < 2 * extent)
    scale = jnp.sum(jnp.where(wanted, values[:, 2 * wide : 4 * wide], 0.0), axis=1)
    corner = values[:, wide : 2 * wide]
    low = values[:, 4 * wide : 5 * wide] * scale[:, None]
    high = values[:, 5 * wide : 6 * wide] * scale[:, None]

    def lanes(array):
        return array.reshape(groups, GROUP * wide)

    return base, place, ends[-1:], lanes(corner), lanes(low), lanes(high)


def shards(
    out_grad,
    saved,
    conv_weight,
    conv_bias,
    tile_ids,
    corner_rows,
    corner_cols,
    row_weight,
    col_weight,
):
    boxes, extent, channels = out_grad.shape[0], out_grad.shape[1], out_grad.shape[3]
    layers = saved.shape[0]
    devices = lax.axis_size("row") * lax.axis_size("col")
    grad_scale = 1.0 / math.sqrt(boxes * devices * extent * extent)
    slots, box_of_slot = describe(tile_ids, corner_rows, corner_cols, row_weight, col_weight)
    slots = lax.all_to_all(
        slots.reshape(devices, 1, -1), AXES, split_axis=0, concat_axis=0, tiled=True
    )

    grad_t = jnp.transpose(out_grad, (1, 2, 0, 3))
    saved_t = jnp.transpose(saved, (0, 2, 3, 1, 4))
    lines = devices * SUM_ROWS
    core = lax.axis_index("row") % 2
    own, give, crops, biases = conv_chain(grad_t, saved_t, conv_weight, conv_bias, core, lines)
    give, slots = lax.optimization_barrier((give, slots))
    other = lax.ppermute(give, "row", hop_core())
    tail = biases.reshape(layers * 2, channels // 2)
    send = pack(box_of_slot.reshape(-1), crops, tail, own, other, boxes)
    send, slots = lax.optimization_barrier((send, slots))
    got = lax.all_to_all(send, AXES, split_axis=0, concat_axis=0, tiled=True)

    base, place, groups, corner, low, high = arrange(slots.reshape(2 * devices, -1).astype(jnp.float32), extent)
    got, corner, low, high = lax.optimization_barrier((got, corner, low, high))
    cols = lax.axis_size("col")
    arrived = got[:, 200:, :].reshape(-1, layers, cols, SUM_ROWS, channels // 2)
    part = jnp.sum(arrived.astype(jnp.float32), axis=(0, 2)).astype(jnp.bfloat16)
    part = ring(ring(part, "col", hop_z), "col", hop_y)
    part, got = lax.optimization_barrier((part, got))
    own = ring(part, "row", hop_x)
    feature_grad, spare = tile_sum(base, place, groups, got, corner, low, high, channels)
    own, feature_grad = lax.optimization_barrier((own, feature_grad))
    other = lax.ppermute(own, "row", hop_core())
    weight_grad = widen(own, other, 9 * channels, grad_scale)
    bias_grad = (spare[4 : 4 + 2 * layers] * grad_scale).reshape(layers, channels)
    return (weight_grad, bias_grad, feature_grad)


def solution(mesh):
    in_specs = (
        P(AXES, None, None, None),
        P(None, AXES, None, None, None),
        P(),
        P(),
        P(AXES, None),
        P(AXES, None, None),
        P(AXES, None, None),
        P(AXES, None, None, None),
        P(AXES, None, None, None),
    )
    out_specs = (P(), P(), P("row", "col", None))
    return jax.shard_map(shards, mesh=mesh, in_specs=in_specs, out_specs=out_specs, check_vma=False)
```

```python
import functools
import math

import jax
import jax.numpy as jnp
from jax import lax
from jax.experimental import pallas as pl
from jax.experimental.pallas import tpu as pltpu
from jax.sharding import PartitionSpec as P

TILE = 64
SUM_ROWS = 40
GROUP = 32
UNROLL = 16
VMEM = pltpu.MemorySpace.VMEM
SMEM = pltpu.MemorySpace.SMEM
AXES = ("row", "col")


def params(megabytes):
    return pltpu.CompilerParams(vmem_limit_bytes=megabytes * 1024 * 1024)


def gelu_slope(pre_act):
    normal_cdf = 0.5 * (1.0 + lax.erf(pre_act * 0.7071067811865476))
    return normal_cdf + pre_act * jnp.exp(-0.5 * pre_act * pre_act) * 0.3989422804014327


def chain_kernel(
    grad_hbm,
    saved_hbm,
    weight_hbm,
    bias_ref,
    core_ref,
    own_hbm,
    give_hbm,
    crops_hbm,
    biases_ref,
    terms_ref,
    crops_ref,
    both,
    slopes,
    flow,
    grad_ref,
    weight_ref,
    sems,
    term_sems,
    crop_sems,
):
    extent, boxes, channels = grad_ref.shape[0], grad_ref.shape[2], grad_ref.shape[3]
    rows = extent * boxes
    inner = pl.ds(1, extent)
    fetches = {}
    for layer in (1, 0):
        fetches[layer] = [
            pltpu.make_async_copy(
                saved_hbm.at[layer], both.at[layer, inner, inner], sems.at[2 * layer]
            ),
            pltpu.make_async_copy(
                weight_hbm.at[layer], weight_ref.at[layer], sems.at[2 * layer + 1]
            ),
        ]
    fetches[1].append(pltpu.make_async_copy(grad_hbm, grad_ref, sems.at[4]))
    for layer in (1, 0):
        for fetch in fetches[layer]:
            fetch.start()

    def crop_copy(i):
        part = pl.ds(i * rows, rows)
        return pltpu.make_async_copy(
            crops_ref.at[:, part, :], crops_hbm.at[:, part, :], crop_sems.at[i]
        )

    slopes[...] = jnp.zeros_like(slopes)
    edge = jnp.zeros((extent + 2, boxes, channels), jnp.bfloat16)
    for layer in (1, 0):
        for end in (0, extent + 1):
            both[layer, end] = edge
            both[layer, 1 : extent + 1, end] = edge[:extent]
    for layer in (1, 0):
        padded = both.at[layer]
        for fetch in fetches[layer]:
            fetch.wait()

        def forward(i, sums, layer=layer, padded=padded):
            pieces = [
                padded[i + a, b : b + extent].reshape(rows, channels)
                for a in range(3)
                for b in range(3)
            ]
            pre = jnp.dot(
                jnp.concatenate(pieces, axis=1),
                weight_ref[layer].reshape(9 * channels, channels),
                preferred_element_type=jnp.float32,
            )
            pre = pre + bias_ref[layer : layer + 1, :]
            upper = grad_ref[i] if layer == 1 else flow[i]
            upper = upper.reshape(rows, channels).astype(jnp.float32)
            slope = (upper * gelu_slope(pre)).astype(jnp.bfloat16)
            slopes[i + 1, 1 : extent + 1] = slope.reshape(extent, boxes, channels)
            return sums + jnp.sum(
                slope.astype(jnp.float32).reshape(rows // 8, 8, channels), axis=0
            )

        sums = jnp.zeros((8, channels), jnp.float32)
        for i in range(extent):
            sums = forward(i, sums)
        sums = jnp.sum(sums, axis=0, keepdims=True)
        for half in range(2):
            biases_ref[2 * layer + half : 2 * layer + half + 1, :] = (
                sums[:, half * channels // 2 : (half + 1) * channels // 2]
            )

        def emit(target_hbm, layer=layer):
            return pltpu.make_async_copy(terms_ref.at[layer], target_hbm, term_sems.at[layer])

        whole = slopes[1 : extent + 1, 1 : extent + 1].reshape(extent * rows, channels)
        for k in range(9):
            piece = padded[pl.ds(k // 3, extent), pl.ds(k % 3, extent)]
            term = lax.dot_general(
                piece.reshape(extent * rows, channels),
                whole,
                (((0,), (0,)), ((), ())),
                preferred_element_type=jnp.float32,
            ).astype(jnp.bfloat16)
            for half in range(2):
                terms_ref[layer, (9 * half + k) * channels : (9 * half + k + 1) * channels, :] = (
                    term[:, half * channels // 2 : (half + 1) * channels // 2]
                )
        last = 18 * channels
        terms_ref[layer, last:, :] = jnp.zeros(
            (terms_ref.shape[1] - last, channels // 2), jnp.bfloat16
        )

        @pl.when(core_ref[0] == layer)
        def _(emit=emit):
            emit(own_hbm).start()

        @pl.when(core_ref[0] != layer)
        def _(emit=emit):
            emit(give_hbm).start()

        def backward(i, carry, layer=layer):
            total = jnp.zeros((rows, channels), jnp.float32)
            for a in range(3):
                for b in range(3):
                    piece = slopes[i + 2 - a, 2 - b : 2 - b + extent].reshape(rows, channels)
                    total = total + lax.dot_general(
                        piece,
                        weight_ref[layer, 3 * a + b],
                        (((1,), (1,)), ((), ())),
                        preferred_element_type=jnp.float32,
                    )
            if layer == 1:
                flow[i] = total.astype(jnp.bfloat16).reshape(extent, boxes, channels)
            else:
                place = pl.ds(i * rows, rows)
                crops_ref[0, place, :] = total[:, : channels // 2]
                crops_ref[1, place, :] = total[:, channels // 2 :]
                crop_copy(i).start()
            return carry

        for i in range(extent):
            backward(i, 0)
    for layer in (1, 0):
        pltpu.make_async_copy(terms_ref.at[layer], own_hbm, term_sems.at[layer]).wait()
    for i in range(extent):
        crop_copy(i).wait()


def conv_chain(grad_t, saved_t, weight, bias, core, lines):
    extent, boxes, channels = grad_t.shape[0], grad_t.shape[2], grad_t.shape[3]
    layers = saved_t.shape[0]
    padded = (extent + 2, extent + 2, boxes, channels)
    return pl.pallas_call(
        chain_kernel,
        name="conv_chain",
        out_shape=(
            jax.ShapeDtypeStruct((lines, channels // 2), jnp.bfloat16),
            jax.ShapeDtypeStruct((lines, channels // 2), jnp.bfloat16),
            jax.ShapeDtypeStruct((2, extent * extent * boxes, channels // 2), jnp.float32),
            jax.ShapeDtypeStruct((2 * layers, channels // 2), jnp.float32),
        ),
        in_specs=[pl.BlockSpec(memory_space=pl.ANY)] * 3
        + [pl.BlockSpec(memory_space=VMEM), pl.BlockSpec(memory_space=SMEM)],
        out_specs=(pl.BlockSpec(memory_space=pl.ANY),) * 3 + (pl.BlockSpec(memory_space=VMEM),),
        scratch_shapes=[
            pltpu.VMEM((layers, lines, channels // 2), jnp.bfloat16),
            pltpu.VMEM((2, extent * extent * boxes, channels // 2), jnp.float32),
            pltpu.VMEM((layers,) + padded, jnp.bfloat16),
            pltpu.VMEM(padded, jnp.bfloat16),
            pltpu.VMEM((extent, extent, boxes, channels), jnp.bfloat16),
            pltpu.VMEM(grad_t.shape, jnp.bfloat16),
            pltpu.VMEM(weight.shape, jnp.bfloat16),
            pltpu.SemaphoreType.DMA((5,)),
            pltpu.SemaphoreType.DMA((layers,)),
            pltpu.SemaphoreType.DMA((extent,)),
        ],
        compiler_params=params(56),
        cost_estimate=pl.CostEstimate(flops=22000000000, bytes_accessed=9000000, transcendentals=0),
    )(grad_t, saved_t, weight, bias, core.reshape(1))


def pack_kernel(
    box_ref,
    crops_hbm,
    tail_ref,
    own_hbm,
    other_hbm,
    out_hbm,
    first,
    second,
    staged,
    sums,
    out_ref,
    sems,
    crops_ref,
    own_ref,
    other_ref,
    fetch_sems,
):
    crops_fetch = pltpu.make_async_copy(crops_hbm, crops_ref, fetch_sems.at[0])
    own_fetch = pltpu.make_async_copy(own_hbm, own_ref, fetch_sems.at[1])
    other_fetch = pltpu.make_async_copy(other_hbm, other_ref, fetch_sems.at[2])
    crops_fetch.start()
    own_fetch.start()
    other_fetch.start()
    steps = sems.shape[0]
    owners = out_ref.shape[0]
    count = owners // steps
    lines = count * SUM_ROWS
    boxes = first.shape[0]
    bins = crops_ref.shape[1] // boxes
    staged[...] = jnp.zeros_like(staged)
    crops_fetch.wait()
    for box in range(boxes):
        for half in range(2):
            rows = crops_ref[half, pl.ds(box, bins, stride=boxes), :]
            staged[0, box, half * bins : (half + 1) * bins, :] = rows
            staged[1, box, half * bins + 2 : (half + 1) * bins + 2, :] = rows
        staged[1, box, 2 * bins + 2 : 2 * bins + 6, :] = tail_ref[...]
        first[box] = staged[0, box].astype(jnp.bfloat16)
        second[box] = staged[1, box].astype(jnp.bfloat16)
    blank = jnp.zeros((8, sums.shape[1]), jnp.float32)

    def both(left, right):
        return (left.astype(jnp.float32) + right.astype(jnp.float32)).astype(jnp.bfloat16)

    own_fetch.wait()
    other_fetch.wait()
    sends = []
    for step in range(steps):
        block = slice(step * lines, (step + 1) * lines)
        sums[...] = own_ref[block, :].astype(jnp.float32) + other_ref[block, :].astype(jnp.float32)

        def place(index, carry, step=step):
            owner = step * count + index
            one, two = first[box_ref[owner]], second[box_ref[owners + owner]]
            chunk = sums[pl.ds(pl.multiple_of(index * SUM_ROWS, 8), SUM_ROWS), :]
            chunk = jnp.concatenate([blank, chunk], axis=0).astype(jnp.bfloat16)
            out_ref[owner] = jnp.concatenate(
                [
                    one[:96],
                    both(one[96:112], two[:16]),
                    two[16:96],
                    both(two[96:112], chunk[:16]),
                    chunk[16:],
                ],
                axis=0,
            )
            return carry

        lax.fori_loop(0, count, place, 0, unroll=4)
        part = pl.ds(step * count, count)
        send = pltpu.make_async_copy(out_ref.at[part], out_hbm.at[part], sems.at[step])
        send.start()
        sends.append(send)
    for send in sends:
        send.wait()


def pack(box_of_slot, crops, tail, own, other, boxes):
    owners = box_of_slot.shape[0] // 2
    steps = 16
    half = crops.shape[2]
    rows = 200 + SUM_ROWS
    return pl.pallas_call(
        pack_kernel,
        name="pack",
        out_shape=jax.ShapeDtypeStruct((owners, rows, half), jnp.bfloat16),
        grid_spec=pltpu.PrefetchScalarGridSpec(
            num_scalar_prefetch=1,
            grid=(1,),
            in_specs=[
                pl.BlockSpec(memory_space=pl.ANY),
                pl.BlockSpec(tail.shape, lambda g, ids: (0, 0)),
                pl.BlockSpec(memory_space=pl.ANY),
                pl.BlockSpec(memory_space=pl.ANY),
            ],
            out_specs=pl.BlockSpec(memory_space=pl.ANY),
            scratch_shapes=[
                pltpu.VMEM((boxes, 112, half), jnp.bfloat16),
                pltpu.VMEM((boxes, 112, half), jnp.bfloat16),
                pltpu.VMEM((2, boxes, 112, half), jnp.float32),
                pltpu.VMEM((owners // steps * SUM_ROWS, half), jnp.float32),
                pltpu.VMEM((owners, rows, half), jnp.bfloat16),
                pltpu.SemaphoreType.DMA((steps,)),
                pltpu.VMEM(crops.shape, crops.dtype),
                pltpu.VMEM(own.shape, own.dtype),
                pltpu.VMEM(other.shape, other.dtype),
                pltpu.SemaphoreType.DMA((3,)),
            ],
        ),
        compiler_params=params(56),
        cost_estimate=pl.CostEstimate(flops=1_000_000, bytes_accessed=9_000_000, transcendentals=0),
    )(box_of_slot, crops, tail, own, other)


def hop_core():
    return [(r, r ^ 1) for r in range(8)]


def hop_x(k):
    return [(r, (r // 2 + k) % 4 * 2 + r % 2) for r in range(8)]


def hop_y(k):
    return [(c, c // 4 * 4 + (c % 4 + k) % 4) for c in range(16)]


def hop_z(k):
    return [(c, (c // 4 + k) % 4 * 4 + c % 4) for c in range(16)]


def ring(part, name, hop):
    return jnp.stack([part] + [lax.ppermute(part, name, hop(k)) for k in (3, 2, 1)])


def widen_kernel(place_ref, own_ref, other_ref, out_hbm, out_ref, sems, *, scale):
    length, half = out_ref.shape[1], out_ref.shape[2] // 2
    turns = [[lax.rem(q + 4 - place_ref[axis], 4) for q in range(4)] for axis in range(3)]

    def copy(core, source_ref):
        for x in range(4):
            for z in range(4):
                for y in range(4):
                    start = (((x * 2 + core) * 4 + z) * 4 + y) * SUM_ROWS
                    values = source_ref[turns[0][x], turns[1][y], turns[2][z]].astype(jnp.float32)
                    values = values * scale
                    for column in range(2):
                        low = max(start, column * length)
                        high = min(start + SUM_ROWS, (column + 1) * length)
                        if low < high:
                            out_ref[
                                :,
                                low - column * length : high - column * length,
                                column * half : (column + 1) * half,
                            ] = values[:, low - start : high - start, :]

    for core in range(2):

        @pl.when(place_ref[3] == core)
        def _(core=core):
            copy(core, own_ref)
            copy(1 - core, other_ref)

    parts = sems.shape[0]
    rows = length // parts
    sends = []
    for step in range(parts):
        part = pl.ds(step * rows, rows)
        sends.append(
            pltpu.make_async_copy(out_ref.at[:, part, :], out_hbm.at[:, part, :], sems.at[step])
        )
    for send in sends:
        send.start()
    for send in sends:
        send.wait()


def widen(own, other, length, scale):
    row, col = lax.axis_index("row"), lax.axis_index("col")
    place = jnp.stack([row // 2, col % 4, col // 4, row % 2]).astype(jnp.int32)
    layers, half = own.shape[3], own.shape[5]
    return pl.pallas_call(
        functools.partial(widen_kernel, scale=scale),
        name="widen",
        out_shape=jax.ShapeDtypeStruct((layers, length, 2 * half), jnp.float32),
        in_specs=[
            pl.BlockSpec(memory_space=SMEM),
            pl.BlockSpec(memory_space=VMEM),
            pl.BlockSpec(memory_space=VMEM),
        ],
        out_specs=pl.BlockSpec(memory_space=pl.ANY),
        scratch_shapes=[
            pltpu.VMEM((layers, length, 2 * half), jnp.float32),
            pltpu.SemaphoreType.DMA((8,)),
        ],
        compiler_params=params(24),
        cost_estimate=pl.CostEstimate(flops=3_000_000, bytes_accessed=10_000_000, transcendentals=0),
    )(place, own, other)


def order_kernel(rows_ref, start_ref, end_ref, entry_ref, count):
    places = start_ref.shape[0]
    extent = 7
    slots = rows_ref.shape[0] // extent

    def begin(p, carry):
        count[p] = start_ref[p]
        return carry

    lax.fori_loop(0, places, begin, 0)

    def enter(slot, carry):
        @pl.when(rows_ref[slot * extent] >= 0)
        def _():
            for i in range(extent):
                first = rows_ref[slot * extent + i]
                for a in range(2):
                    n = count[first + a]
                    count[first + a] = n + 1
                    entry_ref[n] = slot * 16 + 2 * i + a

        return carry

    lax.fori_loop(0, slots, enter, 0)

    def fill(p, carry):
        def blank(n, inner):
            entry_ref[n] = 14
            return inner

        return lax.fori_loop(count[p], end_ref[p], blank, carry)

    lax.fori_loop(0, places, fill, 0)


def order_entries(rows, start, end, entries):
    return pl.pallas_call(
        order_kernel,
        name="order_entries",
        out_shape=jax.ShapeDtypeStruct((entries,), jnp.int32),
        in_specs=[pl.BlockSpec(memory_space=SMEM)] * 3,
        out_specs=pl.BlockSpec(memory_space=SMEM),
        scratch_shapes=[pltpu.SMEM((TILE,), jnp.int32)],
        cost_estimate=pl.CostEstimate(flops=10_000_000, bytes_accessed=30_000_000, transcendentals=0),
    )(rows, start, end)


def tile_kernel(
    base_ref,
    place_ref,
    groups_ref,
    got_hbm,
    corner_ref,
    low_ref,
    high_ref,
    out_hbm,
    biases_ref,
    landed,
    crops,
    out_ref,
    sems,
    out_sems,
):
    steps = sems.shape[0]
    owners, half = landed.shape[0] // steps, landed.shape[2]
    bins = 49
    block = owners * 200

    def fetch(step):
        part = pl.ds(step * owners, owners)
        used = pl.ds(0, landed.shape[1])
        return pltpu.make_async_copy(
            got_hbm.at[part, used, :], landed.at[part], sems.at[step]
        )

    for step in range(steps):
        fetch(step).start()
    out_ref[...] = jnp.zeros_like(out_ref)

    def convert(step, spare):
        fetch(step).wait()
        wide = landed[pl.ds(step * owners, owners)].astype(jnp.float32)[:, :200, :]
        crops[pl.ds(pl.multiple_of(step * block, 8), block), :] = wide.reshape(block, half)
        return spare + jnp.sum(wide[:, 192:, :], axis=0)

    biases_ref[...] = lax.fori_loop(0, steps, convert, jnp.zeros(biases_ref.shape, jnp.float32))

    position = lax.broadcasted_iota(jnp.int32, (TILE, corner_ref.shape[1]), 0).astype(jnp.float32)

    def columns(t):
        line = pl.ds(t, 1)
        corner = corner_ref[line, :]
        near = jnp.where(position == corner, low_ref[line, :], 0.0)
        far = jnp.where(position == corner + 1.0, high_ref[line, :], 0.0)
        return (near + far).astype(jnp.bfloat16)

    def group(t):
        left, right = [], []
        for n in range(GROUP):
            base = base_ref[t * GROUP + n]
            left.append(crops[pl.ds(base, 8), :])
            right.append(crops[pl.ds(base + bins, 8), :])
        values = jnp.concatenate(
            [jnp.concatenate(left, axis=0), jnp.concatenate(right, axis=0)], axis=1
        ).astype(jnp.bfloat16)
        return jnp.dot(columns(t), values, preferred_element_type=jnp.float32)

    def several(t, carry):
        terms = [group(t * UNROLL + u) for u in range(UNROLL)]
        for u in range(UNROLL):
            out_ref[place_ref[t * UNROLL + u]] += terms[u]
        return carry

    lax.fori_loop(0, (groups_ref[0] + UNROLL - 1) // UNROLL, several, 0)
    rows = out_ref.shape[0] // out_sems.shape[0]
    sends = []
    for step in range(out_sems.shape[0]):
        part = pl.ds(step * rows, rows)
        sends.append(pltpu.make_async_copy(out_ref.at[part], out_hbm.at[part], out_sems.at[step]))
    for send in sends:
        send.start()
    for send in sends:
        send.wait()


def tile_sum(base, place, groups, got, corner, low, high, channels):
    owners, rows, half = got.shape
    tile = (TILE, TILE, channels)
    return pl.pallas_call(
        tile_kernel,
        name="tile_sum",
        out_shape=(
            jax.ShapeDtypeStruct(tile, jnp.float32),
            jax.ShapeDtypeStruct((8, half), jnp.float32),
        ),
        grid_spec=pltpu.PrefetchScalarGridSpec(
            num_scalar_prefetch=3,
            grid=(1,),
            in_specs=[pl.BlockSpec(memory_space=pl.ANY)]
            + [pl.BlockSpec(corner.shape, lambda g, *refs: (0, 0))] * 3,
            out_specs=(
                pl.BlockSpec(memory_space=pl.ANY),
                pl.BlockSpec((8, half), lambda g, *refs: (0, 0)),
            ),
            scratch_shapes=[
                pltpu.VMEM((owners, 208, half), jnp.bfloat16),
                pltpu.VMEM((owners * 200, half), jnp.float32),
                pltpu.VMEM(tile, jnp.float32),
                pltpu.SemaphoreType.DMA((16,)),
                pltpu.SemaphoreType.DMA((8,)),
            ],
        ),
        compiler_params=params(58),
        cost_estimate=pl.CostEstimate(
            flops=2 * TILE * corner.size * channels, bytes_accessed=17_000_000, transcendentals=0
        ),
    )(base, place, groups, got, corner, low, high)


def fields_kernel(tiles_ref, rows_ref, cols_ref, row_weight_ref, col_weight_ref, send_ref, boxes_ref):
    per_box, boxes = tiles_ref.shape
    extent = rows_ref.shape[0]
    pieces = per_box * boxes

    def wide(parts):
        return jnp.concatenate(parts, axis=1)

    targets = wide([tiles_ref[t : t + 1, :].astype(jnp.float32) for t in range(per_box)])
    rows = wide([rows_ref[:, t, :].astype(jnp.float32) for t in range(per_box)])
    cols = wide([cols_ref[:, t, :].astype(jnp.float32) for t in range(per_box)])
    row_weight = [
        wide([row_weight_ref[t, :, a, :].astype(jnp.float32) for t in range(per_box)])
        for a in range(2)
    ]
    col_weight = [
        wide([col_weight_ref[t, :, a, :].astype(jnp.float32) for t in range(per_box)])
        for a in range(2)
    ]
    blank = jnp.zeros((1, pieces), jnp.float32)
    parts = [targets, jnp.zeros((6, pieces), jnp.float32), jnp.ones((1, pieces), jnp.float32)]
    for array in [rows, cols] + row_weight + col_weight:
        parts = parts + [array, blank]
    parts.append(jnp.zeros((8, pieces), jnp.float32))
    fields = jnp.concatenate(parts, axis=0).astype(jnp.bfloat16)
    tile = lax.broadcasted_iota(jnp.int32, (pieces, pieces), 0)
    piece = lax.broadcasted_iota(jnp.int32, (pieces, pieces), 1)
    match = targets.astype(jnp.int32) == tile
    upper = jnp.where(tile < piece, 1.0, 0.0).astype(jnp.bfloat16)
    chosen = jnp.where(match, 1.0, 0.0)
    earlier = jnp.dot(chosen.astype(jnp.bfloat16), upper, preferred_element_type=jnp.float32)
    box = (lax.broadcasted_iota(jnp.int32, (8, pieces), 1) % boxes).astype(jnp.float32)
    slots = []
    for rank in range(2):
        ranked = jnp.where(earlier == float(rank), chosen, 0.0).astype(jnp.bfloat16)
        found = lax.dot_general(
            box.astype(jnp.bfloat16),
            ranked,
            (((1,), (1,)), ((), ())),
            preferred_element_type=jnp.float32,
        )
        boxes_ref[rank : rank + 1, :] = found[:1].astype(jnp.int32)
        slots.append(
            lax.dot_general(
                ranked, fields, (((1,), (1,)), ((), ())), preferred_element_type=jnp.float32
            )
        )
    send_ref[:, 0, :] = jnp.concatenate(slots, axis=1).astype(jnp.bfloat16)


def describe(tile_ids, corner_rows, corner_cols, row_weight, col_weight):
    pieces = tile_ids.size
    arrays = (
        jnp.transpose(tile_ids),
        jnp.transpose(corner_rows, (2, 1, 0)),
        jnp.transpose(corner_cols, (2, 1, 0)),
        jnp.transpose(row_weight, (1, 2, 3, 0)),
        jnp.transpose(col_weight, (1, 2, 3, 0)),
    )
    return pl.pallas_call(
        fields_kernel,
        name="describe",
        out_shape=(
            jax.ShapeDtypeStruct((pieces, 1, 128), jnp.bfloat16),
            jax.ShapeDtypeStruct((2, pieces), jnp.int32),
        ),
        grid=(1,),
        in_specs=[pl.BlockSpec(array.shape, lambda g, n=array.ndim: (0,) * n) for array in arrays],
        out_specs=(
            pl.BlockSpec((pieces, 1, 128), lambda g: (0, 0, 0)),
            pl.BlockSpec((2, pieces), lambda g: (0, 0)),
        ),
        compiler_params=params(58),
        cost_estimate=pl.CostEstimate(flops=10_000_000, bytes_accessed=200_000, transcendentals=0),
    )(*arrays)


def arrange(slots, extent):
    count = slots.shape[0]
    groups = count * extent * 2 // GROUP + TILE
    entries = groups * GROUP
    wide = extent + 1
    rows = jnp.where(slots[:, 7:8] > 0.5, slots[:, 8 : 8 + extent], -4.0).astype(jnp.int32)
    pixel = jnp.arange(TILE, dtype=jnp.int32)
    flat = rows.reshape(-1)
    hits = (flat == pixel[:, None]).astype(jnp.int32) + (flat + 1 == pixel[:, None]).astype(jnp.int32)
    tally = jnp.sum(hits, axis=1)
    needed = (tally + GROUP - 1) // GROUP
    ends = jnp.sum(jnp.where(pixel[None, :] <= pixel[:, None], needed[None, :], 0), axis=1)
    start = (ends - needed) * GROUP
    place = jnp.sum((jnp.arange(groups)[:, None] >= ends[None, :-1]).astype(jnp.int32), axis=1)
    entry = order_entries(flat, start, ends * GROUP, entries)
    inside = jnp.arange(entries, dtype=jnp.int32) < ends[-1] * GROUP
    entry = jnp.where(inside, entry, 14)
    owner, code = entry // 16, entry % 16
    line = jnp.minimum(code // 2, extent - 1)
    base = owner // 2 * 200 + owner % 2 * 98 + extent * line
    chosen = (owner[:, None] == jnp.arange(count)).astype(jnp.bfloat16)
    values = jnp.dot(chosen, slots[:, 8:].astype(jnp.bfloat16), preferred_element_type=jnp.float32)
    which = jnp.arange(2 * wide, dtype=jnp.int32)
    wanted = (which[None, :] % wide == line[:, None]) & (which[None, :] // wide == code[:, None] % 2)
    wanted = wanted & (code[:, None] < 2 * extent)
    scale = jnp.sum(jnp.where(wanted, values[:, 2 * wide : 4 * wide], 0.0), axis=1)
    corner = values[:, wide : 2 * wide]
    low = values[:, 4 * wide : 5 * wide] * scale[:, None]
    high = values[:, 5 * wide : 6 * wide] * scale[:, None]

    def lanes(array):
        return array.reshape(groups, GROUP * wide)

    return base, place, ends[-1:], lanes(corner), lanes(low), lanes(high)


def shards(
    out_grad,
    saved,
    conv_weight,
    conv_bias,
    tile_ids,
    corner_rows,
    corner_cols,
    row_weight,
    col_weight,
):
    boxes, extent, channels = out_grad.shape[0], out_grad.shape[1], out_grad.shape[3]
    layers = saved.shape[0]
    devices = lax.axis_size("row") * lax.axis_size("col")
    grad_scale = 1.0 / math.sqrt(boxes * devices * extent * extent)
    slots, box_of_slot = describe(tile_ids, corner_rows, corner_cols, row_weight, col_weight)
    slots = lax.all_to_all(slots, AXES, split_axis=0, concat_axis=0, tiled=True)

    grad_t = jnp.transpose(out_grad, (1, 2, 0, 3))
    saved_t = jnp.transpose(saved, (0, 2, 3, 1, 4))
    lines = devices * SUM_ROWS
    core = lax.axis_index("row") % 2
    own, give, crops, biases = conv_chain(grad_t, saved_t, conv_weight, conv_bias, core, lines)
    give, slots = lax.optimization_barrier((give, slots))
    other = lax.ppermute(give, "row", hop_core())
    send = pack(box_of_slot.reshape(-1), crops, biases, own, other, boxes)
    send, slots = lax.optimization_barrier((send, slots))
    got = lax.all_to_all(send, AXES, split_axis=0, concat_axis=0, tiled=True)

    base, place, groups, corner, low, high = arrange(slots.reshape(2 * devices, -1).astype(jnp.float32), extent)
    got, place, corner, low, high = lax.optimization_barrier((got, place, corner, low, high))
    cols = lax.axis_size("col")
    arrived = got[:, 200:, :].reshape(-1, layers, cols, SUM_ROWS, channels // 2)
    part = jnp.sum(arrived.astype(jnp.float32), axis=(0, 2)).astype(jnp.bfloat16)
    part = ring(ring(part, "col", hop_z), "col", hop_y)
    part, got = lax.optimization_barrier((part, got))
    own = ring(part, "row", hop_x)
    feature_grad, spare = tile_sum(base, place, groups, got, corner, low, high, channels)
    own, feature_grad = lax.optimization_barrier((own, feature_grad))
    other = lax.ppermute(own, "row", hop_core())
    weight_grad = widen(own, other, 9 * channels, grad_scale)
    bias_grad = (spare[4 : 4 + 2 * layers] * grad_scale).reshape(layers, channels)
    return (weight_grad, bias_grad, feature_grad)


def solution(mesh):
    in_specs = (
        P(AXES, None, None, None),
        P(None, AXES, None, None, None),
        P(),
        P(),
        P(AXES, None),
        P(AXES, None, None),
        P(AXES, None, None),
        P(AXES, None, None, None),
        P(AXES, None, None, None),
    )
    out_specs = (P(), P(), P("row", "col", None))
    return jax.shard_map(shards, mesh=mesh, in_specs=in_specs, out_specs=out_specs, check_vma=False)
```

```python
import functools
import math

import jax
import jax.numpy as jnp
from jax import lax
from jax.experimental import pallas as pl
from jax.experimental.pallas import tpu as pltpu
from jax.sharding import PartitionSpec as P

TILE = 64
SUM_ROWS = 40
GROUP = 32
UNROLL = 16
VMEM = pltpu.MemorySpace.VMEM
SMEM = pltpu.MemorySpace.SMEM
AXES = ("row", "col")


def params(megabytes):
    return pltpu.CompilerParams(vmem_limit_bytes=megabytes * 1024 * 1024)


def gelu_slope(pre_act):
    normal_cdf = 0.5 * (1.0 + lax.erf(pre_act * 0.7071067811865476))
    return normal_cdf + pre_act * jnp.exp(-0.5 * pre_act * pre_act) * 0.3989422804014327


def chain_kernel(
    grad_hbm,
    saved_hbm,
    weight_hbm,
    bias_ref,
    core_ref,
    own_hbm,
    give_hbm,
    crops_hbm,
    biases_ref,
    terms_ref,
    crops_ref,
    both,
    slopes,
    flow,
    grad_ref,
    weight_ref,
    sems,
    term_sems,
    crop_sems,
):
    extent, boxes, channels = grad_ref.shape[0], grad_ref.shape[2], grad_ref.shape[3]
    rows = extent * boxes
    inner = pl.ds(1, extent)
    fetches = {}
    for layer in (1, 0):
        fetches[layer] = [
            pltpu.make_async_copy(
                saved_hbm.at[layer], both.at[layer, inner, inner], sems.at[2 * layer]
            ),
            pltpu.make_async_copy(
                weight_hbm.at[layer], weight_ref.at[layer], sems.at[2 * layer + 1]
            ),
        ]
    fetches[1].append(pltpu.make_async_copy(grad_hbm, grad_ref, sems.at[4]))
    for layer in (1, 0):
        for fetch in fetches[layer]:
            fetch.start()

    def crop_copy(i):
        part = pl.ds(i * rows, rows)
        return pltpu.make_async_copy(
            crops_ref.at[:, part, :], crops_hbm.at[:, part, :], crop_sems.at[i]
        )

    slopes[...] = jnp.zeros_like(slopes)
    edge = jnp.zeros((extent + 2, boxes, channels), jnp.bfloat16)
    for layer in (1, 0):
        for end in (0, extent + 1):
            both[layer, end] = edge
            both[layer, 1 : extent + 1, end] = edge[:extent]
    for layer in (1, 0):
        padded = both.at[layer]
        for fetch in fetches[layer]:
            fetch.wait()

        def forward(i, sums, layer=layer, padded=padded):
            pieces = [
                padded[i + a, b : b + extent].reshape(rows, channels)
                for a in range(3)
                for b in range(3)
            ]
            pre = jnp.dot(
                jnp.concatenate(pieces, axis=1),
                weight_ref[layer].reshape(9 * channels, channels),
                preferred_element_type=jnp.float32,
            )
            pre = pre + bias_ref[layer : layer + 1, :]
            upper = grad_ref[i] if layer == 1 else flow[i]
            upper = upper.reshape(rows, channels).astype(jnp.float32)
            slope = (upper * gelu_slope(pre)).astype(jnp.bfloat16)
            slopes[i + 1, 1 : extent + 1] = slope.reshape(extent, boxes, channels)
            return sums + jnp.sum(
                slope.astype(jnp.float32).reshape(rows // 8, 8, channels), axis=0
            )

        sums = jnp.zeros((8, channels), jnp.float32)
        for i in range(extent):
            sums = forward(i, sums)
        sums = jnp.sum(sums, axis=0, keepdims=True)
        for half in range(2):
            biases_ref[2 * layer + half : 2 * layer + half + 1, :] = (
                sums[:, half * channels // 2 : (half + 1) * channels // 2]
            )

        def emit(target_hbm, layer=layer):
            return pltpu.make_async_copy(terms_ref.at[layer], target_hbm, term_sems.at[layer])

        whole = slopes[1 : extent + 1, 1 : extent + 1].reshape(extent * rows, channels)
        for k in range(9):
            piece = padded[pl.ds(k // 3, extent), pl.ds(k % 3, extent)]
            term = lax.dot_general(
                piece.reshape(extent * rows, channels),
                whole,
                (((0,), (0,)), ((), ())),
                preferred_element_type=jnp.float32,
            ).astype(jnp.bfloat16)
            for half in range(2):
                terms_ref[layer, (9 * half + k) * channels : (9 * half + k + 1) * channels, :] = (
                    term[:, half * channels // 2 : (half + 1) * channels // 2]
                )
        last = 18 * channels
        terms_ref[layer, last:, :] = jnp.zeros(
            (terms_ref.shape[1] - last, channels // 2), jnp.bfloat16
        )

        @pl.when(core_ref[0] == layer)
        def _(emit=emit):
            emit(own_hbm).start()

        @pl.when(core_ref[0] != layer)
        def _(emit=emit):
            emit(give_hbm).start()

        def backward(i, carry, layer=layer):
            total = jnp.zeros((rows, channels), jnp.float32)
            for a in range(3):
                for b in range(3):
                    piece = slopes[i + 2 - a, 2 - b : 2 - b + extent].reshape(rows, channels)
                    total = total + lax.dot_general(
                        piece,
                        weight_ref[layer, 3 * a + b],
                        (((1,), (1,)), ((), ())),
                        preferred_element_type=jnp.float32,
                    )
            if layer == 1:
                flow[i] = total.astype(jnp.bfloat16).reshape(extent, boxes, channels)
            else:
                place = pl.ds(i * rows, rows)
                crops_ref[0, place, :] = total[:, : channels // 2]
                crops_ref[1, place, :] = total[:, channels // 2 :]
                crop_copy(i).start()
            return carry

        for i in range(extent):
            backward(i, 0)
    for layer in (1, 0):
        pltpu.make_async_copy(terms_ref.at[layer], own_hbm, term_sems.at[layer]).wait()
    for i in range(extent):
        crop_copy(i).wait()


def conv_chain(grad_t, saved_t, weight, bias, core, lines):
    extent, boxes, channels = grad_t.shape[0], grad_t.shape[2], grad_t.shape[3]
    layers = saved_t.shape[0]
    padded = (extent + 2, extent + 2, boxes, channels)
    return pl.pallas_call(
        chain_kernel,
        name="conv_chain",
        out_shape=(
            jax.ShapeDtypeStruct((lines, channels // 2), jnp.bfloat16),
            jax.ShapeDtypeStruct((lines, channels // 2), jnp.bfloat16),
            jax.ShapeDtypeStruct((2, extent * extent * boxes, channels // 2), jnp.float32),
            jax.ShapeDtypeStruct((2 * layers, channels // 2), jnp.float32),
        ),
        in_specs=[pl.BlockSpec(memory_space=pl.ANY)] * 3
        + [pl.BlockSpec(memory_space=VMEM), pl.BlockSpec(memory_space=SMEM)],
        out_specs=(pl.BlockSpec(memory_space=pl.ANY),) * 3 + (pl.BlockSpec(memory_space=VMEM),),
        scratch_shapes=[
            pltpu.VMEM((layers, lines, channels // 2), jnp.bfloat16),
            pltpu.VMEM((2, extent * extent * boxes, channels // 2), jnp.float32),
            pltpu.VMEM((layers,) + padded, jnp.bfloat16),
            pltpu.VMEM(padded, jnp.bfloat16),
            pltpu.VMEM((extent, extent, boxes, channels), jnp.bfloat16),
            pltpu.VMEM(grad_t.shape, jnp.bfloat16),
            pltpu.VMEM(weight.shape, jnp.bfloat16),
            pltpu.SemaphoreType.DMA((5,)),
            pltpu.SemaphoreType.DMA((layers,)),
            pltpu.SemaphoreType.DMA((extent,)),
        ],
        compiler_params=params(56),
        cost_estimate=pl.CostEstimate(flops=22000000000, bytes_accessed=9000000, transcendentals=0),
    )(grad_t, saved_t, weight, bias, core.reshape(1))


def pack_kernel(
    box_ref,
    crops_hbm,
    tail_ref,
    own_hbm,
    other_hbm,
    out_hbm,
    first,
    second,
    staged,
    sums,
    out_ref,
    sems,
    crops_ref,
    own_ref,
    other_ref,
    fetch_sems,
):
    crops_fetch = pltpu.make_async_copy(crops_hbm, crops_ref, fetch_sems.at[0])
    own_fetch = pltpu.make_async_copy(own_hbm, own_ref, fetch_sems.at[1])
    other_fetch = pltpu.make_async_copy(other_hbm, other_ref, fetch_sems.at[2])
    crops_fetch.start()
    own_fetch.start()
    other_fetch.start()
    steps = sems.shape[0]
    owners = out_ref.shape[0]
    count = owners // steps
    lines = count * SUM_ROWS
    boxes = first.shape[0]
    bins = crops_ref.shape[1] // boxes
    staged[...] = jnp.zeros_like(staged)
    crops_fetch.wait()
    for box in range(boxes):
        for half in range(2):
            rows = crops_ref[half, pl.ds(box, bins, stride=boxes), :]
            staged[0, box, half * bins : (half + 1) * bins, :] = rows
            staged[1, box, half * bins + 2 : (half + 1) * bins + 2, :] = rows
        staged[1, box, 2 * bins + 2 : 2 * bins + 6, :] = tail_ref[...]
        first[box] = staged[0, box].astype(jnp.bfloat16)
        second[box] = staged[1, box].astype(jnp.bfloat16)
    blank = jnp.zeros((8, sums.shape[1]), jnp.float32)

    def both(left, right):
        return (left.astype(jnp.float32) + right.astype(jnp.float32)).astype(jnp.bfloat16)

    own_fetch.wait()
    other_fetch.wait()
    sends = []
    for step in range(steps):
        block = slice(step * lines, (step + 1) * lines)
        sums[...] = own_ref[block, :].astype(jnp.float32) + other_ref[block, :].astype(jnp.float32)

        def place(index, carry, step=step):
            owner = step * count + index
            one, two = first[box_ref[owner]], second[box_ref[owners + owner]]
            chunk = sums[pl.ds(pl.multiple_of(index * SUM_ROWS, 8), SUM_ROWS), :]
            chunk = jnp.concatenate([blank, chunk], axis=0).astype(jnp.bfloat16)
            out_ref[owner] = jnp.concatenate(
                [
                    one[:96],
                    both(one[96:112], two[:16]),
                    two[16:96],
                    both(two[96:112], chunk[:16]),
                    chunk[16:],
                ],
                axis=0,
            )
            return carry

        lax.fori_loop(0, count, place, 0, unroll=4)
        part = pl.ds(step * count, count)
        send = pltpu.make_async_copy(out_ref.at[part], out_hbm.at[part], sems.at[step])
        send.start()
        sends.append(send)
    for send in sends:
        send.wait()


def pack(box_of_slot, crops, tail, own, other, boxes):
    owners = box_of_slot.shape[0] // 2
    steps = 16
    half = crops.shape[2]
    rows = 200 + SUM_ROWS
    return pl.pallas_call(
        pack_kernel,
        name="pack",
        out_shape=jax.ShapeDtypeStruct((owners, rows, half), jnp.bfloat16),
        grid_spec=pltpu.PrefetchScalarGridSpec(
            num_scalar_prefetch=1,
            grid=(1,),
            in_specs=[
                pl.BlockSpec(memory_space=pl.ANY),
                pl.BlockSpec(tail.shape, lambda g, ids: (0, 0)),
                pl.BlockSpec(memory_space=pl.ANY),
                pl.BlockSpec(memory_space=pl.ANY),
            ],
            out_specs=pl.BlockSpec(memory_space=pl.ANY),
            scratch_shapes=[
                pltpu.VMEM((boxes, 112, half), jnp.bfloat16),
                pltpu.VMEM((boxes, 112, half), jnp.bfloat16),
                pltpu.VMEM((2, boxes, 112, half), jnp.float32),
                pltpu.VMEM((owners // steps * SUM_ROWS, half), jnp.float32),
                pltpu.VMEM((owners, rows, half), jnp.bfloat16),
                pltpu.SemaphoreType.DMA((steps,)),
                pltpu.VMEM(crops.shape, crops.dtype),
                pltpu.VMEM(own.shape, own.dtype),
                pltpu.VMEM(other.shape, other.dtype),
                pltpu.SemaphoreType.DMA((3,)),
            ],
        ),
        compiler_params=params(56),
        cost_estimate=pl.CostEstimate(flops=1_000_000, bytes_accessed=9_000_000, transcendentals=0),
    )(box_of_slot, crops, tail, own, other)


def hop_core():
    return [(r, r ^ 1) for r in range(8)]


def hop_x(k):
    return [(r, (r // 2 + k) % 4 * 2 + r % 2) for r in range(8)]


def hop_y(k):
    return [(c, c // 4 * 4 + (c % 4 + k) % 4) for c in range(16)]


def hop_z(k):
    return [(c, (c // 4 + k) % 4 * 4 + c % 4) for c in range(16)]


def ring(part, name, hop):
    return jnp.stack([part] + [lax.ppermute(part, name, hop(k)) for k in (3, 2, 1)])


def widen_kernel(place_ref, own_ref, other_ref, out_hbm, out_ref, sems, *, scale):
    length, half = out_ref.shape[1], out_ref.shape[2] // 2
    turns = [[lax.rem(q + 4 - place_ref[axis], 4) for q in range(4)] for axis in range(3)]

    def copy(core, source_ref):
        for x in range(4):
            for z in range(4):
                for y in range(4):
                    start = (((x * 2 + core) * 4 + z) * 4 + y) * SUM_ROWS
                    values = source_ref[turns[0][x], turns[1][y], turns[2][z]].astype(jnp.float32)
                    values = values * scale
                    for column in range(2):
                        low = max(start, column * length)
                        high = min(start + SUM_ROWS, (column + 1) * length)
                        if low < high:
                            out_ref[
                                :,
                                low - column * length : high - column * length,
                                column * half : (column + 1) * half,
                            ] = values[:, low - start : high - start, :]

    for core in range(2):

        @pl.when(place_ref[3] == core)
        def _(core=core):
            copy(core, own_ref)
            copy(1 - core, other_ref)

    parts = sems.shape[0]
    rows = length // parts
    sends = []
    for step in range(parts):
        part = pl.ds(step * rows, rows)
        sends.append(
            pltpu.make_async_copy(out_ref.at[:, part, :], out_hbm.at[:, part, :], sems.at[step])
        )
    for send in sends:
        send.start()
    for send in sends:
        send.wait()


def widen(own, other, length, scale):
    row, col = lax.axis_index("row"), lax.axis_index("col")
    place = jnp.stack([row // 2, col % 4, col // 4, row % 2]).astype(jnp.int32)
    layers, half = own.shape[3], own.shape[5]
    return pl.pallas_call(
        functools.partial(widen_kernel, scale=scale),
        name="widen",
        out_shape=jax.ShapeDtypeStruct((layers, length, 2 * half), jnp.float32),
        in_specs=[
            pl.BlockSpec(memory_space=SMEM),
            pl.BlockSpec(memory_space=VMEM),
            pl.BlockSpec(memory_space=VMEM),
        ],
        out_specs=pl.BlockSpec(memory_space=pl.ANY),
        scratch_shapes=[
            pltpu.VMEM((layers, length, 2 * half), jnp.float32),
            pltpu.SemaphoreType.DMA((8,)),
        ],
        compiler_params=params(24),
        cost_estimate=pl.CostEstimate(flops=3_000_000, bytes_accessed=10_000_000, transcendentals=0),
    )(place, own, other)


def order_kernel(rows_ref, start_ref, end_ref, entry_ref, count):
    places = start_ref.shape[0]
    extent = 7
    slots = rows_ref.shape[0] // extent

    def begin(p, carry):
        count[p] = start_ref[p]
        return carry

    lax.fori_loop(0, places, begin, 0)

    def enter(slot, carry):
        @pl.when(rows_ref[slot * extent] >= 0)
        def _():
            for i in range(extent):
                first = rows_ref[slot * extent + i]
                for a in range(2):
                    n = count[first + a]
                    count[first + a] = n + 1
                    entry_ref[n] = slot * 16 + 2 * i + a

        return carry

    lax.fori_loop(0, slots, enter, 0)

    def fill(p, carry):
        def blank(n, inner):
            entry_ref[n] = 14
            return inner

        return lax.fori_loop(count[p], end_ref[p], blank, carry)

    lax.fori_loop(0, places, fill, 0)


def order_entries(rows, start, end, entries):
    return pl.pallas_call(
        order_kernel,
        name="order_entries",
        out_shape=jax.ShapeDtypeStruct((entries,), jnp.int32),
        in_specs=[pl.BlockSpec(memory_space=SMEM)] * 3,
        out_specs=pl.BlockSpec(memory_space=SMEM),
        scratch_shapes=[pltpu.SMEM((TILE,), jnp.int32)],
        cost_estimate=pl.CostEstimate(flops=10_000_000, bytes_accessed=30_000_000, transcendentals=0),
    )(rows, start, end)


def tile_kernel(
    base_ref,
    place_ref,
    groups_ref,
    got_hbm,
    corner_ref,
    low_ref,
    high_ref,
    out_hbm,
    biases_ref,
    landed,
    crops,
    out_ref,
    sems,
    out_sems,
):
    steps = sems.shape[0]
    owners, half = landed.shape[0] // steps, landed.shape[2]
    bins = 49
    block = owners * 200

    def fetch(step):
        part = pl.ds(step * owners, owners)
        used = pl.ds(0, landed.shape[1])
        return pltpu.make_async_copy(
            got_hbm.at[part, used, :], landed.at[part], sems.at[step]
        )

    for step in range(steps):
        fetch(step).start()
    out_ref[...] = jnp.zeros_like(out_ref)

    def convert(step, spare):
        fetch(step).wait()
        wide = landed[pl.ds(step * owners, owners)].astype(jnp.float32)[:, :200, :]
        crops[pl.ds(pl.multiple_of(step * block, 8), block), :] = wide.reshape(block, half)
        return spare + jnp.sum(wide[:, 192:, :], axis=0)

    biases_ref[...] = lax.fori_loop(0, steps, convert, jnp.zeros(biases_ref.shape, jnp.float32))

    position = lax.broadcasted_iota(jnp.int32, (TILE, corner_ref.shape[1]), 0).astype(jnp.float32)

    def columns(t):
        line = pl.ds(t, 1)
        corner = corner_ref[line, :]
        near = jnp.where(position == corner, low_ref[line, :], 0.0)
        far = jnp.where(position == corner + 1.0, high_ref[line, :], 0.0)
        return (near + far).astype(jnp.bfloat16)

    def group(t):
        left, right = [], []
        for n in range(GROUP):
            base = base_ref[t * GROUP + n]
            left.append(crops[pl.ds(base, 8), :])
            right.append(crops[pl.ds(base + bins, 8), :])
        values = jnp.concatenate(
            [jnp.concatenate(left, axis=0), jnp.concatenate(right, axis=0)], axis=1
        ).astype(jnp.bfloat16)
        return jnp.dot(columns(t), values, preferred_element_type=jnp.float32)

    def several(t, carry):
        terms = [group(t * UNROLL + u) for u in range(UNROLL)]
        for u in range(UNROLL):
            out_ref[place_ref[t * UNROLL + u]] += terms[u]
        return carry

    lax.fori_loop(0, (groups_ref[0] + UNROLL - 1) // UNROLL, several, 0)
    rows = out_ref.shape[0] // out_sems.shape[0]
    sends = []
    for step in range(out_sems.shape[0]):
        part = pl.ds(step * rows, rows)
        sends.append(pltpu.make_async_copy(out_ref.at[part], out_hbm.at[part], out_sems.at[step]))
    for send in sends:
        send.start()
    for send in sends:
        send.wait()


def tile_sum(base, place, groups, got, corner, low, high, channels):
    owners, rows, half = got.shape
    tile = (TILE, TILE, channels)
    return pl.pallas_call(
        tile_kernel,
        name="tile_sum",
        out_shape=(
            jax.ShapeDtypeStruct(tile, jnp.float32),
            jax.ShapeDtypeStruct((8, half), jnp.float32),
        ),
        grid_spec=pltpu.PrefetchScalarGridSpec(
            num_scalar_prefetch=3,
            grid=(1,),
            in_specs=[pl.BlockSpec(memory_space=pl.ANY)]
            + [pl.BlockSpec(corner.shape, lambda g, *refs: (0, 0))] * 3,
            out_specs=(
                pl.BlockSpec(memory_space=pl.ANY),
                pl.BlockSpec((8, half), lambda g, *refs: (0, 0)),
            ),
            scratch_shapes=[
                pltpu.VMEM((owners, 208, half), jnp.bfloat16),
                pltpu.VMEM((owners * 200, half), jnp.float32),
                pltpu.VMEM(tile, jnp.float32),
                pltpu.SemaphoreType.DMA((16,)),
                pltpu.SemaphoreType.DMA((8,)),
            ],
        ),
        compiler_params=params(58),
        cost_estimate=pl.CostEstimate(
            flops=2 * TILE * corner.size * channels, bytes_accessed=17_000_000, transcendentals=0
        ),
    )(base, place, groups, got, corner, low, high)


def fields_kernel(tiles_ref, rows_ref, cols_ref, row_weight_ref, col_weight_ref, send_ref, boxes_ref):
    per_box, boxes = tiles_ref.shape
    extent = rows_ref.shape[0]
    pieces = per_box * boxes

    def wide(parts):
        return jnp.concatenate(parts, axis=1)

    targets = wide([tiles_ref[t : t + 1, :].astype(jnp.float32) for t in range(per_box)])
    rows = wide([rows_ref[:, t, :].astype(jnp.float32) for t in range(per_box)])
    cols = wide([cols_ref[:, t, :].astype(jnp.float32) for t in range(per_box)])
    row_weight = [
        wide([row_weight_ref[t, :, a, :].astype(jnp.float32) for t in range(per_box)])
        for a in range(2)
    ]
    col_weight = [
        wide([col_weight_ref[t, :, a, :].astype(jnp.float32) for t in range(per_box)])
        for a in range(2)
    ]
    blank = jnp.zeros((1, pieces), jnp.float32)
    parts = [targets, jnp.zeros((6, pieces), jnp.float32), jnp.ones((1, pieces), jnp.float32)]
    for array in [rows, cols] + row_weight + col_weight:
        parts = parts + [array, blank]
    parts.append(jnp.zeros((8, pieces), jnp.float32))
    fields = jnp.concatenate(parts, axis=0).astype(jnp.bfloat16)
    tile = lax.broadcasted_iota(jnp.int32, (pieces, pieces), 0)
    piece = lax.broadcasted_iota(jnp.int32, (pieces, pieces), 1)
    match = targets.astype(jnp.int32) == tile
    upper = jnp.where(tile < piece, 1.0, 0.0).astype(jnp.bfloat16)
    chosen = jnp.where(match, 1.0, 0.0)
    earlier = jnp.dot(chosen.astype(jnp.bfloat16), upper, preferred_element_type=jnp.float32)
    box = (lax.broadcasted_iota(jnp.int32, (8, pieces), 1) % boxes).astype(jnp.float32)
    slots = []
    for rank in range(2):
        ranked = jnp.where(earlier == float(rank), chosen, 0.0).astype(jnp.bfloat16)
        found = lax.dot_general(
            box.astype(jnp.bfloat16),
            ranked,
            (((1,), (1,)), ((), ())),
            preferred_element_type=jnp.float32,
        )
        boxes_ref[rank : rank + 1, :] = found[:1].astype(jnp.int32)
        slots.append(
            lax.dot_general(
                ranked, fields, (((1,), (1,)), ((), ())), preferred_element_type=jnp.float32
            )
        )
    send_ref[:, 0, :] = jnp.concatenate(slots, axis=1).astype(jnp.bfloat16)


def describe(tile_ids, corner_rows, corner_cols, row_weight, col_weight):
    pieces = tile_ids.size
    arrays = (
        jnp.transpose(tile_ids),
        jnp.transpose(corner_rows, (2, 1, 0)),
        jnp.transpose(corner_cols, (2, 1, 0)),
        jnp.transpose(row_weight, (1, 2, 3, 0)),
        jnp.transpose(col_weight, (1, 2, 3, 0)),
    )
    return pl.pallas_call(
        fields_kernel,
        name="describe",
        out_shape=(
            jax.ShapeDtypeStruct((pieces, 1, 128), jnp.bfloat16),
            jax.ShapeDtypeStruct((2, pieces), jnp.int32),
        ),
        grid=(1,),
        in_specs=[pl.BlockSpec(array.shape, lambda g, n=array.ndim: (0,) * n) for array in arrays],
        out_specs=(
            pl.BlockSpec((pieces, 1, 128), lambda g: (0, 0, 0)),
            pl.BlockSpec((2, pieces), lambda g: (0, 0)),
        ),
        compiler_params=params(58),
        cost_estimate=pl.CostEstimate(flops=10_000_000, bytes_accessed=200_000, transcendentals=0),
    )(*arrays)


def arrange(slots, extent):
    count = slots.shape[0]
    groups = count * extent * 2 // GROUP + TILE
    entries = groups * GROUP
    wide = extent + 1
    rows = jnp.where(slots[:, 7:8] > 0.5, slots[:, 8 : 8 + extent], -4.0).astype(jnp.int32)
    pixel = jnp.arange(TILE, dtype=jnp.int32)
    flat = rows.reshape(-1)
    hits = (flat == pixel[:, None]).astype(jnp.int32) + (flat + 1 == pixel[:, None]).astype(jnp.int32)
    tally = jnp.sum(hits, axis=1)
    needed = (tally + GROUP - 1) // GROUP
    ends = jnp.sum(jnp.where(pixel[None, :] <= pixel[:, None], needed[None, :], 0), axis=1)
    start = (ends - needed) * GROUP
    place = jnp.sum((jnp.arange(groups)[:, None] >= ends[None, :-1]).astype(jnp.int32), axis=1)
    entry = order_entries(flat, start, ends * GROUP, entries)
    inside = jnp.arange(entries, dtype=jnp.int32) < ends[-1] * GROUP
    entry = jnp.where(inside, entry, 14)
    owner, code = entry // 16, entry % 16
    line = jnp.minimum(code // 2, extent - 1)
    base = owner // 2 * 200 + owner % 2 * 98 + extent * line
    chosen = (owner[:, None] == jnp.arange(count)).astype(jnp.bfloat16)
    values = jnp.dot(chosen, slots[:, 8:].astype(jnp.bfloat16), preferred_element_type=jnp.float32)
    which = jnp.arange(2 * wide, dtype=jnp.int32)
    wanted = (which[None, :] % wide == line[:, None]) & (which[None, :] // wide == code[:, None] % 2)
    wanted = wanted & (code[:, None] < 2 * extent)
    scale = jnp.sum(jnp.where(wanted, values[:, 2 * wide : 4 * wide], 0.0), axis=1)
    corner = values[:, wide : 2 * wide]
    low = values[:, 4 * wide : 5 * wide] * scale[:, None]
    high = values[:, 5 * wide : 6 * wide] * scale[:, None]

    def lanes(array):
        return array.reshape(groups, GROUP * wide)

    return base, place, ends[-1:], lanes(corner), lanes(low), lanes(high)


def shards(
    out_grad,
    saved,
    conv_weight,
    conv_bias,
    tile_ids,
    corner_rows,
    corner_cols,
    row_weight,
    col_weight,
):
    boxes, extent, channels = out_grad.shape[0], out_grad.shape[1], out_grad.shape[3]
    layers = saved.shape[0]
    devices = lax.axis_size("row") * lax.axis_size("col")
    grad_scale = 1.0 / math.sqrt(boxes * devices * extent * extent)

    grad_t = jnp.transpose(out_grad, (1, 2, 0, 3))
    saved_t = jnp.transpose(saved, (0, 2, 3, 1, 4))
    lines = devices * SUM_ROWS
    core = lax.axis_index("row") % 2
    own, give, crops, biases = conv_chain(grad_t, saved_t, conv_weight, conv_bias, core, lines)
    give, tile_ids = lax.optimization_barrier((give, tile_ids))
    slots, box_of_slot = describe(tile_ids, corner_rows, corner_cols, row_weight, col_weight)
    slots = lax.all_to_all(slots, AXES, split_axis=0, concat_axis=0, tiled=True)
    other = lax.ppermute(give, "row", hop_core())
    send = pack(box_of_slot.reshape(-1), crops, biases, own, other, boxes)
    send, slots = lax.optimization_barrier((send, slots))
    got = lax.all_to_all(send, AXES, split_axis=0, concat_axis=0, tiled=True)

    base, place, groups, corner, low, high = arrange(slots.reshape(2 * devices, -1).astype(jnp.float32), extent)
    got, place, corner, low, high = lax.optimization_barrier((got, place, corner, low, high))
    cols = lax.axis_size("col")
    arrived = got[:, 200:, :].reshape(-1, layers, cols, SUM_ROWS, channels // 2)
    part = jnp.sum(arrived.astype(jnp.float32), axis=(0, 2)).astype(jnp.bfloat16)
    part = ring(ring(part, "col", hop_z), "col", hop_y)
    part, got = lax.optimization_barrier((part, got))
    own = ring(part, "row", hop_x)
    feature_grad, spare = tile_sum(base, place, groups, got, corner, low, high, channels)
    own, feature_grad = lax.optimization_barrier((own, feature_grad))
    other = lax.ppermute(own, "row", hop_core())
    weight_grad = widen(own, other, 9 * channels, grad_scale)
    bias_grad = (spare[4 : 4 + 2 * layers] * grad_scale).reshape(layers, channels)
    return (weight_grad, bias_grad, feature_grad)


def solution(mesh):
    in_specs = (
        P(AXES, None, None, None),
        P(None, AXES, None, None, None),
        P(),
        P(),
        P(AXES, None),
        P(AXES, None, None),
        P(AXES, None, None),
        P(AXES, None, None, None),
        P(AXES, None, None, None),
    )
    out_specs = (P(), P(), P("row", "col", None))
    return jax.shard_map(shards, mesh=mesh, in_specs=in_specs, out_specs=out_specs, check_vma=False)
```
